32 devices in a mesh: fsdp: 32 (over z, y, x, core).
Axes of the slice: x: 2, y: 2, z: 4, core: 2. Of those that a mesh axis runs over, the one named last changes fastest.
Arguments:
- latents: float32 [32, 256, 16], P('fsdp'), may hold values from -6 to 6
- targets: float32 [32, 256, 16], P('fsdp'), may hold values from -6 to 6
- features: float32 [32, 256, 768], P('fsdp'), may hold values from -7 to 7
- time_weights: float32 [32], P('fsdp'), may hold values from 0.5 to 7.5
- timesteps: int32 [32], P('fsdp'), may hold values from 0 to 999
- classes: int32 [32], P('fsdp'), may hold values from 0 to 1000
- block_in: float32 [2, 768, 10752], P(None, 'fsdp'), may hold values from -0.21875 to 0.21875
- block_in_rows: float32 [2, 768], P(None, 'fsdp'), may hold values from 2.49084326e-14 to 6.3765587e-12
- block_in_cols: float32 [2, 10752], replicated, may hold values from 2.49084326e-14 to 6.3765587e-12
- block_down: float32 [2, 3072, 768], P(None, 'fsdp'), may hold values from -0.109375 to 0.109375
- block_down_rows: float32 [2, 3072], P(None, 'fsdp'), may hold values from 7.9706984e-11 to 3.1882794e-10
- block_down_cols: float32 [2, 768], replicated, may hold values from 7.9706984e-11 to 3.1882794e-10
- stem_main: float32 [768, 5625], P('fsdp'), may hold values from -4 to 4
- stem_main_rows: float32 [768], P('fsdp'), may hold values from 7.9706984e-11 to 3.1882794e-10
- stem_main_cols: float32 [5625], replicated, may hold values from 7.9706984e-11 to 3.1882794e-10
- stem_proj: float32 [2048, 2816], P('fsdp'), may hold values from -0.125 to 0.125
- stem_proj_rows: float32 [2048], P('fsdp'), may hold values from 2.4908433e-15 to 6.376559e-13
- stem_proj_cols: float32 [2816], replicated, may hold values from 2.4908433e-15 to 6.376559e-13
- head_weight: float32 [769, 16], replicated, may hold values from -0.21875 to 0.21875
- head_rows: float32 [769], replicated, may hold values from 7.9706984e-11 to 3.1882794e-10
- head_cols: float32 [16], replicated, may hold values from 7.9706984e-11 to 3.1882794e-10
- biases: float32 [31744], P('fsdp'), may hold values from -1.25 to 1.25
- bias_second: float32 [31744], P('fsdp'), may hold values from 7.9706984e-11 to 4e-05
Outputs:
- loss: float32 [], replicated
- grad_norm: float32 [], replicated
- new_block_in: float32 [2, 768, 10752], P(None, 'fsdp')
- clip_block_in: float32 [2, 768, 10752], P(None, 'fsdp')
- rows_block_in: float32 [2, 768], P(None, 'fsdp')
- cols_block_in: float32 [2, 10752], replicated
- copy_block_in: bfloat16 [2, 768, 10752], P(None, 'fsdp')
- new_block_down: float32 [2, 3072, 768], P(None, 'fsdp')
- clip_block_down: float32 [2, 3072, 768], P(None, 'fsdp')
- rows_block_down: float32 [2, 3072], P(None, 'fsdp')
- cols_block_down: float32 [2, 768], replicated
- copy_block_down: bfloat16 [2, 3072, 768], P(None, 'fsdp')
- new_stem_main: float32 [768, 5625], P('fsdp')
- clip_stem_main: float32 [768, 5625], P('fsdp')
- rows_stem_main: float32 [768], P('fsdp')
- cols_stem_main: float32 [5625], replicated
- copy_stem_main: bfloat16 [768, 5625], P('fsdp')
- new_stem_proj: float32 [2048, 2816], P('fsdp')
- clip_stem_proj: float32 [2048, 2816], P('fsdp')
- rows_stem_proj: float32 [2048], P('fsdp')
- cols_stem_proj: float32 [2816], replicated
- copy_stem_proj: bfloat16 [2048, 2816], P('fsdp')
- new_head: float32 [769, 16], replicated
- clip_head: float32 [769, 16], replicated
- rows_head: float32 [769], replicated
- cols_head: float32 [16], replicated
- new_biases: float32 [31744], P('fsdp')
- clip_biases: float32 [31744], P('fsdp')
- second_biases: float32 [31744], P('fsdp')
The draws below stay inside these ranges and needn't reach their ends.
All inputs are finite; a program needn't handle non-finite values.
Results may differ from the reference program's by a relative error of at most 0.01.
Values may be sent and summed in bfloat16 or wider, within the bound.
No kernel may reach another device: no remote copies, remote signals or barrier semaphores. Data moves between devices by JAX's collectives and lax.ppermute only.
A program may use at most 448 MiB of HBM per device.

```python
import math
import jax
import jax.numpy as jnp
from jax import lax

D = 768
HEADS = 12
HD = 64
F = 3072
P_SIZE = 2048
Z = 768
NCLS = 1001
PD = 16
TF = 256
L = 2
GRID = 16
TOK = 256
IMG = 32
WIN = 10752
SDC = 5625
VB = 11520
NB = 31744
PARAMS = 31364880


def log_range(base_key, array_shape, lowest, spread):
    return lowest * jnp.exp(jax.random.uniform(base_key, array_shape, jnp.float32, 0.0, math.log(spread)))


def draw_time_weights(key, part):
    key = jax.random.fold_in(key, 11)
    place = jnp.arange(IMG, dtype=jnp.float32) / max(IMG - 1, 1)
    return (1.0 + 2.0 * place) * jax.random.uniform(key, (IMG,), jnp.float32, 0.75, 1.25)


def draw_stem_main(key, part):
    key = jax.random.fold_in(key, 23)
    place = jnp.arange(D, dtype=jnp.float32) / max(D - 1, 1)
    small = D ** (-0.5)
    rise = 1.0 + 2.0 * place
    base = jnp.clip(jax.random.normal(key, (D, SDC), jnp.float32), -4.0, 4.0)
    flat = jnp.full((SDC,), small, jnp.float32)
    lifted = jnp.concatenate([jnp.zeros((3 * D,), jnp.float32), jnp.full((NCLS,), 0.15, jnp.float32), jnp.full((PD,), 0.25, jnp.float32), jnp.zeros((P_SIZE + TF,), jnp.float32)])
    marked = jnp.concatenate([jnp.zeros((3 * D,), jnp.float32), jnp.ones((NCLS + PD,), jnp.float32), jnp.zeros((P_SIZE + TF,), jnp.float32)])
    column_scale = flat * (1.0 - marked)[None, :] + lifted[None, :] * rise[:, None]
    return base * column_scale


def draw_features(key, part):
    key = jax.random.fold_in(key, 31)
    common_key, noise_key = jax.random.split(key)
    common = jnp.clip(jax.random.normal(common_key, (Z,), jnp.float32), -3.0, 3.0)
    noise = jnp.clip(jax.random.normal(noise_key, (IMG, TOK, Z), jnp.float32), -4.0, 4.0)
    return common[None, None, :] + noise


def draw_block_in_rows(key, part):
    key = jax.random.fold_in(key, 41)
    lowest = 5e-05 / PARAMS
    return log_range(key, (L, D), lowest, 4.0)


def draw_block_in_cols(key, part):
    key = jax.random.fold_in(key, 43)
    lowest = 5e-05 / PARAMS
    return log_range(key, (L, WIN), lowest, 4.0)


def draw_stem_proj_rows(key, part):
    key = jax.random.fold_in(key, 47)
    lowest = 5e-06 / PARAMS
    return log_range(key, (P_SIZE,), lowest, 4.0)


def draw_stem_proj_cols(key, part):
    key = jax.random.fold_in(key, 53)
    lowest = 5e-06 / PARAMS
    return log_range(key, (P_SIZE + Z,), lowest, 4.0)


def draw_bias_second(key, part):
    key = jax.random.fold_in(key, 59)
    lowest = 0.0025 / PARAMS
    return log_range(key, (NB,), lowest, 4.0)


def place_ends(values, rng, smallest, largest):
    dims = values.shape
    spot = [jax.random.randint(jax.random.fold_in(rng, axis), (), 0, dims[axis]) for axis in range(len(dims))]
    values = values.at[tuple(spot)].set(smallest)
    longest = dims.index(max(dims))
    spot[longest] = (spot[longest] + 1) % dims[longest]
    return values.at[tuple(spot)].set(largest)


def steps_of(rng, shape, pieces, least, top_value):
    def one(axis_at, shards_of):
        draws = jax.random.uniform(jax.random.fold_in(jax.random.fold_in(rng, 6), axis_at), (shards_of,), jnp.float32, least / len(pieces), top_value / len(pieces))
        return jnp.repeat(jnp.exp(draws), shape[axis_at] // shards_of).reshape((-1,) + (1,) * (len(shape) - axis_at - 1))

    level = one(*pieces[0])
    for cut in pieces[1:]:
        level = level * one(*cut)
    return level


def bell_draw(rng, dims, scale, most, cuts=(), kind=jnp.bfloat16):
    values = jax.random.normal(rng, dims, jnp.float32) * scale
    if len(cuts) > 0:
        values = steps_of(rng, dims, cuts, -0.22, 0.18) * values
    return jnp.clip(values, min=-most, max=most).astype(kind)


def setup_inputs(seed: int = 0) -> dict:
    keys = jax.random.split(jax.random.key(seed), 24)
    latents = bell_draw(keys[0], (IMG, TOK, PD), 1.0, 6.0, ((0, 32),), jnp.float32)
    targets = bell_draw(keys[1], (IMG, TOK, PD), 1.0, 6.0, ((0, 32),), jnp.float32)
    features = draw_features(jax.random.fold_in(keys[23], 71), 0)
    time_weights = draw_time_weights(jax.random.fold_in(keys[23], 71), 0)
    timesteps = place_ends(jax.random.randint(keys[4], (IMG,), 0, 1000), jax.random.fold_in(keys[4], 1), 0, 999).astype(jnp.int32)
    classes = place_ends(jax.random.randint(keys[5], (IMG,), 0, NCLS), jax.random.fold_in(keys[5], 1), 0, NCLS - 1).astype(jnp.int32)
    block_in = bell_draw(keys[6], (L, D, WIN), D ** -0.5, 0.21875, ((1, 32),), jnp.float32)
    block_in_rows = draw_block_in_rows(jax.random.fold_in(keys[23], 71), 0)
    block_in_cols = draw_block_in_cols(jax.random.fold_in(keys[23], 71), 0)
    block_down = bell_draw(keys[9], (L, F, D), F ** -0.5, 0.109375, ((1, 32),), jnp.float32)
    block_down_rows = jnp.clip(jnp.exp(math.log(3.1882793627424633e-10) - 1.3862944 * jax.random.uniform(keys[10], (L, F), jnp.float32) ** steps_of(keys[10], (L, F), ((1, 32),), -0.2, 0.2)), 7.970698406856158e-11, 3.1882793627424633e-10)
    block_down_cols = jnp.clip(jnp.exp(jax.random.uniform(keys[11], (L, D), jnp.float32, math.log(7.970698406856158e-11), math.log(3.1882793627424633e-10))), 7.970698406856158e-11, 3.1882793627424633e-10)
    stem_main = draw_stem_main(jax.random.fold_in(keys[23], 71), 0)
    stem_main_rows = jnp.clip(jnp.exp(math.log(3.1882793627424633e-10) - 1.3862944 * jax.random.uniform(keys[13], (D,), jnp.float32) ** steps_of(keys[13], (D,), ((0, 32),), -0.2, 0.2)), 7.970698406856158e-11, 3.1882793627424633e-10)
    stem_main_cols = jnp.clip(jnp.exp(jax.random.uniform(keys[14], (SDC,), jnp.float32, math.log(7.970698406856158e-11), math.log(3.1882793627424633e-10))), 7.970698406856158e-11, 3.1882793627424633e-10)
    stem_proj = bell_draw(keys[15], (P_SIZE, P_SIZE + Z), P_SIZE ** -0.5, 0.125, ((0, 32),), jnp.float32)
    stem_proj_rows = draw_stem_proj_rows(jax.random.fold_in(keys[23], 71), 0)
    stem_proj_cols = draw_stem_proj_cols(jax.random.fold_in(keys[23], 71), 0)
    head_weight = bell_draw(keys[18], (D + 1, PD), D ** -0.5, 0.21875, (), jnp.float32)
    head_rows = jnp.clip(jnp.exp(jax.random.uniform(keys[19], (D + 1,), jnp.float32, math.log(7.970698406856158e-11), math.log(3.1882793627424633e-10))), 7.970698406856158e-11, 3.1882793627424633e-10)
    head_cols = jnp.clip(jnp.exp(jax.random.uniform(keys[20], (PD,), jnp.float32, math.log(7.970698406856158e-11), math.log(3.1882793627424633e-10))), 7.970698406856158e-11, 3.1882793627424633e-10)
    biases = bell_draw(keys[21], (NB,), 0.2, 1.25, ((0, 32),), jnp.float32)
    bias_second = draw_bias_second(jax.random.fold_in(keys[23], 71), 0)
    return dict(latents=latents, targets=targets, features=features, time_weights=time_weights, timesteps=timesteps, classes=classes, block_in=block_in, block_in_rows=block_in_rows, block_in_cols=block_in_cols, block_down=block_down, block_down_rows=block_down_rows, block_down_cols=block_down_cols, stem_main=stem_main, stem_main_rows=stem_main_rows, stem_main_cols=stem_main_cols, stem_proj=stem_proj, stem_proj_rows=stem_proj_rows, stem_proj_cols=stem_proj_cols, head_weight=head_weight, head_rows=head_rows, head_cols=head_cols, biases=biases, bias_second=bias_second)


NORM_EPS = 1e-06
SCORE_SCALE = 0.125
LEARN_RATE = 0.03
DECAY_RATE = 0.5
CLIP_LIMIT = 0.05
FACTOR_EPS = 1e-30

@jax.custom_vjp
def low(v):
    return lax.optimization_barrier(v.astype(jnp.bfloat16)).astype(jnp.float32)

@jax.custom_vjp
def low_back(v):
    return v

def low_keep(v):
    return (low(v), None)

def low_pass(kept, grad):
    return (grad,)

def back_keep(v):
    return (v, None)

def back_low(kept, grad):
    return (low(grad),)
low.defvjp(low_keep, low_pass)
low_back.defvjp(back_keep, back_low)

def matmul(left_side, weight_side):
    return low_back(jnp.dot(low(left_side), low(weight_side), precision=lax.Precision.HIGHEST))

def cut_parts(array, part_widths):
    borders = []
    running = 0
    for part_width in part_widths[:-1]:
        running += part_width
        borders.append(running)
    return jnp.split(array, borders, axis=-1)

def layer_norm(values):
    centred = values - lax.optimization_barrier(jnp.mean(values, axis=-1, keepdims=True))
    return centred * lax.rsqrt(lax.optimization_barrier(jnp.mean(centred * centred, axis=-1, keepdims=True)) + NORM_EPS)

def modulate(values, shift_part, scale_part):
    return layer_norm(values) * (1.0 + scale_part[:, None, :]) + shift_part[:, None, :]

def positions():
    quarter = D // 4
    omega_rate = jnp.exp(-math.log(10000.0) * jnp.arange(quarter, dtype=jnp.float32) / quarter)
    token_place = jnp.arange(TOK)
    column = (token_place % GRID).astype(jnp.float32)
    row_place = (token_place // GRID).astype(jnp.float32)

    def encode(coords):
        angles = coords[:, None] * omega_rate[None, :]
        return jnp.concatenate([jnp.sin(angles), jnp.cos(angles)], axis=1)
    return jnp.concatenate([encode(column), encode(row_place)], axis=1)

def time_freq(timesteps):
    half_width = TF // 2
    freq_rate = jnp.exp(-math.log(10000.0) * jnp.arange(half_width, dtype=jnp.float32) / half_width)
    angles = timesteps.astype(jnp.float32)[:, None] * freq_rate[None, :]
    return jnp.concatenate([jnp.cos(angles), jnp.sin(angles)], axis=1)

def cosine_loss(projected, features):
    inner = lax.optimization_barrier(jnp.sum(projected * features, axis=-1))
    lengths = jnp.sqrt(lax.optimization_barrier(jnp.sum(projected * projected, axis=-1)) + NORM_EPS) * jnp.sqrt(lax.optimization_barrier(jnp.sum(features * features, axis=-1)) + NORM_EPS)
    return -0.5 * jnp.sum(lax.optimization_barrier(jnp.mean(inner / lengths, axis=1)))

def forward(block_in, block_down, stem_main, stem_proj, head_weight, biases, latents, targets, features, time_weights, timesteps, classes):
    batch_rows = latents.shape[0]
    bias_all = low(biases)
    block_bias = bias_all[:L * VB].reshape(L, VB)
    stem_bias = bias_all[L * VB:]
    time_out, final_ada, table_t, patch_t, proj_one, time_in = cut_parts(stem_main, [D, 2 * D, NCLS, PD, P_SIZE, TF])
    proj_two, proj_three = cut_parts(stem_proj, [P_SIZE, Z])
    bias_tin, bias_tout, bias_final, bias_patch, bias_one, bias_two, bias_three = cut_parts(stem_bias, [D, D, 2 * D, D, P_SIZE, P_SIZE, Z])
    embed_hidden = matmul(time_freq(timesteps), time_in.T) + bias_tin
    condition = matmul(jax.nn.silu(embed_hidden), time_out) + bias_tout + jnp.take(low(table_t), classes, axis=1).T
    cond_act = jax.nn.silu(condition)
    hidden = matmul(latents, patch_t.T) + bias_patch + positions()
    first_out = hidden
    for level_index in range(L):
        weight_qkv, weight_proj, weight_up, weight_ada = cut_parts(block_in[level_index], [3 * D, D, F, 6 * D])
        bias_qkv, bias_proj, bias_up, bias_ada, bias_down = cut_parts(block_bias[level_index], [3 * D, D, F, 6 * D, D])
        modulation = matmul(cond_act, weight_ada) + bias_ada
        shift_one, scale_one, gate_one, shift_two, scale_two, gate_two = jnp.split(modulation, 6, axis=-1)
        normed = modulate(hidden, shift_one, scale_one)
        packed = (matmul(normed, weight_qkv) + bias_qkv).reshape(batch_rows, TOK, 3, HEADS, HD)
        scores = low_back(jnp.einsum('bqhd,bkhd->bhqk', low(packed[:, :, 0]), low(packed[:, :, 1]), precision=lax.Precision.HIGHEST)) * SCORE_SCALE
        attention = jax.nn.softmax(scores, axis=-1)
        attended = low_back(jnp.einsum('bhqk,bkhd->bqhd', low(attention), low(packed[:, :, 2]), precision=lax.Precision.HIGHEST)).reshape(batch_rows, TOK, D)
        hidden = hidden + gate_one[:, None, :] * (matmul(attended, weight_proj) + bias_proj)
        normed = modulate(hidden, shift_two, scale_two)
        activated = jax.nn.gelu(matmul(normed, weight_up) + bias_up, approximate=True)
        hidden = hidden + gate_two[:, None, :] * (matmul(activated, block_down[level_index]) + bias_down)
        if level_index == 0:
            first_out = hidden
    proj_hidden = jax.nn.silu(matmul(first_out, proj_one) + bias_one)
    proj_hidden = jax.nn.silu(matmul(proj_hidden, proj_two) + bias_two)
    projected = matmul(proj_hidden, proj_three) + bias_three
    final_mods = matmul(cond_act, final_ada) + bias_final
    shift_final, scale_final = jnp.split(final_mods, 2, axis=-1)
    output = matmul(modulate(hidden, shift_final, scale_final), head_weight[:D]) + head_weight[D]
    residual = output - targets
    return jnp.sum(time_weights * lax.optimization_barrier(jnp.mean(residual * residual, axis=(1, 2)))) + cosine_loss(projected, features)

def factored(weight, gradient, row_old, col_old):
    square = gradient * gradient + FACTOR_EPS
    row_new = DECAY_RATE * row_old + (1.0 - DECAY_RATE) * lax.optimization_barrier(jnp.mean(square, axis=1))
    col_new = DECAY_RATE * col_old + (1.0 - DECAY_RATE) * lax.optimization_barrier(jnp.mean(square, axis=0))
    estimate = row_new[:, None] * col_new[None, :] / jnp.mean(row_new)
    return (weight - LEARN_RATE * gradient * lax.rsqrt(estimate), row_new, col_new)

def reference(latents, targets, features, time_weights, timesteps, classes, block_in, block_in_rows, block_in_cols, block_down, block_down_rows, block_down_cols, stem_main, stem_main_rows, stem_main_cols, stem_proj, stem_proj_rows, stem_proj_cols, head_weight, head_rows, head_cols, biases, bias_second):
    params = (block_in, block_down, stem_main, stem_proj, head_weight, biases)
    group_size = 16
    group_count = latents.shape[0] // group_size

    def regroup(array):
        return array.reshape((group_count, group_size) + array.shape[1:])
    data = tuple((regroup(array) for array in (latents, targets, features, time_weights, timesteps, classes)))

    def step(carry, batch):
        loss_sum, grad_sums = carry
        value, pull = jax.vjp(lambda *weights: forward(*weights, *batch), *params)
        fresh = pull(jnp.float32(1.0))
        return ((loss_sum + value, tuple((old + new for old, new in zip(grad_sums, fresh)))), None)
    start = (jnp.float32(0.0), tuple((jnp.zeros_like(weight) for weight in params)))
    (loss, grads), _ = lax.scan(step, start, data)
    total = jnp.float32(0.0)
    for gradient in grads:
        total = total + jnp.sum(gradient * gradient)
    grad_norm = jnp.sqrt(total)
    clip_scale = jnp.minimum(1.0, CLIP_LIMIT / grad_norm)
    clip_in, clip_down, clip_main, clip_proj, clip_head, clip_bias = [clip_scale * gradient for gradient in grads]
    new_in, rows_in, cols_in = jax.vmap(factored)(block_in, clip_in, block_in_rows, block_in_cols)
    new_down, rows_down, cols_down = jax.vmap(factored)(block_down, clip_down, block_down_rows, block_down_cols)
    new_main, rows_main, cols_main = factored(stem_main, clip_main, stem_main_rows, stem_main_cols)
    new_proj, rows_proj, cols_proj = factored(stem_proj, clip_proj, stem_proj_rows, stem_proj_cols)
    new_head, rows_head, cols_head = factored(head_weight, clip_head, head_rows, head_cols)
    second_new = DECAY_RATE * bias_second + (1.0 - DECAY_RATE) * (clip_bias * clip_bias + FACTOR_EPS)
    new_bias = biases - LEARN_RATE * clip_bias * lax.rsqrt(second_new)
    return (loss, grad_norm, new_in, clip_in, rows_in, cols_in, new_in.astype(jnp.bfloat16), new_down, clip_down, rows_down, cols_down, new_down.astype(jnp.bfloat16), new_main, clip_main, rows_main, cols_main, new_main.astype(jnp.bfloat16), new_proj, clip_proj, rows_proj, cols_proj, new_proj.astype(jnp.bfloat16), new_head, clip_head, rows_head, cols_head, new_bias, clip_bias, second_new)
```

```python
import functools
import math

import jax
import jax.numpy as jnp
from jax import lax
from jax.sharding import PartitionSpec as P

D = 768
HD = 64
F = 3072
P_SIZE = 2048
Z = 768
NCLS = 1001
PD = 16
TF = 256
L = 2
GRID = 16
TOK = 256
VB = 11520


NORM_EPS = 1e-06
SCORE_SCALE = 0.125
LEARN_RATE = 0.03
DECAY_RATE = 0.5
CLIP_LIMIT = 0.05
FACTOR_EPS = 1e-30


def cut_parts(array, part_widths):
    borders = []
    running = 0
    for part_width in part_widths[:-1]:
        running += part_width
        borders.append(running)
    return jnp.split(array, borders, axis=-1)


def layer_norm(values):
    centred = values - jnp.mean(values, axis=-1, keepdims=True)
    return centred * lax.rsqrt(jnp.mean(centred * centred, axis=-1, keepdims=True) + NORM_EPS)


def modulate(values, shift_part, scale_part):
    return layer_norm(values) * (1.0 + scale_part[:, None, :]) + shift_part[:, None, :]


def positions():
    quarter = D // 4
    omega_rate = jnp.exp(-math.log(10000.0) * jnp.arange(quarter, dtype=jnp.float32) / quarter)
    token_place = jnp.arange(TOK)
    column = (token_place % GRID).astype(jnp.float32)
    row_place = (token_place // GRID).astype(jnp.float32)

    def encode(coords):
        angles = coords[:, None] * omega_rate[None, :]
        return jnp.concatenate([jnp.sin(angles), jnp.cos(angles)], axis=1)

    return jnp.concatenate([encode(column), encode(row_place)], axis=1)


def time_freq(timesteps):
    half_width = TF // 2
    freq_rate = jnp.exp(-math.log(10000.0) * jnp.arange(half_width, dtype=jnp.float32) / half_width)
    angles = timesteps.astype(jnp.float32)[:, None] * freq_rate[None, :]
    return jnp.concatenate([jnp.cos(angles), jnp.sin(angles)], axis=1)


def cosine_loss(projected, features):
    inner = jnp.sum(projected * features, axis=-1)
    lengths = jnp.sqrt(jnp.sum(projected * projected, axis=-1) + NORM_EPS) * jnp.sqrt(
        jnp.sum(features * features, axis=-1) + NORM_EPS
    )
    return -0.5 * jnp.sum(jnp.mean(inner / lengths, axis=1))


def gelu_tanh(values):
    return jax.nn.gelu(values, approximate=True)


def silu_back(before, grad_after):
    return jax.vjp(jax.nn.silu, before)[1](grad_after)[0]


def total_rows(values):
    return jnp.sum(values.reshape(-1, values.shape[-1]), axis=0)


def linear(left_side, weight_side):
    return jnp.dot(left_side, weight_side, preferred_element_type=jnp.float32)


def linear_back(grad_out, left_side, weight_side):
    grad_low = grad_out.astype(jnp.bfloat16)
    grad_left = lax.dot_general(
        grad_low,
        weight_side,
        (((grad_low.ndim - 1,), (1,)), ((), ())),
        preferred_element_type=jnp.float32,
    )
    flat_left = left_side.reshape(-1, left_side.shape[-1])
    flat_grad = grad_low.reshape(-1, grad_low.shape[-1])
    grad_weight = lax.dot_general(
        flat_left, flat_grad, (((0,), (0,)), ((), ())), preferred_element_type=jnp.float32
    ).astype(jnp.bfloat16)
    return (grad_left, grad_weight)


def split_heads(packed):
    heads_view = packed.reshape(packed.shape[0], packed.shape[1], 3, -1, HD).astype(jnp.bfloat16)
    return (heads_view[:, :, 0], heads_view[:, :, 1], heads_view[:, :, 2])


def attention_forward(packed):
    queries, keys_low, values_low = split_heads(packed)
    scores = (
        jnp.einsum("bqhd,bkhd->bhqk", queries, keys_low, preferred_element_type=jnp.float32)
        * SCORE_SCALE
    )
    top_score = jnp.max(scores, axis=-1, keepdims=True)
    log_total = top_score + jnp.log(jnp.sum(jnp.exp(scores - top_score), axis=-1, keepdims=True))
    attention = jnp.exp(scores - log_total).astype(jnp.bfloat16)
    attended = jnp.einsum(
        "bhqk,bkhd->bqhd", attention, values_low, preferred_element_type=jnp.float32
    )
    return (attended.reshape(packed.shape[0], packed.shape[1], -1).astype(jnp.bfloat16), log_total)


def attention_backward(grad_out, packed, log_total):
    queries, keys_low, values_low = split_heads(packed)
    grad_low = grad_out.reshape(packed.shape[0], packed.shape[1], -1, HD).astype(jnp.bfloat16)
    scores = (
        jnp.einsum("bqhd,bkhd->bhqk", queries, keys_low, preferred_element_type=jnp.float32)
        * SCORE_SCALE
    )
    attention = jnp.exp(scores - log_total)
    grad_attention = jnp.einsum(
        "bqhd,bkhd->bhqk", grad_low, values_low, preferred_element_type=jnp.float32
    )
    grad_values = jnp.einsum(
        "bhqk,bqhd->bkhd",
        attention.astype(jnp.bfloat16),
        grad_low,
        preferred_element_type=jnp.float32,
    )
    grad_scores = attention * (
        grad_attention - jnp.sum(attention * grad_attention, axis=-1, keepdims=True)
    )
    score_low = (grad_scores * SCORE_SCALE).astype(jnp.bfloat16)
    grad_queries = jnp.einsum(
        "bhqk,bkhd->bqhd", score_low, keys_low, preferred_element_type=jnp.float32
    )
    grad_keys = jnp.einsum(
        "bhqk,bqhd->bkhd", score_low, queries, preferred_element_type=jnp.float32
    )
    return jnp.stack([grad_queries, grad_keys, grad_values], axis=2).reshape(
        packed.shape[0], packed.shape[1], -1
    )


def layer_forward(hidden, modulation, layer_low, layer_bias):
    weight_in, weight_down = layer_low
    weight_qkv, weight_proj, weight_up = cut_parts(weight_in, [3 * D, D, F])
    bias_qkv, bias_proj, bias_up, _, bias_down = cut_parts(layer_bias, [3 * D, D, F, 6 * D, D])
    shift_one, scale_one, gate_one, shift_two, scale_two, gate_two = jnp.split(
        modulation, 6, axis=-1
    )
    normed_one = modulate(hidden, shift_one, scale_one).astype(jnp.bfloat16)
    packed = linear(normed_one, weight_qkv) + bias_qkv
    attended, log_total = attention_forward(packed)
    branch_one = linear(attended, weight_proj) + bias_proj
    middle = hidden + gate_one[:, None, :] * branch_one
    normed_two = modulate(middle, shift_two, scale_two).astype(jnp.bfloat16)
    pre_act = linear(normed_two, weight_up) + bias_up
    activated = gelu_tanh(pre_act).astype(jnp.bfloat16)
    branch_two = linear(activated, weight_down) + bias_down
    layer_cache = (
        modulation,
        normed_one,
        packed,
        attended,
        log_total,
        branch_one,
        middle,
        normed_two,
        pre_act,
        activated,
        branch_two,
    )
    return (middle + gate_two[:, None, :] * branch_two, layer_cache)


def layer_backward(grad_out, hidden, layer_low, layer_cache):
    weight_in, weight_down = layer_low
    weight_qkv, weight_proj, weight_up = cut_parts(weight_in, [3 * D, D, F])
    (
        modulation,
        normed_one,
        packed,
        attended,
        log_total,
        branch_one,
        middle,
        normed_two,
        pre_act,
        activated,
        branch_two,
    ) = layer_cache
    shift_one, scale_one, gate_one, shift_two, scale_two, gate_two = jnp.split(
        modulation, 6, axis=-1
    )
    grad_gate_two = jnp.sum(grad_out * branch_two, axis=1)
    grad_branch_two = grad_out * gate_two[:, None, :]
    grad_activated, grad_weight_down = linear_back(grad_branch_two, activated, weight_down)
    grad_pre = jax.vjp(gelu_tanh, pre_act)[1](grad_activated)[0]
    grad_normed_two, grad_weight_up = linear_back(grad_pre, normed_two, weight_up)
    grad_middle, grad_shift_two, grad_scale_two = jax.vjp(modulate, middle, shift_two, scale_two)[
        1
    ](grad_normed_two)
    grad_middle = grad_middle + grad_out
    grad_gate_one = jnp.sum(grad_middle * branch_one, axis=1)
    grad_branch_one = grad_middle * gate_one[:, None, :]
    grad_attended, grad_weight_proj = linear_back(grad_branch_one, attended, weight_proj)
    grad_packed = attention_backward(grad_attended, packed, log_total)
    grad_normed_one, grad_weight_qkv = linear_back(grad_packed, normed_one, weight_qkv)
    grad_hidden, grad_shift_one, grad_scale_one = jax.vjp(modulate, hidden, shift_one, scale_one)[
        1
    ](grad_normed_one)
    grad_hidden = grad_hidden + grad_middle
    grad_modulation = jnp.concatenate(
        [
            grad_shift_one,
            grad_scale_one,
            grad_gate_one,
            grad_shift_two,
            grad_scale_two,
            grad_gate_two,
        ],
        axis=-1,
    )
    grad_bias = jnp.concatenate(
        [
            total_rows(grad_packed),
            total_rows(grad_branch_one),
            total_rows(grad_pre),
            total_rows(grad_modulation),
            total_rows(grad_branch_two),
        ]
    )
    weight_grads = (grad_weight_qkv, grad_weight_proj, grad_weight_up, grad_weight_down)
    return (grad_hidden, weight_grads, grad_bias, grad_modulation)


def swap(array, mask, count):
    return lax.ppermute(array, "fsdp", [(place, place ^ mask) for place in range(count)])


def bit_of(position, bit):
    return (position >> bit) & 1


def pick(array, bits, chosen):
    sizes, starts, lengths = [], [], []
    previous = None
    for bit in bits:
        fixed = bit in chosen
        if fixed != previous:
            sizes.append(1)
            starts.append(0)
            lengths.append(1)
        sizes[-1] *= 2
        if fixed:
            starts[-1] = starts[-1] * 2 + chosen[bit]
        else:
            lengths[-1] *= 2
        previous = fixed
    tail = array.shape[1:]
    view = array.reshape(tuple(sizes) + tail)
    starts = [jnp.asarray(start, jnp.int32) for start in starts] + [jnp.int32(0)] * len(tail)
    taken = lax.dynamic_slice(view, starts, tuple(lengths) + tail)
    return taken.reshape((-1,) + tail)


def scatter_sum(parts, bit_order, position, count, kind):
    all_bits = list(reversed(range(count.bit_length() - 1)))
    held = [(parts, all_bits)]
    fixed = {}

    def total(chosen):
        summed = None
        for arrays, bits in held:
            wanted = {bit: value for bit, value in chosen.items() if bit in bits}
            piece = [pick(array, bits, wanted).astype(jnp.float32) for array in arrays]
            piece = piece[0] if len(piece) == 1 else jnp.concatenate(piece, axis=-1)
            summed = piece if summed is None else summed + piece
        return summed

    for bit in bit_order:
        mine = bit_of(position, bit)
        sent = total({**fixed, bit: 1 - mine}).astype(kind)
        received = swap(sent, 1 << bit, count)
        fixed[bit] = mine
        held.append(([received], [other for other in all_bits if other not in fixed]))
    return total(fixed)[0]


def gather_all(array, count):
    blocks = array[None]
    mask = 1
    while mask < count:
        blocks = jnp.concatenate([blocks, swap(blocks, mask, count)], axis=0)
        mask *= 2
    return blocks


def sum_all(array, count):
    mask = 1
    while mask < count:
        array = array + swap(array, mask, count)
        mask *= 2
    return array


def split_high(values):
    return (values // 32).astype(jnp.bfloat16), (values % 32).astype(jnp.bfloat16)


def factored(weight, raw, row_old, col_old, row_square, col_square, row_old_sum, rows_all, clip):
    columns = weight.shape[-1]
    row_new = DECAY_RATE * row_old + (1.0 - DECAY_RATE) * (
        clip * (clip * (row_square / columns)) + FACTOR_EPS
    )
    col_new = DECAY_RATE * col_old + (1.0 - DECAY_RATE) * (
        clip * (clip * (col_square / rows_all)) + FACTOR_EPS
    )
    row_mean = (
        DECAY_RATE * row_old_sum
        + (1.0 - DECAY_RATE) * (clip * (clip * (jnp.sum(col_square) / columns)))
    ) / rows_all + (1.0 - DECAY_RATE) * FACTOR_EPS
    clipped = clip * raw
    estimate = row_new[:, None] * col_new[None, :] / row_mean
    return (weight - LEARN_RATE * clipped * lax.rsqrt(estimate), clipped, row_new, col_new)


def body(
    count,
    latents,
    targets,
    features,
    time_weights,
    timesteps,
    classes,
    block_in,
    block_in_rows,
    block_in_cols,
    block_down,
    block_down_rows,
    block_down_cols,
    stem_main,
    stem_main_rows,
    stem_main_cols,
    stem_proj,
    stem_proj_rows,
    stem_proj_cols,
    head_weight,
    head_rows,
    head_cols,
    biases,
    bias_second,
):
    position = lax.axis_index("fsdp")
    images = count * latents.shape[0]
    width_rows = block_in.shape[1]
    down_rows = block_down.shape[1]
    proj_rows = stem_proj.shape[0]
    bias_part = biases.shape[0]
    bias_cols = -(-bias_part // width_rows)
    bits = count.bit_length() - 1
    deep_bits = list(reversed(range(3, bits)))
    order_a = [bit for bit in (0, 1, 2) if bit < bits] + deep_bits
    order_b = [bit for bit in (0, 2, 1) if bit < bits] + deep_bits
    to_canonical = (
        (jnp.arange(count)[:, None] ^ jnp.arange(count)[None, :]) == position
    ).astype(jnp.bfloat16)

    def gather_ordered(array):
        blocks = gather_all(array, count)
        flat = blocks.reshape(count, -1)
        ordered = jnp.dot(to_canonical, flat, preferred_element_type=jnp.float32)
        return ordered.astype(jnp.bfloat16).reshape(blocks.shape)

    def bias_blocks(values):
        return jnp.pad(values, ((0, 0), (0, width_rows * bias_cols - bias_part))).reshape(
            values.shape[0], width_rows, bias_cols
        )

    time_out_part, final_ada_part, table_part, patch_part, proj_one_part, time_in_part = cut_parts(
        stem_main, [D, 2 * D, NCLS, PD, P_SIZE, TF]
    )
    time_high, time_low = split_high(timesteps)
    class_high, class_low = split_high(classes)
    marks = jnp.stack([time_high, time_low, class_high, class_low], axis=1)
    marks = jnp.broadcast_to(marks.reshape(1, 4), (width_rows, 4))
    small_pack = jnp.concatenate(
        [
            time_out_part.astype(jnp.bfloat16),
            time_in_part.astype(jnp.bfloat16),
            table_part.astype(jnp.bfloat16),
            patch_part.astype(jnp.bfloat16),
            marks,
            bias_blocks(biases[None])[0].astype(jnp.bfloat16),
        ],
        axis=1,
    )
    used = small_pack.shape[1]
    small_pack = jnp.pad(small_pack, ((0, 0), (0, -used % 128)))
    stem_low = lax.all_gather(small_pack, "fsdp", axis=0, tiled=True)
    time_out, time_in, table_t, patch_t, mark_cols, bias_low, _ = cut_parts(
        stem_low, [D, TF, NCLS, PD, 4, bias_cols, 0]
    )
    mark_all = mark_cols.reshape(count, width_rows, 4)[:, 0].astype(jnp.int32)
    times_all = mark_all[:, 0] * 32 + mark_all[:, 1]
    classes_all = mark_all[:, 2] * 32 + mark_all[:, 3]
    bias_full = (
        bias_low.reshape(count, width_rows * bias_cols)[:, :bias_part]
        .reshape(-1)
        .astype(jnp.float32)
    )
    block_bias = bias_full[: L * VB].reshape(L, VB)
    stem_bias = bias_full[L * VB :]
    bias_tin, bias_tout, bias_final, bias_patch, bias_one, bias_two, bias_three = cut_parts(
        stem_bias, [D, D, 2 * D, D, P_SIZE, P_SIZE, Z]
    )

    freq_low = time_freq(times_all).astype(jnp.bfloat16)
    embed_hidden = (
        lax.dot_general(
            freq_low, time_in, (((1,), (1,)), ((), ())), preferred_element_type=jnp.float32
        )
        + bias_tin
    )
    embed_act = jax.nn.silu(embed_hidden).astype(jnp.bfloat16)
    one_hot = classes_all[:, None] == jnp.arange(NCLS)[None, :]
    class_embed = lax.dot_general(
        one_hot.astype(jnp.bfloat16),
        table_t,
        (((1,), (1,)), ((), ())),
        preferred_element_type=jnp.float32,
    )
    condition = linear(embed_act, time_out) + bias_tout + class_embed
    cond_low = jax.nn.silu(condition).astype(jnp.bfloat16)

    def my_columns(values):
        return lax.dynamic_slice_in_dim(values, position * width_rows, width_rows, axis=1)

    cond_mine = my_columns(cond_low)
    ada_mine = jnp.concatenate(
        [block_in[level, :, 3 * D + D + F :] for level in range(L)] + [final_ada_part], axis=1
    ).astype(jnp.bfloat16)
    mod_part = linear(cond_mine, ada_mine)[:, None, :]
    mods = scatter_sum([mod_part], order_a, position, count, jnp.float32)
    bias_ada = jnp.concatenate(
        [block_bias[level, 3 * D + D + F : 3 * D + D + F + 6 * D] for level in range(L)]
        + [bias_final]
    )
    mods = mods + bias_ada[None, :]

    latent_low = latents.astype(jnp.bfloat16)
    hidden = (
        lax.dot_general(
            latent_low, patch_t, (((2,), (1,)), ((), ())), preferred_element_type=jnp.float32
        )
        + bias_patch
        + positions()
    )
    main_width = 3 * D + D + F
    layers_low = [
        (
            lax.all_gather(
                block_in[level, :, :main_width].astype(jnp.bfloat16), "fsdp", axis=0, tiled=True
            ),
            lax.all_gather(block_down[level].astype(jnp.bfloat16), "fsdp", axis=0, tiled=True),
        )
        for level in range(L)
    ]
    proj_one = lax.all_gather(proj_one_part.astype(jnp.bfloat16), "fsdp", axis=0, tiled=True)
    proj_low = lax.all_gather(stem_proj.astype(jnp.bfloat16), "fsdp", axis=0, tiled=True)
    proj_two, proj_three = cut_parts(proj_low, [P_SIZE, Z])
    inputs_seen = []
    saved_caches = []
    first_out = hidden
    for level in range(L):
        inputs_seen.append(hidden)
        modulation = mods[:, level * 6 * D : (level + 1) * 6 * D]
        hidden, layer_cache = layer_forward(
            hidden, modulation, layers_low[level], block_bias[level]
        )
        saved_caches.append(layer_cache)
        if level == 0:
            first_out = hidden
    first_low = first_out.astype(jnp.bfloat16)
    proj_pre_one = linear(first_low, proj_one) + bias_one
    proj_act_one = jax.nn.silu(proj_pre_one).astype(jnp.bfloat16)
    proj_pre_two = linear(proj_act_one, proj_two) + bias_two
    proj_act_two = jax.nn.silu(proj_pre_two).astype(jnp.bfloat16)
    projected = linear(proj_act_two, proj_three) + bias_three
    cosine_part, cosine_pull = jax.vjp(lambda values: cosine_loss(values, features), projected)
    shift_final, scale_final = jnp.split(mods[:, L * 6 * D :], 2, axis=-1)
    final_normed, final_pull = jax.vjp(modulate, hidden, shift_final, scale_final)
    final_low = final_normed.astype(jnp.bfloat16)
    head_low = head_weight[:D].astype(jnp.bfloat16)
    output = linear(final_low, head_low) + head_weight[D]
    residual = output - targets
    local_loss = jnp.sum(time_weights * jnp.mean(residual * residual, axis=(1, 2))) + cosine_part
    grad_output = 2.0 / (TOK * PD) * time_weights[:, None, None] * residual
    grad_output_low = grad_output.astype(jnp.bfloat16)
    grad_final = lax.dot_general(
        grad_output_low, head_low, (((2,), (1,)), ((), ())), preferred_element_type=jnp.float32
    )
    grad_head = lax.dot_general(
        final_low,
        grad_output_low,
        (((0, 1), (0, 1)), ((), ())),
        preferred_element_type=jnp.float32,
    )
    grad_head_full = jnp.concatenate([grad_head, total_rows(grad_output)[None, :]], axis=0)
    grad_hidden, grad_shift_final, grad_scale_final = final_pull(grad_final)
    grad_final_mods = jnp.concatenate([grad_shift_final, grad_scale_final], axis=-1)

    grad_projected = cosine_pull(jnp.float32(1.0))[0]
    grad_act_two, grad_proj_three = linear_back(grad_projected, proj_act_two, proj_three)
    grad_pre_two = silu_back(proj_pre_two, grad_act_two)
    grad_act_one, grad_proj_two = linear_back(grad_pre_two, proj_act_one, proj_two)
    grad_pre_one = silu_back(proj_pre_one, grad_act_one)
    grad_first, grad_proj_one = linear_back(grad_pre_one, first_low, proj_one)

    def by_owner(values):
        return values.reshape(count, -1, values.shape[-1])

    def summed(parts, order):
        return scatter_sum([by_owner(part) for part in parts], order, position, count, jnp.bfloat16)

    bias_grads = [None] * L
    mod_grads = [None] * L
    grad_hidden, weight_grads, bias_grads[1], mod_grads[1] = layer_backward(
        grad_hidden, inputs_seen[1], layers_low[1], saved_caches[1]
    )
    down_one = summed(weight_grads[3:], order_a)
    in_one = summed(list(weight_grads[:3]) + [grad_proj_one], order_b)
    proj_shard = summed([grad_proj_two, grad_proj_three], order_a)
    grad_hidden, weight_grads, bias_grads[0], mod_grads[0] = layer_backward(
        grad_hidden + grad_first, inputs_seen[0], layers_low[0], saved_caches[0]
    )
    down_zero = summed(weight_grads[3:], order_b)
    late_zero = summed(weight_grads[1:3], order_a)
    grad_patch = lax.dot_general(
        grad_hidden.astype(jnp.bfloat16),
        latent_low,
        (((0, 1), (0, 1)), ((), ())),
        preferred_element_type=jnp.float32,
    )
    grad_bias_all = jnp.concatenate(
        bias_grads
        + [
            jnp.zeros((2 * D,), jnp.float32),
            total_rows(grad_final_mods),
            total_rows(grad_hidden),
            total_rows(grad_pre_one),
            total_rows(grad_pre_two),
            total_rows(grad_projected),
        ]
    )
    bias_piece = bias_blocks(grad_bias_all.reshape(count, bias_part))
    extra = PD + bias_cols
    last_piece = jnp.concatenate(
        [
            by_owner(grad_patch.astype(jnp.bfloat16)),
            bias_piece.astype(jnp.bfloat16),
            jnp.zeros((count, width_rows, -extra % 128), jnp.bfloat16),
        ],
        axis=-1,
    )
    last_zero = scatter_sum(
        [by_owner(weight_grads[0]), last_piece], order_b, position, count, jnp.bfloat16
    )
    patch_shard = last_zero[:, 3 * D : 3 * D + PD]
    bias_shard = last_zero[:, 3 * D + PD : 3 * D + extra].reshape(-1)[:bias_part]

    grad_mods = jnp.concatenate(mod_grads + [grad_final_mods], axis=-1).astype(jnp.bfloat16)
    grad_mods_all = gather_ordered(grad_mods[0])
    grad_ada_mine = lax.dot_general(
        cond_mine, grad_mods_all, (((0,), (0,)), ((), ())), preferred_element_type=jnp.float32
    )
    grad_cond_mine = lax.dot_general(
        grad_mods_all, ada_mine, (((1,), (1,)), ((), ())), preferred_element_type=jnp.float32
    )
    grad_condition = silu_back(my_columns(condition), grad_cond_mine)
    grad_table = lax.dot_general(
        grad_condition,
        one_hot.astype(jnp.float32),
        (((0,), (0,)), ((), ())),
        precision=lax.Precision.HIGHEST,
    )
    grad_condition_low = gather_ordered(grad_condition.astype(jnp.bfloat16))
    grad_condition_low = jnp.transpose(grad_condition_low, (1, 0, 2)).reshape(images, D)
    grad_time_out = lax.dot_general(
        my_columns(embed_act),
        grad_condition_low,
        (((0,), (0,)), ((), ())),
        preferred_element_type=jnp.float32,
    )
    grad_embed_act = lax.dot_general(
        grad_condition_low,
        time_out_part.astype(jnp.bfloat16),
        (((1,), (1,)), ((), ())),
        preferred_element_type=jnp.float32,
    )
    grad_embed = silu_back(my_columns(embed_hidden), grad_embed_act)
    grad_time_in = lax.dot_general(
        grad_embed.astype(jnp.bfloat16),
        freq_low,
        (((0,), (0,)), ((), ())),
        preferred_element_type=jnp.float32,
    )
    late_bias = jnp.zeros((2, D), jnp.float32)
    late_bias = lax.dynamic_update_slice(
        late_bias,
        jnp.stack([jnp.sum(grad_embed, axis=0), jnp.sum(grad_condition, axis=0)]),
        (0, position * width_rows),
    )

    ada_zero, ada_one, grad_final_ada = cut_parts(grad_ada_mine, [6 * D, 6 * D, 2 * D])
    raw_in = jnp.stack(
        [
            jnp.concatenate([last_zero[:, : 3 * D], late_zero, ada_zero], axis=1),
            jnp.concatenate([in_one[:, :main_width], ada_one], axis=1),
        ]
    )
    raw_down = jnp.stack([down_zero, down_one])
    raw_main = jnp.concatenate(
        [
            grad_time_out,
            grad_final_ada,
            grad_table,
            patch_shard,
            in_one[:, main_width:],
            grad_time_in,
        ],
        axis=1,
    )
    raw_proj = proj_shard
    raws = [raw_in[0], raw_in[1], raw_down[0], raw_down[1], raw_main, raw_proj]
    row_olds = [
        block_in_rows[0],
        block_in_rows[1],
        block_down_rows[0],
        block_down_rows[1],
        stem_main_rows,
        stem_proj_rows,
    ]
    squares = [raw * raw for raw in raws]
    row_squares = [jnp.sum(square, axis=1) for square in squares]
    late_list = [jnp.sum(square, axis=0) for square in squares] + [
        jnp.stack([jnp.sum(row_old) for row_old in row_olds]),
        jnp.stack([jnp.sum(bias_shard * bias_shard), local_loss]),
        late_bias.reshape(-1),
        grad_head_full.reshape(-1),
    ]
    late_sizes = [values.shape[0] for values in late_list]
    late_all = jnp.concatenate(late_list)
    late_all = jnp.pad(late_all, (0, -late_all.shape[0] % 1024)).reshape(-1, 128)
    late_all = sum_all(late_all, count).reshape(-1)
    late_sums = []
    running = 0
    for size in late_sizes:
        late_sums.append(late_all[running : running + size])
        running += size
    col_squares = late_sums[:6]
    row_old_sums, bias_loss, late_bias, head_sum = late_sums[6:]
    head_sum = head_sum.reshape(D + 1, PD)
    loss_total = bias_loss[1]
    total_square = bias_loss[0] + jnp.sum(late_bias * late_bias) + jnp.sum(head_sum * head_sum)
    for col_square in col_squares:
        total_square = total_square + jnp.sum(col_square)
    grad_norm = jnp.sqrt(total_square)
    clip = jnp.minimum(1.0, CLIP_LIMIT / grad_norm)

    weights = [block_in[0], block_in[1], block_down[0], block_down[1], stem_main, stem_proj]
    col_olds = [
        block_in_cols[0],
        block_in_cols[1],
        block_down_cols[0],
        block_down_cols[1],
        stem_main_cols,
        stem_proj_cols,
    ]
    results = [
        factored(
            weights[slot],
            raws[slot],
            row_olds[slot],
            col_olds[slot],
            row_squares[slot],
            col_squares[slot],
            row_old_sums[slot],
            count * weights[slot].shape[0],
            clip,
        )
        for slot in range(6)
    ]
    new_in, clip_in, rows_in, cols_in = [
        jnp.stack([results[0][part], results[1][part]]) for part in range(4)
    ]
    new_down, clip_down, rows_down, cols_down = [
        jnp.stack([results[2][part], results[3][part]]) for part in range(4)
    ]
    new_main, clip_main, rows_main, cols_main = results[4]
    new_proj, clip_proj, rows_proj, cols_proj = results[5]
    head_square = head_sum * head_sum
    new_head, head_clip, rows_head, cols_head = factored(
        head_weight,
        head_sum,
        head_rows,
        head_cols,
        jnp.sum(head_square, axis=1),
        jnp.sum(head_square, axis=0),
        jnp.sum(head_rows),
        D + 1,
        clip,
    )
    late_flat = jnp.zeros((count * bias_part,), jnp.float32)
    late_flat = lax.dynamic_update_slice(late_flat, late_bias, (L * VB,))
    bias_raw = bias_shard + lax.dynamic_slice(late_flat, (position * bias_part,), (bias_part,))
    clip_bias = clip * bias_raw
    second_new = DECAY_RATE * bias_second + (1.0 - DECAY_RATE) * (
        clip_bias * clip_bias + FACTOR_EPS
    )
    new_bias = biases - LEARN_RATE * clip_bias * lax.rsqrt(second_new)
    return (
        loss_total,
        grad_norm,
        new_in,
        clip_in,
        rows_in,
        cols_in,
        new_in.astype(jnp.bfloat16),
        new_down,
        clip_down,
        rows_down,
        cols_down,
        new_down.astype(jnp.bfloat16),
        new_main,
        clip_main,
        rows_main,
        cols_main,
        new_main.astype(jnp.bfloat16),
        new_proj,
        clip_proj,
        rows_proj,
        cols_proj,
        new_proj.astype(jnp.bfloat16),
        new_head,
        head_clip,
        rows_head,
        cols_head,
        new_bias,
        clip_bias,
        second_new,
    )


def solution(mesh):
    return jax.shard_map(
        functools.partial(body, mesh.shape["fsdp"]),
        mesh=mesh,
        in_specs=(
            P("fsdp", None, None),
            P("fsdp", None, None),
            P("fsdp", None, None),
            P("fsdp"),
            P("fsdp"),
            P("fsdp"),
            P(None, "fsdp", None),
            P(None, "fsdp"),
            P(),
            P(None, "fsdp", None),
            P(None, "fsdp"),
            P(),
            P("fsdp", None),
            P("fsdp"),
            P(),
            P("fsdp", None),
            P("fsdp"),
            P(),
            P(),
            P(),
            P(),
            P("fsdp"),
            P("fsdp"),
        ),
        out_specs=(
            P(),
            P(),
            P(None, "fsdp", None),
            P(None, "fsdp", None),
            P(None, "fsdp"),
            P(),
            P(None, "fsdp", None),
            P(None, "fsdp", None),
            P(None, "fsdp", None),
            P(None, "fsdp"),
            P(),
            P(None, "fsdp", None),
            P("fsdp", None),
            P("fsdp", None),
            P("fsdp"),
            P(),
            P("fsdp", None),
            P("fsdp", None),
            P("fsdp", None),
            P("fsdp"),
            P(),
            P("fsdp", None),
            P(),
            P(),
            P(),
            P(),
            P("fsdp"),
            P("fsdp"),
            P("fsdp"),
        ),
        check_vma=False,
    )
```

```python
import functools
import math

import jax
import jax.numpy as jnp
from jax import lax
from jax.experimental import pallas as pl
from jax.experimental.pallas import tpu as pltpu
from jax.sharding import PartitionSpec as P

D = 768
HD = 64
F = 3072
P_SIZE = 2048
Z = 768
NCLS = 1001
PD = 16
TF = 256
L = 2
GRID = 16
TOK = 256
VB = 11520


NORM_EPS = 1e-06
SCORE_SCALE = 0.125
LEARN_RATE = 0.03
DECAY_RATE = 0.5
CLIP_LIMIT = 0.05
FACTOR_EPS = 1e-30


def cut_parts(array, part_widths):
    borders = []
    running = 0
    for part_width in part_widths[:-1]:
        running += part_width
        borders.append(running)
    return jnp.split(array, borders, axis=-1)


def positions():
    quarter = D // 4
    omega_rate = jnp.exp(-math.log(10000.0) * jnp.arange(quarter, dtype=jnp.float32) / quarter)
    token_place = jnp.arange(TOK)
    column = (token_place % GRID).astype(jnp.float32)
    row_place = (token_place // GRID).astype(jnp.float32)

    def encode(coords):
        angles = coords[:, None] * omega_rate[None, :]
        return jnp.concatenate([jnp.sin(angles), jnp.cos(angles)], axis=1)

    return jnp.concatenate([encode(column), encode(row_place)], axis=1)


def time_freq(timesteps):
    half_width = TF // 2
    freq_rate = jnp.exp(-math.log(10000.0) * jnp.arange(half_width, dtype=jnp.float32) / half_width)
    angles = timesteps.astype(jnp.float32)[:, None] * freq_rate[None, :]
    return jnp.concatenate([jnp.cos(angles), jnp.sin(angles)], axis=1)


def silu_back(before, grad_after):
    return jax.vjp(jax.nn.silu, before)[1](grad_after)[0]


def total_rows(values):
    return jnp.sum(values.reshape(-1, values.shape[-1]), axis=0)


def linear(left_side, weight_side):
    return jnp.dot(left_side, weight_side, preferred_element_type=jnp.float32)


LOW = jnp.bfloat16
FULL = jnp.float32


def dot(left, right):
    return jnp.dot(left, right, preferred_element_type=jnp.float32)


def dot_rows(left, right):
    return lax.dot_general(
        left, right, (((1,), (1,)), ((), ())), preferred_element_type=jnp.float32
    )


def dot_tokens(left, right):
    return lax.dot_general(
        left, right, (((0,), (0,)), ((), ())), preferred_element_type=jnp.float32
    )


def bf16(values):
    return values.astype(jnp.bfloat16)


def moved(values, order):
    return bf16(dot(values, order))


def moved_back(values, order):
    return bf16(dot_rows(values, order))


def moved_back_wide(values, order):
    high = bf16(values)
    return dot_rows(high, order) + dot_rows(bf16(values - high.astype(FULL)), order)


def row_sum(values):
    return jnp.sum(values, axis=0, keepdims=True)


def norm_parts(values):
    centred = values - jnp.mean(values, axis=-1, keepdims=True)
    scale = lax.rsqrt(jnp.mean(centred * centred, axis=-1, keepdims=True) + NORM_EPS)
    return centred * scale, scale


def norm_back(unit, scale, grad_unit):
    mean_grad = jnp.mean(grad_unit, axis=-1, keepdims=True)
    mean_both = jnp.mean(grad_unit * unit, axis=-1, keepdims=True)
    return scale * (grad_unit - mean_grad - unit * mean_both)


GELU_ROOT = math.sqrt(2.0 / math.pi)
GELU_CUBE = 0.044715


def gelu_parts(values):
    square = values * values
    bent = jnp.tanh(GELU_ROOT * values * (1.0 + GELU_CUBE * square))
    half = 0.5 * (1.0 + bent)
    slope = half + 0.5 * values * (1.0 - bent * bent) * GELU_ROOT * (
        1.0 + 3.0 * GELU_CUBE * square
    )
    return values * half, slope


def silu_parts(values):
    gate = jax.nn.sigmoid(values)
    return values * gate, gate * (1.0 + values * (1.0 - gate))


def half_lanes(shape, which):
    lane = lax.broadcasted_iota(jnp.int32, shape, 1)
    return (lane < HD) if which == 0 else (lane >= HD)


def fetch(source, target, semaphore):
    return pltpu.make_async_copy(source, target, semaphore)


def group_of(groups, place, block, half):
    base = 5 * (place // 4)
    if place % 4 < 3:
        return groups[base + place % 4].at[block]
    if block < half:
        return groups[base + 3].at[block]
    return groups[base + 4].at[block - half]


def load_blocks(groups, half, first, size, held, semaphores, rows):
    copies = []
    for block in range(size):
        copies.append(
            [
                fetch(
                    group_of(groups, place, first + block, half),
                    held.at[block, pl.ds(place * rows, rows)],
                    semaphores.at[block, place],
                )
                for place in range(8)
            ]
        )
    return copies


def start_all(copies):
    for copy in copies:
        copy.start()


def wait_all(copies):
    for copy in copies:
        copy.wait()


def depth_of(relative, index):
    if not relative:
        return index
    return index ^ (lax.axis_index("fsdp") // 8)


def attn_forward_kernel(
    half,
    hidden,
    mods,
    bias,
    order,
    *refs,
):
    groups = refs[:10]
    normed_out, packed_out, log_out, attended_out, branch_out, middle_out = refs[10:16]
    held, attended, semaphores = refs[16:]
    copies = load_blocks(groups, half, 0, 4, held, semaphores, 96)
    for block in range(4):
        start_all(copies[block])
    unit, _ = norm_parts(hidden[...])
    normed_out[...] = moved(bf16(unit * (1.0 + mods[1:2]) + mods[0:1]), order[...])
    for block in range(3):
        wait_all(copies[block])
        packed_out[block] = bf16(dot(normed_out[...], held[block]) + bias[block : block + 1])
    lanes = lax.broadcasted_iota(jnp.int32, (TOK, 128), 1)

    def pair(index, logs):
        columns = pl.ds(pl.multiple_of(index * 128, 128), 128)
        queries, keys, values = (packed_out[part, :, columns] for part in range(3))
        halves = []
        for which in range(2):
            mask = half_lanes((TOK, 128), which)
            scores = dot_rows(jnp.where(mask, queries, 0), keys) * SCORE_SCALE
            top = jnp.max(scores, axis=-1, keepdims=True)
            raised = jnp.exp(scores - top)
            total = jnp.sum(raised, axis=-1, keepdims=True)
            halves.append(dot(bf16(raised * (1.0 / total)), values))
            logs = jnp.where(lanes == 2 * index + which, top + jnp.log(total), logs)
        attended[:, columns] = bf16(jnp.where(half_lanes((TOK, 128), 0), *halves))
        return logs

    log_out[...] = lax.fori_loop(0, D // 128, pair, jnp.zeros((TOK, 128), jnp.float32))
    attended_out[...] = moved(attended[...], order[...])
    wait_all(copies[3])
    branch = dot(attended_out[...], held[3]) + bias[3:4]
    branch_out[...] = branch
    middle_out[...] = hidden[...] + mods[2:3] * branch


def mlp_forward_kernel(half, first_down, relative, middle, mods, bias, order, down_order, *refs):
    groups = refs[:10]
    normed_out, slope_out, active_out, branch_out, hidden_out = refs[10:15]
    held_up, held_down, total, before, semaphores_up, semaphores_down = refs[15:]
    ups = load_blocks(groups, half, 4, 4, held_up, semaphores_up, 96)
    downs = load_blocks(groups, half, first_down, 4, held_down, semaphores_down, 96)
    for block in range(4):
        start_all(ups[block])
    for block in range(4):
        start_all(downs[block])
    unit, _ = norm_parts(middle[...])
    normed_out[...] = moved(bf16(unit * (1.0 + mods[4:5]) + mods[3:4]), order[...])
    for block in range(4):
        wait_all(ups[block])
        before[block] = dot(normed_out[...], held_up[block]) + bias[block + 4 : block + 5]
    for depth in range(4):
        active, slope = gelu_parts(before[depth_of(relative, depth)])
        active_out[depth] = moved(bf16(active), down_order[...])
        slope_out[depth] = moved(bf16(slope), down_order[...])
        wait_all(downs[depth])
        part = dot(active_out[depth], held_down[depth])
        total[...] = part if depth == 0 else total[...] + part
    branch = total[...] + bias[14:15]
    branch_out[...] = branch
    hidden_out[...] = middle[...] + mods[5:6] * branch


def mlp_backward_kernel(
    half,
    first_down,
    relative,
    grad_out,
    mods,
    middle,
    normed,
    slope,
    active,
    branch,
    order,
    down_order,
    *refs,
):
    groups = refs[:10]
    grad_middle_out, grad_mods_out, grad_bias_out, mine_out = refs[10:14]
    theirs_out = refs[14:18]
    held_up, held_down, made, low, grad_normed, semaphores_up, semaphores_down, sent = refs[18:]
    ups = load_blocks(groups, half, 4, 4, held_up, semaphores_up, 96)
    downs = load_blocks(groups, half, first_down, 4, held_down, semaphores_down, 96)
    for block in range(4):
        start_all(downs[block])
    for block in range(4):
        start_all(ups[block])
    grad_hidden = grad_out[...]
    grad_branch = grad_hidden * mods[5:6]
    grad_mods_out[2:3] = row_sum(grad_hidden * branch[...])
    grad_bias_out[4:5] = row_sum(grad_branch)
    grad_low = bf16(grad_branch)
    given = []
    for depth in range(4):
        wait_all(downs[depth])
        grad_active = dot_rows(grad_low, held_down[depth])
        made[4 + depth] = bf16(dot_tokens(active[depth], grad_low))
        given += give(made, 4 + depth, mine_out, theirs_out, sent)
        before_low = moved_back(
            bf16(grad_active * slope[depth].astype(FULL)), down_order[...]
        )
        low[depth_of(relative, depth)] = before_low
    for block in range(4):
        before_low = low[block]
        grad_bias_out[block : block + 1] = row_sum(before_low.astype(FULL))
        made[block] = bf16(dot_tokens(normed[...], before_low))
        given += give(made, block, mine_out, theirs_out, sent)
        wait_all(ups[block])
        part = dot_rows(before_low, held_up[block])
        grad_normed[...] = part if block == 0 else grad_normed[...] + part
    unit, scale = norm_parts(middle[...])
    grad_unit = moved_back_wide(grad_normed[...], order[...])
    grad_mods_out[0:1] = row_sum(grad_unit)
    grad_mods_out[1:2] = row_sum(grad_unit * unit)
    grad_middle_out[...] = grad_hidden + norm_back(unit, scale, grad_unit * (1.0 + mods[4:5]))
    wait_all(given)


def give(made, block, mine_out, theirs_outs, sent):
    length = made.shape[1] // 2
    step = theirs_outs[0].shape[0]
    theirs_out = theirs_outs[block // step].at[block % step]
    copies = [
        fetch(made.at[block, pl.ds(0, length)], mine_out.at[block], sent.at[0, block]),
        fetch(made.at[block, pl.ds(length, length)], theirs_out, sent.at[1, block]),
    ]
    start_all(copies)
    return copies


def attn_backward_kernel(
    half,
    grad_middle,
    mods,
    hidden,
    normed,
    packed,
    logs,
    attended,
    branch,
    order,
    *refs,
):
    groups = refs[:10]
    grad_hidden_out, grad_mods_out, grad_bias_out, mine_out = refs[10:14]
    theirs_out = refs[14:16]
    held, made, grad_packed, grad_attended, grad_normed, semaphores, sent = refs[16:]
    copies = load_blocks(groups, half, 0, 4, held, semaphores, 96)
    for block in (3, 0, 1, 2):
        start_all(copies[block])
    grad_mid = grad_middle[...]
    grad_branch = grad_mid * mods[2:3]
    grad_mods_out[2:3] = row_sum(grad_mid * branch[...])
    grad_bias_out[3:4] = row_sum(grad_branch)
    grad_low = bf16(grad_branch)
    made[3] = bf16(dot_tokens(attended[...], grad_low))
    given = give(made, 3, mine_out, theirs_out, sent)
    wait_all(copies[3])
    grad_attended[...] = moved_back(bf16(dot_rows(grad_low, held[3])), order[...])
    lanes = lax.broadcasted_iota(jnp.int32, (TOK, 128), 1)
    first = half_lanes((TOK, 128), 0)

    def pair(index, carry):
        columns = pl.ds(pl.multiple_of(index * 128, 128), 128)
        queries, keys, values = (packed[part, :, columns] for part in range(3))
        grad_pair = grad_attended[:, columns]
        grads = []
        for which in range(2):
            mask = half_lanes((TOK, 128), which)
            log_total = jnp.sum(
                jnp.where(lanes == 2 * index + which, logs[...], 0.0), axis=-1, keepdims=True
            )
            scores = dot_rows(jnp.where(mask, queries, 0), keys) * SCORE_SCALE
            attention = jnp.exp(scores - log_total)
            grad_attention = dot_rows(jnp.where(mask, grad_pair, 0), values)
            grad_values = dot_tokens(bf16(attention), grad_pair)
            weighted = attention * grad_attention
            grad_scores = weighted - attention * jnp.sum(weighted, axis=-1, keepdims=True)
            score_low = bf16(grad_scores * SCORE_SCALE)
            grads.append((dot(score_low, keys), dot_tokens(score_low, queries), grad_values))
        for part in range(3):
            both = jnp.where(first, grads[0][part], grads[1][part])
            grad_bias_out[part : part + 1, columns] = row_sum(both)
            grad_packed[part, :, columns] = bf16(both)
        return carry

    lax.fori_loop(0, D // 128, pair, 0)
    for block in range(3):
        grad_part = grad_packed[block]
        made[block] = bf16(dot_tokens(normed[...], grad_part))
        given += give(made, block, mine_out, theirs_out, sent)
        wait_all(copies[block])
        part = dot_rows(grad_part, held[block])
        grad_normed[...] = part if block == 0 else grad_normed[...] + part
    unit, scale = norm_parts(hidden[...])
    grad_unit = moved_back_wide(grad_normed[...], order[...])
    grad_mods_out[0:1] = row_sum(grad_unit)
    grad_mods_out[1:2] = row_sum(grad_unit * unit)
    grad_hidden_out[...] = grad_mid + norm_back(unit, scale, grad_unit * (1.0 + mods[1:2]))
    wait_all(given)


ONE_WIDTHS = (D, D, P_SIZE - 2 * D)
REST = P_SIZE + Z
CHUNK = P_SIZE // 4


def projector_kernel(
    half,
    first_one,
    relative,
    first,
    features,
    bias_one,
    bias_two,
    bias_three,
    order,
    chunk_order,
    *refs,
):
    groups, rest_groups = refs[:10], refs[10:20]
    outs = refs[20:32]
    grad_first_out, loss_out, grad_bias_one, grad_bias_two, grad_bias_three = outs[:5]
    one_mine, one_theirs, rest_mine, rest_theirs = outs[5], outs[6:7], outs[7], outs[8:]
    (
        held_one,
        held_rest,
        made_one,
        made_rest,
        slope_one,
        slope_two,
        active_one,
        active_two,
        wide,
        low,
        one_semaphores,
        rest_semaphores,
        one_sent,
        rest_sent,
    ) = refs[32:]
    ones = load_blocks(groups, half, first_one, 3, held_one, one_semaphores, 96)
    rests = load_blocks(rest_groups, 2, 0, 4, held_rest, rest_semaphores, 64)
    for copies in ones + rests:
        start_all(copies)
    chunks = [pl.ds(CHUNK * index, CHUNK) for index in range(4)]

    def source(depth):
        return pl.ds(pl.multiple_of(depth_of(relative, depth) * CHUNK, CHUNK), CHUNK)

    def bend(active, slope):
        for depth in range(4):
            values, slopes = silu_parts(wide[:, source(depth)])
            active[:, chunks[depth]] = moved(bf16(values), chunk_order[...])
            slope[:, chunks[depth]] = moved(bf16(slopes), chunk_order[...])

    first_low = moved(bf16(first[...]), order[...])
    running = 0
    for block, width in enumerate(ONE_WIDTHS):
        columns = slice(running, running + width)
        wait_all(ones[block])
        wide[:, columns] = dot(first_low, held_one[block, :, :width]) + bias_one[:, columns]
        running += width
    bend(active_one, slope_one)
    for copies in rests:
        wait_all(copies)

    def product(left, columns):
        total = dot(left[:, chunks[0]], held_rest[0, :, columns])
        for depth in range(1, 4):
            total = total + dot(left[:, chunks[depth]], held_rest[depth, :, columns])
        return total

    for index in range(4):
        wide[:, chunks[index]] = product(active_one, chunks[index]) + bias_two[:, chunks[index]]
    bend(active_two, slope_two)
    tail = pl.ds(P_SIZE, Z)
    result = product(active_two, tail) + bias_three[...]
    wanted = features[...]
    inner = jnp.sum(result * wanted, axis=-1, keepdims=True)
    own = jnp.sum(result * result, axis=-1, keepdims=True) + NORM_EPS
    length = jnp.sqrt(own) * jnp.sqrt(jnp.sum(wanted * wanted, axis=-1, keepdims=True) + NORM_EPS)
    cosine = inner / length
    loss_out[...] = jnp.broadcast_to(-0.5 / TOK * row_sum(cosine), (8, 128))
    grad_result = (-0.5 / TOK) * (wanted / length - result * (cosine / own))
    grad_bias_three[...] = row_sum(grad_result)
    grad_three = bf16(grad_result)
    for depth in range(4):
        made_rest[depth, :, tail] = bf16(dot_tokens(active_two[:, chunks[depth]], grad_three))

    def bend_back(grad, slope, depth, grad_bias):
        columns = source(depth)
        low[:, columns] = moved_back(
            bf16(grad * slope[:, chunks[depth]].astype(FULL)), chunk_order[...]
        )
        grad_bias[:, columns] = row_sum(low[:, columns].astype(FULL))

    for depth in range(4):
        bend_back(dot_rows(grad_three, held_rest[depth, :, tail]), slope_two, depth, grad_bias_two)
    given = []
    main = pl.ds(0, P_SIZE)
    for depth in range(4):
        made_rest[depth, :, main] = bf16(dot_tokens(active_one[:, chunks[depth]], low[...]))
        given += give(made_rest, depth, rest_mine, rest_theirs, rest_sent)
    for depth in range(4):
        wide[:, chunks[depth]] = dot_rows(low[...], held_rest[depth, :, main])
    for depth in range(4):
        bend_back(wide[:, chunks[depth]], slope_one, depth, grad_bias_one)
    running = 0
    grad_first = None
    for block, width in enumerate(ONE_WIDTHS):
        grad_part = low[:, running : running + width]
        made_one[block, :, :width] = bf16(dot_tokens(first_low, grad_part))
        if width < D:
            made_one[block, :, width:] = jnp.zeros((D, D - width), LOW)
        given += give(made_one, block, one_mine, one_theirs, one_sent)
        part = dot_rows(grad_part, held_one[block, :, :width])
        grad_first = part if grad_first is None else grad_first + part
        running += width
    grad_first_out[...] = moved_back_wide(grad_first, order[...])
    wait_all(given)


def head_kernel(
    hidden,
    mods,
    head,
    head_bias,
    targets,
    time_weight,
    grad_hidden_out,
    grad_mods_out,
    grad_head_out,
    grad_head_bias_out,
    loss_out,
):
    unit, scale = norm_parts(hidden[...])
    final_low = bf16(unit * (1.0 + mods[1:2]) + mods[0:1])
    residual = dot(final_low, head[...]) + head_bias[...] - targets[...]
    weight = time_weight[...]
    square = jnp.sum(row_sum(residual * residual), axis=1, keepdims=True)
    loss_out[...] = jnp.broadcast_to(square * weight / (TOK * PD), (8, 128))
    grad_output = (2.0 / (TOK * PD)) * weight * residual
    grad_head_bias_out[...] = row_sum(grad_output)
    grad_low = bf16(grad_output)
    grad_head_out[...] = dot_tokens(final_low, grad_low)
    grad_unit = dot_rows(grad_low, head[...])
    grad_mods_out[0:1] = row_sum(grad_unit)
    grad_mods_out[1:2] = row_sum(grad_unit * unit)
    grad_hidden_out[...] = norm_back(unit, scale, grad_unit * (1.0 + mods[1:2]))


def cost(microseconds):
    return pl.CostEstimate(flops=microseconds, bytes_accessed=0, transcendentals=0)


VMEM_WHOLE = pl.BlockSpec(memory_space=pltpu.VMEM)
IN_PLACE = pl.BlockSpec(memory_space=pl.ANY)


def shaped(kind, *shape):
    return jax.ShapeDtypeStruct(shape, kind)


def call(kernel, inputs, far_inputs, outputs, far_outputs, scratch, microseconds, limit):
    return pl.pallas_call(
        kernel,
        in_specs=[VMEM_WHOLE] * len(inputs) + [IN_PLACE] * len(far_inputs),
        out_specs=[VMEM_WHOLE] * len(outputs) + [IN_PLACE] * len(far_outputs),
        out_shape=[*outputs, *far_outputs],
        scratch_shapes=scratch,
        cost_estimate=cost(microseconds),
        compiler_params=pltpu.CompilerParams(vmem_limit_bytes=limit * 2**20),
    )(*inputs, *far_inputs)


BLOCK_SEMAPHORES = pltpu.SemaphoreType.DMA((4, 8))


def orders_kernel(narrow_source, down_source, chunk_source, narrow, down, chunk):
    for source, order in [(narrow_source, narrow), (down_source, down), (chunk_source, chunk)]:
        rows = lax.broadcasted_iota(jnp.int32, order.shape, 0)
        order[...] = jnp.where(rows == source[...], 1.0, 0.0).astype(LOW)


class Orders:
    def __init__(self, position, relative):
        self.relative = relative
        near, depth = (position & 7, position >> 3) if relative else (0, 0)

        def places(index):
            if not relative:
                return index
            return near ^ (((index & 3) << 1) | (index >> 2))

        column = jnp.arange(D)
        narrow = column
        if relative:
            group, deep, inner = column // 96, (column // 24) % 4, column % 24
            narrow = ((deep ^ depth) * 8 + places(group)) * 24 + inner
        down = places(column // 96) * 96 + column % 96
        column = jnp.arange(CHUNK)
        chunk = places(column // 64) * 64 + column % 64
        sources = [source[None].astype(jnp.int32) for source in (narrow, down, chunk)]
        self.narrow, self.down, self.chunk = pl.pallas_call(
            orders_kernel,
            in_specs=[VMEM_WHOLE] * 3,
            out_specs=[VMEM_WHOLE] * 3,
            out_shape=[shaped(LOW, D, D), shaped(LOW, D, D), shaped(LOW, CHUNK, CHUNK)],
            cost_estimate=cost(3),
            compiler_params=pltpu.CompilerParams(vmem_limit_bytes=16 * 2**20),
        )(*sources)


def attn_forward(hidden, mods, bias, orders, gathered):
    return call(
        functools.partial(attn_forward_kernel, gathered.half),
        [hidden, mods, bias, orders.narrow],
        gathered.groups,
        [
            shaped(LOW, TOK, D),
            shaped(LOW, 3, TOK, D),
            shaped(FULL, TOK, 128),
            shaped(LOW, TOK, D),
            shaped(FULL, TOK, D),
            shaped(FULL, TOK, D),
        ],
        [],
        [pltpu.VMEM((4, D, D), LOW), pltpu.VMEM((TOK, D), LOW), BLOCK_SEMAPHORES],
        11,
        32,
    )


def mlp_forward(middle, mods, bias, orders, gathered):
    return call(
        functools.partial(
            mlp_forward_kernel, gathered.half, gathered.first_down, orders.relative
        ),
        [middle, mods, bias, orders.narrow, orders.down],
        gathered.groups,
        [
            shaped(LOW, TOK, D),
            shaped(LOW, 4, TOK, D),
            shaped(LOW, 4, TOK, D),
            shaped(FULL, TOK, D),
            shaped(FULL, TOK, D),
        ],
        [],
        [
            pltpu.VMEM((4, D, D), LOW),
            pltpu.VMEM((4, D, D), LOW),
            pltpu.VMEM((TOK, D), FULL),
            pltpu.VMEM((4, TOK, D), FULL),
            BLOCK_SEMAPHORES,
            BLOCK_SEMAPHORES,
        ],
        11,
        40,
    )


def mlp_backward(grad_out, mods, kept, orders, gathered):
    return call(
        functools.partial(
            mlp_backward_kernel, gathered.half, gathered.first_down, orders.relative
        ),
        [grad_out, mods, *kept, orders.narrow, orders.down],
        gathered.groups,
        [shaped(FULL, TOK, D), shaped(FULL, 3, D), shaped(FULL, 5, D)],
        [shaped(LOW, 8, D // 2, D)] + [shaped(LOW, 2, D // 2, D)] * 4,
        [
            pltpu.VMEM((4, D, D), LOW),
            pltpu.VMEM((4, D, D), LOW),
            pltpu.VMEM((8, D, D), LOW),
            pltpu.VMEM((4, TOK, D), LOW),
            pltpu.VMEM((TOK, D), FULL),
            BLOCK_SEMAPHORES,
            BLOCK_SEMAPHORES,
            pltpu.SemaphoreType.DMA((2, 8)),
        ],
        16,
        48,
    )


def attn_backward(grad_middle, mods, kept, orders, gathered):
    return call(
        functools.partial(attn_backward_kernel, gathered.half),
        [grad_middle, mods, *kept, orders.narrow],
        gathered.groups,
        [shaped(FULL, TOK, D), shaped(FULL, 3, D), shaped(FULL, 4, D)],
        [shaped(LOW, 4, D // 2, D)] + [shaped(LOW, 2, D // 2, D)] * 2,
        [
            pltpu.VMEM((4, D, D), LOW),
            pltpu.VMEM((4, D, D), LOW),
            pltpu.VMEM((3, TOK, D), LOW),
            pltpu.VMEM((TOK, D), LOW),
            pltpu.VMEM((TOK, D), FULL),
            BLOCK_SEMAPHORES,
            pltpu.SemaphoreType.DMA((2, 4)),
        ],
        13,
        40,
    )


def projector(first, features, bias_one, bias_two, bias_three, orders, gathered, rest_gathered):
    return call(
        functools.partial(
            projector_kernel, gathered.half, gathered.first_one, orders.relative
        ),
        [first, features, bias_one, bias_two, bias_three, orders.narrow, orders.chunk],
        [*gathered.groups, *rest_gathered.groups],
        [
            shaped(FULL, TOK, D),
            shaped(FULL, 8, 128),
            shaped(FULL, 1, P_SIZE),
            shaped(FULL, 1, P_SIZE),
            shaped(FULL, 1, Z),
        ],
        [
            shaped(LOW, 3, D // 2, D),
            shaped(LOW, 3, D // 2, D),
            shaped(LOW, 4, CHUNK // 2, REST),
        ]
        + [shaped(LOW, 1, CHUNK // 2, REST)] * 4,
        [
            pltpu.VMEM((3, D, D), LOW),
            pltpu.VMEM((4, CHUNK, REST), LOW),
            pltpu.VMEM((3, D, D), LOW),
            pltpu.VMEM((4, CHUNK, REST), LOW),
            pltpu.VMEM((TOK, P_SIZE), LOW),
            pltpu.VMEM((TOK, P_SIZE), LOW),
            pltpu.VMEM((TOK, P_SIZE), LOW),
            pltpu.VMEM((TOK, P_SIZE), LOW),
            pltpu.VMEM((TOK, P_SIZE), FULL),
            pltpu.VMEM((TOK, P_SIZE), LOW),
            pltpu.SemaphoreType.DMA((3, 8)),
            BLOCK_SEMAPHORES,
            pltpu.SemaphoreType.DMA((2, 3)),
            pltpu.SemaphoreType.DMA((2, 4)),
        ],
        27,
        56,
    )


def head(hidden, mods, head_low, head_bias, targets, time_weight):
    return call(
        head_kernel,
        [hidden, mods, head_low, head_bias, targets, time_weight],
        [],
        [
            shaped(FULL, TOK, D),
            shaped(FULL, 2, D),
            shaped(FULL, D, PD),
            shaped(FULL, 1, PD),
            shaped(FULL, 8, 128),
        ],
        [],
        [],
        5,
        24,
    )


def swap(array, mask, count):
    return lax.ppermute(array, "fsdp", [(place, place ^ mask) for place in range(count)])


def bit_of(position, bit):
    return (position >> bit) & 1


def pick(array, bits, chosen):
    sizes, starts, lengths = [], [], []
    previous = None
    for bit in bits:
        fixed = bit in chosen
        if fixed != previous:
            sizes.append(1)
            starts.append(0)
            lengths.append(1)
        sizes[-1] *= 2
        if fixed:
            starts[-1] = starts[-1] * 2 + chosen[bit]
        else:
            lengths[-1] *= 2
        previous = fixed
    ahead, tail = array.shape[:1], array.shape[2:]
    view = array.reshape(ahead + tuple(sizes) + tail)
    starts = [jnp.int32(0)] + [jnp.asarray(start, jnp.int32) for start in starts]
    starts += [jnp.int32(0)] * len(tail)
    taken = lax.dynamic_slice(view, starts, ahead + tuple(lengths) + tail)
    return taken.reshape(ahead + (-1,) + tail)


def scatter_sum(parts, bit_order, position, count, kind, before=()):
    before = dict(before)
    all_bits = list(reversed(range(count.bit_length() - 1)))
    held = [(parts, all_bits)]
    fixed = {}

    def totals(chosen):
        summed = [None] * len(parts)
        for arrays, bits in held:
            wanted = {bit: value for bit, value in chosen.items() if bit in bits}
            for slot, array in enumerate(arrays):
                piece = pick(array, bits, wanted).astype(jnp.float32)
                summed[slot] = piece if summed[slot] is None else summed[slot] + piece
        return summed

    for bit in bit_order:
        mine = bit_of(position, bit)
        pieces = [piece.astype(kind) for piece in totals({**fixed, bit: 1 - mine})]
        if bit in before:
            pieces = before[bit](pieces)
        shapes = [piece.shape for piece in pieces]
        if len(pieces) == 1:
            received = [swap(pieces[0], 1 << bit, count)]
        else:
            width = pieces[0].shape[-1]
            flat = [piece.reshape(-1, width) for piece in pieces]
            moved = swap(jnp.concatenate(flat), 1 << bit, count)
            received, running = [], 0
            for piece, shape in zip(flat, shapes):
                received.append(moved[running : running + piece.shape[0]].reshape(shape))
                running += piece.shape[0]
        fixed[bit] = mine
        held.append((received, [other for other in all_bits if other not in fixed]))
    return [piece[:, 0] for piece in totals(fixed)]


def meet(*values):
    return lax.optimization_barrier(values)


class Gather:
    def __init__(self, pack, wide, count):
        self.pack, self.wide, self.count = pack, wide, count

    def move(self, array, mask):
        return swap(array, mask, self.count)

    def merged(self, packs):
        width = self.pack.shape[-1]
        long = [pack[self.wide :].reshape(1, -1, width) for pack in packs]
        if not self.wide:
            return jnp.concatenate(long)
        short = jnp.stack([pack[: self.wide] for pack in packs], axis=1)
        return jnp.concatenate([short.reshape(self.wide, -1, width)] + long)

    def along_z(self):
        own = self.pack
        self.quad = self.merged([own] + [self.move(own, mask) for mask in (8, 16, 24)])
        self.half = self.quad.shape[0] // 2

    def along_xy(self):
        self.by_y = self.move(self.quad, 4)
        self.by_x = self.move(self.quad, 2)

    def across(self):
        self.far = [
            self.move(self.by_y[: self.half], 2),
            self.move(self.by_x[self.half :], 4),
        ]

    def finish(self):
        own = [self.quad, self.by_x, self.by_y, *self.far]
        self.groups = own + [self.move(group, 1) for group in own]


class PlainGather(Gather):
    def along_z(self):
        pass

    along_xy = across = along_z

    def finish(self):
        full = lax.all_gather(self.pack, "fsdp")
        _, _, rows, width = full.shape
        long = full[:, self.wide :].reshape(4, 8, -1, width)
        blocks = long
        if self.wide:
            short = jnp.swapaxes(full[:, : self.wide], 0, 1).reshape(self.wide, 8, -1, width)
            blocks = jnp.concatenate([short, long])
        self.half = blocks.shape[0] // 2
        self.groups = []
        for core in range(2):
            group = [blocks[:, 4 * core + place] for place in range(4)]
            self.groups += group[:3] + [group[3][: self.half], group[3][self.half :]]


def across_kernel(counts, rows, half, *refs):
    arrays, (far_y, far_x, own, other, semaphores) = refs[:-5], refs[-5:]
    copies = load_sums(arrays, counts, 3 * rows, rows, own, other, semaphores)
    start_all(copies)
    wait_all(copies)
    for block in range(sum(map(sum, counts))):
        total = bf16(own[block].astype(FULL) + other[block].astype(FULL))
        if block < half:
            far_y[block] = total
        else:
            far_x[block - half] = total


def load_sums(arrays, counts, first, rows, own, other, semaphores):
    copies, running, index = [], 0, 0

    def load(target, start, size):
        source = arrays[index].at[:, pl.ds(first, rows)]
        copies.append(fetch(source, target.at[pl.ds(start, size)], semaphores.at[index]))

    for sizes in counts:
        load(own, running, sum(sizes))
        index += 1
        for size in sizes:
            load(other, running, size)
            index += 1
            running += size
    return copies


def along_xy_kernel(counts, rows, half, far_y, far_x, *refs):
    arrays, (to_x, to_y, own, other, semaphores) = refs[:-5], refs[-5:]
    copies = load_sums(arrays, counts, rows, 2 * rows, own, other, semaphores)
    start_all(copies)
    wait_all(copies)
    for block in range(sum(map(sum, counts))):
        total = own[block, :rows].astype(FULL) + other[block, :rows].astype(FULL)
        if block < half:
            total = total + far_y[block].astype(FULL)
        to_x[block] = bf16(total)
        total = own[block, rows:].astype(FULL) + other[block, rows:].astype(FULL)
        if block >= half:
            total = total + far_x[block - half].astype(FULL)
        to_y[block] = bf16(total)


def along_z_kernel(counts, rows, kinds, by_x, by_y, *refs):
    arrays, outs, (own, other, semaphores) = refs[:-7], refs[-7:-3], refs[-3:]
    copies = load_sums(arrays, counts, 0, rows, own, other, semaphores)
    start_all(copies)
    wait_all(copies)
    made = 0
    for block, (kind, depth) in enumerate(kinds):
        total = own[block].astype(FULL) + other[block].astype(FULL)
        total = total + by_x[block].astype(FULL) + by_y[block].astype(FULL)
        if kind == "long":
            step = outs[0].shape[1]
            for index in range(rows // step):
                part = total[index * step : (index + 1) * step]
                outs[depth][made + index] = part.astype(outs[depth].dtype)
            made += rows // step if depth == 3 else 0
        else:
            step = rows // 4
            for deep in range(4):
                part = total[deep * step : (deep + 1) * step]
                outs[deep][made] = part.astype(outs[deep].dtype)
            made += 1


class Scatter:
    def __init__(self, parts, count):
        self.parts, self.count = parts, count
        self.sizes = [[piece.shape[0] for piece in theirs] for _, theirs, _, _ in parts]
        self.blocks = sum(map(sum, self.sizes))
        self.half = self.blocks // 2
        self.rows, self.width = parts[0][0].shape[1] // 4, parts[0][0].shape[2]

    def move(self, array, mask):
        return swap(array, mask, self.count)

    def cores(self):
        self.held = []
        for mine, theirs, _, _ in self.parts:
            self.held += [mine] + [self.move(piece, 1) for piece in theirs]

    def call(self, kernel, extra, near, outs, length):
        return pl.pallas_call(
            kernel,
            in_specs=[VMEM_WHOLE] * len(near) + [IN_PLACE] * len(self.held),
            out_specs=[VMEM_WHOLE] * len(outs),
            out_shape=outs,
            scratch_shapes=[
                pltpu.VMEM((self.blocks, length, self.width), LOW),
                pltpu.VMEM((self.blocks, length, self.width), LOW),
                pltpu.SemaphoreType.DMA((len(self.held),)),
            ],
            cost_estimate=cost(4),
            compiler_params=pltpu.CompilerParams(vmem_limit_bytes=48 * 2**20),
        )(*near, *self.held)

    def make_far(self):
        self.to_far = self.call(
            functools.partial(across_kernel, self.sizes, self.rows, self.half),
            (),
            [],
            [
                shaped(LOW, self.half, self.rows, self.width),
                shaped(LOW, self.blocks - self.half, self.rows, self.width),
            ],
            self.rows,
        )

    def across(self):
        self.far = [self.move(self.to_far[0], 4), self.move(self.to_far[1], 2)]

    def make_near(self):
        self.to_near = self.call(
            functools.partial(along_xy_kernel, self.sizes, self.rows, self.half),
            (),
            self.far,
            [shaped(LOW, self.blocks, self.rows, self.width)] * 2,
            2 * self.rows,
        )

    def along_xy(self):
        self.near = [self.move(self.to_near[0], 2), self.move(self.to_near[1], 4)]

    def make_deep(self):
        kinds = []
        for _, _, short, long in self.parts:
            kinds += [("short", 0)] * short + [("long", depth) for depth in range(long)]
        shorts = sum(short for _, _, short, _ in self.parts)
        step, made = (self.rows // 4, self.blocks) if shorts else (self.rows, 1)
        outs = [shaped(FULL, made, step, self.width)]
        outs += [shaped(LOW, made, step, self.width)] * 3
        self.own, *self.to_deep = self.call(
            functools.partial(along_z_kernel, self.sizes, self.rows, kinds),
            (),
            self.near,
            outs,
            self.rows,
        )

    def along_z(self):
        self.deep = [self.move(part, mask) for part, mask in zip(self.to_deep, (8, 16, 24))]

    def result(self):
        total = self.own
        for part in self.deep:
            total = total + part.astype(FULL)
        return total


class PlainScatter(Scatter):
    def cores(self):
        pass

    make_far = across = make_near = along_xy = make_deep = along_z = cores

    def result(self):
        whole = []
        for mine, theirs, short, long in self.parts:
            full = jnp.concatenate([mine, jnp.concatenate(theirs)], axis=1)
            if short:
                whole.append(full[:short].reshape(short, self.count, -1, self.width))
            if long:
                whole.append(full[short:].reshape(1, self.count, -1, self.width))
        position = lax.axis_index("fsdp")
        order = range(self.count.bit_length() - 1)
        sums = scatter_sum(whole, order, position, self.count, LOW)
        rows = min(part.shape[1] for part in sums)
        return jnp.concatenate([part.reshape(-1, rows, self.width) for part in sums])


def order_of(places, position):
    device = jnp.arange(len(places))[:, None]
    return (device == (jnp.array(places)[None, :] ^ position)).astype(LOW)


def ordered(blocks, places, position):
    flat = dot(order_of(places, position), blocks.reshape(len(places), -1))
    return flat.astype(LOW).reshape(blocks.shape)


def gather_all(array, position, count, masks, between=None):
    blocks = array[None]
    places = [0]
    for step, mask in enumerate(masks):
        if step == 2 and between is not None:
            blocks = between(blocks)
        blocks = jnp.concatenate([blocks, swap(blocks, mask, count)], axis=0)
        places = places + [place ^ mask for place in places]
    return ordered(blocks, places, position)


def gather_and_turn(array, parts, position, count, between):
    blocks = array[None]
    places = [0]
    turned = ordered(parts, list(range(count)), position)
    rows = parts.shape[1]
    for bit in reversed(range(count.bit_length() - 1)):
        if bit == 2:
            blocks = between(blocks)
        halves = turned.reshape(-1, 2, 1 << bit, rows, 128)
        kept, sent = halves[:, 0], halves[:, 1]
        sent = jnp.concatenate([blocks.reshape(-1, 128), sent.reshape(-1, 128)])
        received = swap(sent, 1 << bit, count)
        size = blocks.shape[0] * blocks.shape[1]
        blocks = jnp.concatenate([blocks, received[:size].reshape(blocks.shape)])
        places = places + [place ^ (1 << bit) for place in places]
        turned = jnp.stack([kept, received[size:].reshape(kept.shape)], axis=1)
    turned = turned.reshape(parts.shape)
    return ordered(blocks, places, position), ordered(turned, list(range(count)), position)


def gather_and_sum(array, parts, position, count, between):
    blocks = array[None]
    all_bits = list(reversed(range(count.bit_length() - 1)))
    held = [(parts[None], all_bits)]
    fixed = {}

    def total(chosen):
        summed = None
        for part, bits in held:
            wanted = {bit: value for bit, value in chosen.items() if bit in bits}
            piece = pick(part, bits, wanted).astype(FULL)
            summed = piece if summed is None else summed + piece
        return summed

    for bit in range(count.bit_length() - 1):
        mine = bit_of(position, bit)
        piece = total({**fixed, bit: 1 - mine}).astype(LOW)
        sent = jnp.concatenate([blocks.reshape(-1, 128), piece.reshape(-1, 128)])
        if bit == 3:
            sent = between(sent)
        received = swap(sent, 1 << bit, count)
        size = blocks.shape[0] * blocks.shape[1]
        blocks = jnp.concatenate([blocks, received[:size].reshape(blocks.shape)])
        fixed[bit] = mine
        left = [other for other in all_bits if other not in fixed]
        held.append((received[size:].reshape(piece.shape), left))
    return blocks, total(fixed)[0, 0]


def sum_all(array, count):
    mask = 1
    while mask < count:
        array = array + swap(array, mask, count)
        mask *= 2
    return array


def split_high(values):
    return (values // 32).astype(jnp.bfloat16), (values % 32).astype(jnp.bfloat16)


def factored(weight, raw, row_old, col_old, row_square, col_square, row_old_sum, rows_all, clip):
    columns = weight.shape[-1]
    row_new = DECAY_RATE * row_old + (1.0 - DECAY_RATE) * (
        clip * (clip * (row_square / columns)) + FACTOR_EPS
    )
    col_new = DECAY_RATE * col_old + (1.0 - DECAY_RATE) * (
        clip * (clip * (col_square / rows_all)) + FACTOR_EPS
    )
    row_mean = (
        DECAY_RATE * row_old_sum
        + (1.0 - DECAY_RATE) * (clip * (clip * (jnp.sum(col_square) / columns)))
    ) / rows_all + (1.0 - DECAY_RATE) * FACTOR_EPS
    clipped = clip * raw
    estimate = row_new[:, None] * col_new[None, :] / row_mean
    return (weight - LEARN_RATE * clipped * lax.rsqrt(estimate), clipped, row_new, col_new)


def body(
    count,
    latents,
    targets,
    features,
    time_weights,
    timesteps,
    classes,
    block_in,
    block_in_rows,
    block_in_cols,
    block_down,
    block_down_rows,
    block_down_cols,
    stem_main,
    stem_main_rows,
    stem_main_cols,
    stem_proj,
    stem_proj_rows,
    stem_proj_cols,
    head_weight,
    head_rows,
    head_cols,
    biases,
    bias_second,
):
    position = lax.axis_index("fsdp")
    images = count * latents.shape[0]
    width_rows = block_in.shape[1]
    bias_part = biases.shape[0]
    bias_cols = -(-bias_part // width_rows)
    bits = count.bit_length() - 1
    gather = Gather if count == 32 else PlainGather
    scatter = Scatter if count == 32 else PlainScatter
    time_out_part, final_ada_part, table_part, patch_part, proj_one_part, time_in_part = cut_parts(
        stem_main, [D, 2 * D, NCLS, PD, P_SIZE, TF]
    )
    main_width = 3 * D + D + F
    main_blocks = main_width // D
    def blocks_of(part, width):
        return jnp.swapaxes(part.astype(LOW).reshape(part.shape[0], -1, width), 0, 1)

    one_part = jnp.pad(proj_one_part, ((0, 0), (0, 3 * D - P_SIZE)))
    layers = []
    for level in range(L):
        main = [blocks_of(block_in[level, :, :main_width], D)]
        if level == 0:
            main.append(blocks_of(one_part, D))
        down = block_down[level].astype(LOW).reshape(4, width_rows, D)
        wide = sum(part.shape[0] for part in main)
        layers.append(gather(jnp.concatenate(main + [down]), wide, count))
        layers[level].first_one = main_blocks
        layers[level].first_down = wide
    rest = gather(stem_proj.astype(LOW)[None], 0, count)

    time_high, time_low = split_high(timesteps)
    class_high, class_low = split_high(classes)
    small = jnp.concatenate(
        [
            biases.astype(LOW),
            patch_part.astype(LOW).reshape(-1),
            time_high,
            time_low,
            class_high,
            class_low,
        ]
    )
    used = small.shape[0]
    small = jnp.pad(small, (0, -used % 2048))
    head_size = small.shape[0]
    small = jnp.concatenate([small, time_in_part.astype(LOW).reshape(-1)])
    small = jnp.pad(small, (0, -small.shape[0] % 2048)).reshape(-1, 128)
    turned = jnp.swapaxes(time_out_part.astype(LOW).reshape(width_rows, count, width_rows), 0, 1)
    turned = turned.reshape(count, -1)
    turned_used = turned.shape[1]
    turned = jnp.pad(turned, ((0, 0), (0, -turned_used % 2048))).reshape(count, -1, 128)

    def start_gathers(blocks):
        blocks, layers[0].pack = meet(blocks, layers[0].pack)
        layers[0].along_z()
        return blocks

    small_all, time_out_mine = gather_and_turn(small, turned, position, count, start_gathers)
    small_all = small_all.reshape(count, -1)
    orders = Orders(position, count == 32)
    bias_full = small_all[:, :bias_part].reshape(-1).astype(FULL)
    patch_t = small_all[:, bias_part : used - 4].reshape(D, PD)
    marks = small_all[:, used - 4 : used].astype(jnp.int32)
    time_in = small_all[:, head_size : head_size + width_rows * TF].reshape(D, TF)
    time_out_mine = time_out_mine.reshape(count, -1)[:, :turned_used].reshape(D, width_rows)
    times_all = marks[:, 0] * 32 + marks[:, 1]
    classes_all = marks[:, 2] * 32 + marks[:, 3]
    block_bias = bias_full[: L * VB].reshape(L, VB // D, D)
    stem_bias = bias_full[L * VB :]
    bias_tin, bias_tout, bias_final, bias_patch, bias_one, bias_two, bias_three = cut_parts(
        stem_bias, [D, D, 2 * D, D, P_SIZE, P_SIZE, Z]
    )

    def mine(values):
        return lax.dynamic_slice_in_dim(values, position * width_rows, width_rows)

    freq_low = time_freq(times_all).astype(LOW)
    embed_hidden = dot_rows(time_in, freq_low) + bias_tin[:, None]
    embed_act = jax.nn.silu(embed_hidden).astype(LOW)
    one_hot = classes_all[:, None] == jnp.arange(NCLS)[None, :]
    class_embed = dot_rows(table_part.astype(LOW), one_hot.astype(LOW))
    condition = dot_tokens(time_out_mine, embed_act) + mine(bias_tout)[:, None] + class_embed
    cond_low = jax.nn.silu(condition).astype(LOW)

    ada_mine = jnp.concatenate(
        [block_in[level, :, 3 * D + D + F :] for level in range(L)] + [final_ada_part], axis=1
    ).astype(LOW)
    mod_part = dot_tokens(cond_low, ada_mine).reshape(1, images, -1, 128)
    before = {}
    if count == 32:

        def start_near(pieces):
            pieces, layers[0].quad = meet(pieces, layers[0].quad)
            layers[0].along_xy()
            return pieces

        before = {3: start_near}
    (mods,) = scatter_sum([mod_part], range(bits), position, count, FULL, before)
    mods, rest.pack = meet(mods, rest.pack)
    rest.along_z()
    mods = mods.reshape(-1)
    bias_ada = jnp.concatenate(
        [block_bias[level, 8:14].reshape(-1) for level in range(L)] + [bias_final]
    )
    mods = (mods + bias_ada).reshape(-1, D)

    latent_low = latents.reshape(TOK, PD).astype(jnp.bfloat16)
    hidden = (
        lax.dot_general(
            latent_low, patch_t, (((1,), (1,)), ((), ())), preferred_element_type=jnp.float32
        )
        + bias_patch
        + positions()
    )
    layers[0].across()
    if count == 32:
        rest.quad, layers[1].pack = meet(rest.quad, layers[1].pack)
        layers[0].far, rest.quad = meet(layers[0].far, rest.quad)
    rest.along_xy()
    layers[1].along_z()
    layers[0].finish()

    def forward(level, hidden):
        level_mods = mods[6 * level : 6 * level + 6]
        normed, packed, logs, attended, branch, middle = attn_forward(
            hidden, level_mods, block_bias[level], orders, layers[level]
        )
        kept_attn = [hidden, normed, packed, logs, attended, branch]
        if count == 32 and level == 1:
            middle, rest_sum.to_far = meet(middle, rest_sum.to_far)
            rest_sum.across()
        normed, slope, active, branch, hidden = mlp_forward(
            middle, level_mods, block_bias[level], orders, layers[level]
        )
        return hidden, kept_attn, [middle, normed, slope, active, branch]

    kept = [None] * L
    hidden, *kept[0] = forward(0, hidden)
    first_out = hidden
    if count == 32:
        hidden, rest.by_x, rest.by_y = meet(hidden, rest.by_x, rest.by_y)
        rest.across()
        rest.far, layers[1].quad = meet(rest.far, layers[1].quad)
    first_out = hidden
    layers[1].along_xy()
    rest.finish()
    (
        grad_first,
        cosine_part,
        grad_one,
        grad_two,
        grad_three,
        one_mine,
        one_theirs,
        rest_mine,
        *rest_theirs,
    ) = projector(
        first_out,
        features.reshape(TOK, Z),
        bias_one[None],
        bias_two[None],
        bias_three[None],
        orders,
        layers[0],
        rest,
    )
    layers[1].across()
    layers[1].finish()
    rest_sum = scatter([(rest_mine, rest_theirs, 0, 4)], count)
    rest_sum.cores()
    rest_sum.make_far()
    hidden, *kept[1] = forward(1, hidden)
    grad_hidden, grad_final_mods, grad_head, grad_head_bias, head_loss = head(
        hidden,
        mods[6 * L :],
        head_weight[:D].astype(LOW),
        head_weight[D:],
        targets.reshape(TOK, PD),
        time_weights.reshape(1, 1),
    )
    local_loss = head_loss[0, 0] + cosine_part[0, 0]
    grad_head_full = jnp.concatenate([grad_head, grad_head_bias], axis=0)

    bias_grads, mod_grads = [None] * L, [None] * L

    def backward(level, grad_hidden):
        level_mods = mods[6 * level : 6 * level + 6]
        grad_middle, mlp_mods, mlp_bias, mlp_mine, *mlp_theirs = mlp_backward(
            grad_hidden, level_mods, kept[level][1], orders, layers[level]
        )
        grad_hidden, attn_mods, attn_bias, attn_mine, *attn_theirs = attn_backward(
            grad_middle, level_mods, kept[level][0], orders, layers[level]
        )
        mod_grads[level] = jnp.concatenate([attn_mods, mlp_mods])
        bias_grads[level] = jnp.concatenate(
            [attn_bias, mlp_bias[:4], mod_grads[level], mlp_bias[4:]]
        ).reshape(-1)
        parts = [(attn_mine, attn_theirs, 4, 0), (mlp_mine, mlp_theirs, 4, 4)]
        return grad_hidden, parts

    rest_sum.make_near()
    rest_sum.along_xy()
    grad_hidden, parts = backward(1, grad_hidden)
    one_sum = scatter(parts + [(one_mine, [one_theirs], 3, 0)], count)
    one_sum.cores()
    one_sum.make_far()
    grad_hidden = grad_hidden + grad_first
    if count == 32:
        grad_hidden, one_sum.to_far, rest_sum.near = meet(
            grad_hidden, one_sum.to_far, rest_sum.near
        )
    one_sum.across()
    rest_sum.make_deep()
    rest_sum.along_z()
    grad_hidden, parts = backward(0, grad_hidden)
    zero_sum = scatter(parts, count)
    zero_sum.cores()
    zero_sum.make_far()
    one_sum.make_near()
    grad_patch = lax.dot_general(
        grad_hidden.astype(jnp.bfloat16),
        latent_low,
        (((0,), (0,)), ((), ())),
        preferred_element_type=jnp.float32,
    )
    grad_bias_all = jnp.concatenate(
        bias_grads
        + [
            jnp.zeros((2 * D,), jnp.float32),
            grad_final_mods.reshape(-1),
            total_rows(grad_hidden),
            grad_one.reshape(-1),
            grad_two.reshape(-1),
            grad_three.reshape(-1),
        ]
    )
    extra = jnp.concatenate(
        [grad_patch.reshape(count, -1), grad_bias_all.reshape(count, bias_part)], axis=1
    )
    grad_mods = jnp.concatenate(mod_grads + [grad_final_mods]).astype(LOW).reshape(-1, 128)
    mod_rows = grad_mods.shape[0]
    grad_mods = jnp.pad(grad_mods, ((0, -mod_rows % 16), (0, 0)))
    extra = jnp.pad(extra, ((0, 0), (0, -extra.shape[1] % 2048))).reshape(count, -1, 128)
    if count == 32:
        grad_mods, one_sum.to_near = meet(grad_mods, one_sum.to_near)
    one_sum.along_xy()

    def start_far(sent):
        if count == 32:
            sent, one_sum.near, zero_sum.to_far = meet(sent, one_sum.near, zero_sum.to_far)
        zero_sum.across()
        return sent

    grad_mods_all, extra = gather_and_sum(grad_mods, extra, position, count, start_far)
    grad_mods_all = grad_mods_all[:, :mod_rows].reshape(images, -1)
    turned = order_of(list(range(count)), position)
    cond_turned = dot(cond_low, turned).astype(LOW)
    extra = extra.reshape(-1)
    patch_shard = extra[: width_rows * PD].reshape(width_rows, PD)
    bias_shard = extra[width_rows * PD : width_rows * PD + bias_part]

    grad_ada_mine = dot(cond_turned, grad_mods_all)
    grad_cond_mine = jnp.dot(
        dot_rows(ada_mine, grad_mods_all),
        turned.astype(FULL),
        precision=lax.Precision.HIGHEST,
    )
    grad_condition = silu_back(condition, grad_cond_mine)
    grad_table = jnp.dot(
        grad_condition, one_hot.astype(jnp.float32), precision=lax.Precision.HIGHEST
    )
    grad_condition_low = grad_condition.astype(LOW)

    one_sum.make_deep()
    zero_sum.make_near()

    def between(blocks):
        if count == 32:
            blocks, one_sum.to_deep, zero_sum.to_near = meet(
                blocks, one_sum.to_deep, zero_sum.to_near
            )
        one_sum.along_z()
        zero_sum.along_xy()
        return blocks

    masks = [1 << bit for bit in range(3, bits)] + [4, 2, 1]
    grad_condition_low = gather_all(grad_condition_low, position, count, masks, between)
    grad_condition_low = grad_condition_low.reshape(D, images)
    grad_time_out = dot_rows(mine(embed_act), grad_condition_low)
    grad_embed_act = dot(time_out_part.astype(LOW), grad_condition_low)
    grad_embed = silu_back(mine(embed_hidden), grad_embed_act)
    grad_time_in = dot(grad_embed.astype(LOW), freq_low)
    zero_sum.make_deep()
    zero_sum.along_z()
    late_bias = jnp.zeros((2, D), jnp.float32)
    late_bias = lax.dynamic_update_slice(
        late_bias,
        jnp.stack([jnp.sum(grad_embed, axis=1), jnp.sum(grad_condition, axis=1)]),
        (0, position * width_rows),
    )

    def side_by_side(blocks):
        return jnp.swapaxes(blocks, 0, 1).reshape(blocks.shape[1], -1)

    shards = [zero_sum.result(), one_sum.result()]
    ada_zero, ada_one, grad_final_ada = cut_parts(grad_ada_mine, [6 * D, 6 * D, 2 * D])
    raw_in = jnp.stack(
        [
            jnp.concatenate(
                [side_by_side(shards[level][:8]), ada], axis=1
            )
            for level, ada in enumerate([ada_zero, ada_one])
        ]
    )
    raw_down = jnp.stack([shards[0][8:].reshape(-1, D), shards[1][8:12].reshape(-1, D)])
    raw_main = jnp.concatenate(
        [
            grad_time_out,
            grad_final_ada,
            grad_table,
            patch_shard,
            side_by_side(shards[1][12:])[:, :P_SIZE],
            grad_time_in,
        ],
        axis=1,
    )
    raw_proj = rest_sum.result()[0]
    raws = [raw_in[0], raw_in[1], raw_down[0], raw_down[1], raw_main, raw_proj]
    row_olds = [
        block_in_rows[0],
        block_in_rows[1],
        block_down_rows[0],
        block_down_rows[1],
        stem_main_rows,
        stem_proj_rows,
    ]
    squares = [raw * raw for raw in raws]
    row_squares = [jnp.sum(square, axis=1) for square in squares]
    late_list = [jnp.sum(square, axis=0) for square in squares] + [
        jnp.stack([jnp.sum(row_old) for row_old in row_olds]),
        jnp.stack([jnp.sum(bias_shard * bias_shard), local_loss]),
        late_bias.reshape(-1),
        grad_head_full.reshape(-1),
    ]
    late_sizes = [values.shape[0] for values in late_list]
    late_all = jnp.concatenate(late_list)
    late_all = jnp.pad(late_all, (0, -late_all.shape[0] % 1024)).reshape(-1, 128)
    late_all = sum_all(late_all, count).reshape(-1)
    late_sums = []
    running = 0
    for size in late_sizes:
        late_sums.append(late_all[running : running + size])
        running += size
    col_squares = late_sums[:6]
    row_old_sums, bias_loss, late_bias, head_sum = late_sums[6:]
    head_sum = head_sum.reshape(D + 1, PD)
    loss_total = bias_loss[1]
    total_square = bias_loss[0] + jnp.sum(late_bias * late_bias) + jnp.sum(head_sum * head_sum)
    for col_square in col_squares:
        total_square = total_square + jnp.sum(col_square)
    grad_norm = jnp.sqrt(total_square)
    clip = jnp.minimum(1.0, CLIP_LIMIT / grad_norm)

    olds = [block_in[0], block_in[1], block_down[0], block_down[1], stem_main, stem_proj]
    col_olds = [
        block_in_cols[0],
        block_in_cols[1],
        block_down_cols[0],
        block_down_cols[1],
        stem_main_cols,
        stem_proj_cols,
    ]
    results = [
        factored(
            olds[slot],
            raws[slot],
            row_olds[slot],
            col_olds[slot],
            row_squares[slot],
            col_squares[slot],
            row_old_sums[slot],
            count * olds[slot].shape[0],
            clip,
        )
        for slot in range(6)
    ]
    new_in, clip_in, rows_in, cols_in = [
        jnp.stack([results[0][part], results[1][part]]) for part in range(4)
    ]
    new_down, clip_down, rows_down, cols_down = [
        jnp.stack([results[2][part], results[3][part]]) for part in range(4)
    ]
    new_main, clip_main, rows_main, cols_main = results[4]
    new_proj, clip_proj, rows_proj, cols_proj = results[5]
    head_square = head_sum * head_sum
    new_head, head_clip, rows_head, cols_head = factored(
        head_weight,
        head_sum,
        head_rows,
        head_cols,
        jnp.sum(head_square, axis=1),
        jnp.sum(head_square, axis=0),
        jnp.sum(head_rows),
        D + 1,
        clip,
    )
    late_flat = jnp.zeros((count * bias_part,), jnp.float32)
    late_flat = lax.dynamic_update_slice(late_flat, late_bias, (L * VB,))
    bias_raw = bias_shard + lax.dynamic_slice(late_flat, (position * bias_part,), (bias_part,))
    clip_bias = clip * bias_raw
    second_new = DECAY_RATE * bias_second + (1.0 - DECAY_RATE) * (
        clip_bias * clip_bias + FACTOR_EPS
    )
    new_bias = biases - LEARN_RATE * clip_bias * lax.rsqrt(second_new)
    return (
        loss_total,
        grad_norm,
        new_in,
        clip_in,
        rows_in,
        cols_in,
        new_in.astype(jnp.bfloat16),
        new_down,
        clip_down,
        rows_down,
        cols_down,
        new_down.astype(jnp.bfloat16),
        new_main,
        clip_main,
        rows_main,
        cols_main,
        new_main.astype(jnp.bfloat16),
        new_proj,
        clip_proj,
        rows_proj,
        cols_proj,
        new_proj.astype(jnp.bfloat16),
        new_head,
        head_clip,
        rows_head,
        cols_head,
        new_bias,
        clip_bias,
        second_new,
    )


def solution(mesh):
    return jax.shard_map(
        functools.partial(body, mesh.shape["fsdp"]),
        mesh=mesh,
        in_specs=(
            P("fsdp", None, None),
            P("fsdp", None, None),
            P("fsdp", None, None),
            P("fsdp"),
            P("fsdp"),
            P("fsdp"),
            P(None, "fsdp", None),
            P(None, "fsdp"),
            P(),
            P(None, "fsdp", None),
            P(None, "fsdp"),
            P(),
            P("fsdp", None),
            P("fsdp"),
            P(),
            P("fsdp", None),
            P("fsdp"),
            P(),
            P(),
            P(),
            P(),
            P("fsdp"),
            P("fsdp"),
        ),
        out_specs=(
            P(),
            P(),
            P(None, "fsdp", None),
            P(None, "fsdp", None),
            P(None, "fsdp"),
            P(),
            P(None, "fsdp", None),
            P(None, "fsdp", None),
            P(None, "fsdp", None),
            P(None, "fsdp"),
            P(),
            P(None, "fsdp", None),
            P("fsdp", None),
            P("fsdp", None),
            P("fsdp"),
            P(),
            P("fsdp", None),
            P("fsdp", None),
            P("fsdp", None),
            P("fsdp"),
            P(),
            P("fsdp", None),
            P(),
            P(),
            P(),
            P(),
            P("fsdp"),
            P("fsdp"),
            P("fsdp"),
        ),
        check_vma=False,
    )
```

```python
import functools
import math

import jax
import jax.numpy as jnp
from jax import lax
from jax.experimental import pallas as pl
from jax.experimental.pallas import tpu as pltpu
from jax.sharding import PartitionSpec as P

D = 768
HD = 64
F = 3072
P_SIZE = 2048
Z = 768
NCLS = 1001
PD = 16
TF = 256
L = 2
GRID = 16
TOK = 256
VB = 11520


NORM_EPS = 1e-06
SCORE_SCALE = 0.125
LEARN_RATE = 0.03
DECAY_RATE = 0.5
CLIP_LIMIT = 0.05
FACTOR_EPS = 1e-30


def cut_parts(array, part_widths):
    borders = []
    running = 0
    for part_width in part_widths[:-1]:
        running += part_width
        borders.append(running)
    return jnp.split(array, borders, axis=-1)


def positions():
    quarter = D // 4
    omega_rate = jnp.exp(-math.log(10000.0) * jnp.arange(quarter, dtype=jnp.float32) / quarter)
    token_place = jnp.arange(TOK)
    column = (token_place % GRID).astype(jnp.float32)
    row_place = (token_place // GRID).astype(jnp.float32)

    def encode(coords):
        angles = coords[:, None] * omega_rate[None, :]
        return jnp.concatenate([jnp.sin(angles), jnp.cos(angles)], axis=1)

    return jnp.concatenate([encode(column), encode(row_place)], axis=1)


def time_freq(timesteps):
    half_width = TF // 2
    freq_rate = jnp.exp(-math.log(10000.0) * jnp.arange(half_width, dtype=jnp.float32) / half_width)
    angles = timesteps.astype(jnp.float32)[:, None] * freq_rate[None, :]
    return jnp.concatenate([jnp.cos(angles), jnp.sin(angles)], axis=1)


def silu_back(before, grad_after):
    return jax.vjp(jax.nn.silu, before)[1](grad_after)[0]


def total_rows(values):
    return jnp.sum(values.reshape(-1, values.shape[-1]), axis=0)


def linear(left_side, weight_side):
    return jnp.dot(left_side, weight_side, preferred_element_type=jnp.float32)


LOW = jnp.bfloat16
FULL = jnp.float32


def dot(left, right):
    return jnp.dot(left, right, preferred_element_type=jnp.float32)


def dot_rows(left, right):
    return lax.dot_general(
        left, right, (((1,), (1,)), ((), ())), preferred_element_type=jnp.float32
    )


def dot_tokens(left, right):
    return lax.dot_general(
        left, right, (((0,), (0,)), ((), ())), preferred_element_type=jnp.float32
    )


def bf16(values):
    return values.astype(jnp.bfloat16)


def moved(values, order):
    return bf16(dot(values, order))


def moved_back(values, order):
    return bf16(dot_rows(values, order))


def moved_back_wide(values, order):
    high = bf16(values)
    return dot_rows(high, order) + dot_rows(bf16(values - high.astype(FULL)), order)


def row_sum(values):
    return jnp.sum(values, axis=0, keepdims=True)


def norm_parts(values):
    centred = values - jnp.mean(values, axis=-1, keepdims=True)
    scale = lax.rsqrt(jnp.mean(centred * centred, axis=-1, keepdims=True) + NORM_EPS)
    return centred * scale, scale


def norm_back(unit, scale, grad_unit):
    mean_grad = jnp.mean(grad_unit, axis=-1, keepdims=True)
    mean_both = jnp.mean(grad_unit * unit, axis=-1, keepdims=True)
    return scale * (grad_unit - mean_grad - unit * mean_both)


GELU_ROOT = math.sqrt(2.0 / math.pi)
GELU_CUBE = 0.044715


def gelu_parts(values):
    square = values * values
    bent = jnp.tanh(GELU_ROOT * values * (1.0 + GELU_CUBE * square))
    half = 0.5 * (1.0 + bent)
    slope = half + 0.5 * values * (1.0 - bent * bent) * GELU_ROOT * (
        1.0 + 3.0 * GELU_CUBE * square
    )
    return values * half, slope


def silu_parts(values):
    gate = jax.nn.sigmoid(values)
    return values * gate, gate * (1.0 + values * (1.0 - gate))


def half_lanes(shape, which):
    lane = lax.broadcasted_iota(jnp.int32, shape, 1)
    return (lane < HD) if which == 0 else (lane >= HD)


def fetch(source, target, semaphore):
    return pltpu.make_async_copy(source, target, semaphore)


def group_of(groups, place, block, half):
    base = 5 * (place // 4)
    if place % 4 < 3:
        return groups[base + place % 4].at[block]
    if block < half:
        return groups[base + 3].at[block]
    return groups[base + 4].at[block - half]


def load_blocks(groups, half, first, size, held, semaphores, rows):
    copies = []
    for block in range(size):
        copies.append(
            [
                fetch(
                    group_of(groups, place, first + block, half),
                    held.at[block, pl.ds(place * rows, rows)],
                    semaphores.at[block, place],
                )
                for place in range(8)
            ]
        )
    return copies


def start_all(copies):
    for copy in copies:
        copy.start()


def wait_all(copies):
    for copy in copies:
        copy.wait()


def depth_of(relative, index):
    if not relative:
        return index
    return index ^ (lax.axis_index("fsdp") // 8)


def attn_forward_kernel(
    half,
    hidden,
    mods,
    bias,
    order,
    *refs,
):
    groups = refs[:10]
    normed_out, packed_out, log_out, attended_out, branch_out, middle_out = refs[10:16]
    held, attended, semaphores = refs[16:]
    copies = load_blocks(groups, half, 0, 4, held, semaphores, 96)
    for block in range(4):
        start_all(copies[block])
    unit, _ = norm_parts(hidden[...])
    normed_out[...] = moved(bf16(unit * (1.0 + mods[1:2]) + mods[0:1]), order[...])
    for block in range(3):
        wait_all(copies[block])
        packed_out[block] = bf16(dot(normed_out[...], held[block]) + bias[block : block + 1])
    lanes = lax.broadcasted_iota(jnp.int32, (TOK, 128), 1)

    def pair(index, logs):
        columns = pl.ds(pl.multiple_of(index * 128, 128), 128)
        queries, keys, values = (packed_out[part, :, columns] for part in range(3))
        halves = []
        for which in range(2):
            mask = half_lanes((TOK, 128), which)
            scores = dot_rows(jnp.where(mask, queries, 0), keys) * SCORE_SCALE
            top = jnp.max(scores, axis=-1, keepdims=True)
            raised = jnp.exp(scores - top)
            total = jnp.sum(raised, axis=-1, keepdims=True)
            halves.append(dot(bf16(raised * (1.0 / total)), values))
            logs = jnp.where(lanes == 2 * index + which, top + jnp.log(total), logs)
        attended[:, columns] = bf16(jnp.where(half_lanes((TOK, 128), 0), *halves))
        return logs

    log_out[...] = lax.fori_loop(0, D // 128, pair, jnp.zeros((TOK, 128), jnp.float32))
    attended_out[...] = moved(attended[...], order[...])
    wait_all(copies[3])
    branch = dot(attended_out[...], held[3]) + bias[3:4]
    branch_out[...] = branch
    middle_out[...] = hidden[...] + mods[2:3] * branch


def mlp_forward_kernel(half, first_down, relative, middle, mods, bias, order, down_order, *refs):
    groups = refs[:10]
    normed_out, slope_out, active_out, branch_out, hidden_out = refs[10:15]
    held_up, held_down, total, before, semaphores_up, semaphores_down = refs[15:]
    ups = load_blocks(groups, half, 4, 4, held_up, semaphores_up, 96)
    downs = load_blocks(groups, half, first_down, 4, held_down, semaphores_down, 96)
    for block in range(4):
        start_all(ups[block])
    for block in range(4):
        start_all(downs[block])
    unit, _ = norm_parts(middle[...])
    normed_out[...] = moved(bf16(unit * (1.0 + mods[4:5]) + mods[3:4]), order[...])
    for block in range(4):
        wait_all(ups[block])
        before[block] = dot(normed_out[...], held_up[block]) + bias[block + 4 : block + 5]
    for depth in range(4):
        active, slope = gelu_parts(before[depth_of(relative, depth)])
        active_out[depth] = moved(bf16(active), down_order[...])
        slope_out[depth] = moved(bf16(slope), down_order[...])
        wait_all(downs[depth])
        part = dot(active_out[depth], held_down[depth])
        total[...] = part if depth == 0 else total[...] + part
    branch = total[...] + bias[14:15]
    branch_out[...] = branch
    hidden_out[...] = middle[...] + mods[5:6] * branch


def mlp_backward_kernel(
    half,
    first_down,
    relative,
    grad_out,
    mods,
    middle,
    normed,
    slope,
    active,
    branch,
    order,
    down_order,
    *refs,
):
    groups = refs[:10]
    grad_middle_out, grad_mods_out, grad_bias_out, mine_out = refs[10:14]
    theirs_out = refs[14:18]
    held_up, held_down, made, low, grad_normed, semaphores_up, semaphores_down, sent = refs[18:]
    ups = load_blocks(groups, half, 4, 4, held_up, semaphores_up, 96)
    downs = load_blocks(groups, half, first_down, 4, held_down, semaphores_down, 96)
    for block in range(4):
        start_all(downs[block])
    for block in range(4):
        start_all(ups[block])
    grad_hidden = grad_out[...]
    grad_branch = grad_hidden * mods[5:6]
    grad_mods_out[2:3] = row_sum(grad_hidden * branch[...])
    grad_bias_out[4:5] = row_sum(grad_branch)
    grad_low = bf16(grad_branch)
    given = []
    for depth in range(4):
        wait_all(downs[depth])
        grad_active = dot_rows(grad_low, held_down[depth])
        made[4 + depth] = bf16(dot_tokens(active[depth], grad_low))
        given += give(made, 4 + depth, mine_out, theirs_out, sent)
        before_low = moved_back(
            bf16(grad_active * slope[depth].astype(FULL)), down_order[...]
        )
        low[depth_of(relative, depth)] = before_low
    for block in range(4):
        before_low = low[block]
        grad_bias_out[block : block + 1] = row_sum(before_low.astype(FULL))
        made[block] = bf16(dot_tokens(normed[...], before_low))
        given += give(made, block, mine_out, theirs_out, sent)
        wait_all(ups[block])
        part = dot_rows(before_low, held_up[block])
        grad_normed[...] = part if block == 0 else grad_normed[...] + part
    unit, scale = norm_parts(middle[...])
    grad_unit = moved_back_wide(grad_normed[...], order[...])
    grad_mods_out[0:1] = row_sum(grad_unit)
    grad_mods_out[1:2] = row_sum(grad_unit * unit)
    grad_middle_out[...] = grad_hidden + norm_back(unit, scale, grad_unit * (1.0 + mods[4:5]))
    wait_all(given)


def give(made, block, mine_out, theirs_outs, sent):
    length = made.shape[1] // 2
    step = theirs_outs[0].shape[0]
    theirs_out = theirs_outs[block // step].at[block % step]
    copies = [
        fetch(made.at[block, pl.ds(0, length)], mine_out.at[block], sent.at[0, block]),
        fetch(made.at[block, pl.ds(length, length)], theirs_out, sent.at[1, block]),
    ]
    start_all(copies)
    return copies


def attn_backward_kernel(
    half,
    grad_middle,
    mods,
    hidden,
    normed,
    packed,
    logs,
    attended,
    branch,
    order,
    *refs,
):
    groups = refs[:10]
    grad_hidden_out, grad_mods_out, grad_bias_out, mine_out = refs[10:14]
    theirs_out = refs[14:16]
    held, made, grad_packed, grad_attended, grad_normed, semaphores, sent = refs[16:]
    copies = load_blocks(groups, half, 0, 4, held, semaphores, 96)
    for block in (3, 0, 1, 2):
        start_all(copies[block])
    grad_mid = grad_middle[...]
    grad_branch = grad_mid * mods[2:3]
    grad_mods_out[2:3] = row_sum(grad_mid * branch[...])
    grad_bias_out[3:4] = row_sum(grad_branch)
    grad_low = bf16(grad_branch)
    made[3] = bf16(dot_tokens(attended[...], grad_low))
    given = give(made, 3, mine_out, theirs_out, sent)
    wait_all(copies[3])
    grad_attended[...] = moved_back(bf16(dot_rows(grad_low, held[3])), order[...])
    lanes = lax.broadcasted_iota(jnp.int32, (TOK, 128), 1)
    first = half_lanes((TOK, 128), 0)

    def pair(index, carry):
        columns = pl.ds(pl.multiple_of(index * 128, 128), 128)
        queries, keys, values = (packed[part, :, columns] for part in range(3))
        grad_pair = grad_attended[:, columns]
        grads = []
        for which in range(2):
            mask = half_lanes((TOK, 128), which)
            log_total = jnp.sum(
                jnp.where(lanes == 2 * index + which, logs[...], 0.0), axis=-1, keepdims=True
            )
            scores = dot_rows(jnp.where(mask, queries, 0), keys) * SCORE_SCALE
            attention = jnp.exp(scores - log_total)
            grad_attention = dot_rows(jnp.where(mask, grad_pair, 0), values)
            grad_values = dot_tokens(bf16(attention), grad_pair)
            weighted = attention * grad_attention
            grad_scores = weighted - attention * jnp.sum(weighted, axis=-1, keepdims=True)
            score_low = bf16(grad_scores * SCORE_SCALE)
            grads.append((dot(score_low, keys), dot_tokens(score_low, queries), grad_values))
        for part in range(3):
            both = jnp.where(first, grads[0][part], grads[1][part])
            grad_bias_out[part : part + 1, columns] = row_sum(both)
            grad_packed[part, :, columns] = bf16(both)
        return carry

    lax.fori_loop(0, D // 128, pair, 0)
    for block in range(3):
        grad_part = grad_packed[block]
        made[block] = bf16(dot_tokens(normed[...], grad_part))
        given += give(made, block, mine_out, theirs_out, sent)
        wait_all(copies[block])
        part = dot_rows(grad_part, held[block])
        grad_normed[...] = part if block == 0 else grad_normed[...] + part
    unit, scale = norm_parts(hidden[...])
    grad_unit = moved_back_wide(grad_normed[...], order[...])
    grad_mods_out[0:1] = row_sum(grad_unit)
    grad_mods_out[1:2] = row_sum(grad_unit * unit)
    grad_hidden_out[...] = grad_mid + norm_back(unit, scale, grad_unit * (1.0 + mods[1:2]))
    wait_all(given)


ONE_WIDTHS = (D, D, P_SIZE - 2 * D)
REST = P_SIZE + Z
CHUNK = P_SIZE // 4


def projector_kernel(
    half,
    first_one,
    relative,
    first,
    features,
    bias_one,
    bias_two,
    bias_three,
    order,
    chunk_order,
    *refs,
):
    groups, rest_groups = refs[:10], refs[10:20]
    outs = refs[20:32]
    grad_first_out, loss_out, grad_bias_one, grad_bias_two, grad_bias_three = outs[:5]
    one_mine, one_theirs, rest_mine, rest_theirs = outs[5], outs[6:7], outs[7], outs[8:]
    (
        held_one,
        held_rest,
        made_one,
        made_rest,
        slope_one,
        slope_two,
        active_one,
        active_two,
        wide,
        low,
        one_semaphores,
        rest_semaphores,
        one_sent,
        rest_sent,
    ) = refs[32:]
    ones = load_blocks(groups, half, first_one, 3, held_one, one_semaphores, 96)
    rests = load_blocks(rest_groups, 2, 0, 4, held_rest, rest_semaphores, 64)
    for copies in ones + rests:
        start_all(copies)
    chunks = [pl.ds(CHUNK * index, CHUNK) for index in range(4)]

    def source(depth):
        return pl.ds(pl.multiple_of(depth_of(relative, depth) * CHUNK, CHUNK), CHUNK)

    def bend(active, slope):
        for depth in range(4):
            values, slopes = silu_parts(wide[:, source(depth)])
            active[:, chunks[depth]] = moved(bf16(values), chunk_order[...])
            slope[:, chunks[depth]] = moved(bf16(slopes), chunk_order[...])

    first_low = moved(bf16(first[...]), order[...])
    running = 0
    for block, width in enumerate(ONE_WIDTHS):
        columns = slice(running, running + width)
        wait_all(ones[block])
        wide[:, columns] = dot(first_low, held_one[block, :, :width]) + bias_one[:, columns]
        running += width
    bend(active_one, slope_one)
    for copies in rests:
        wait_all(copies)

    def product(left, columns):
        total = dot(left[:, chunks[0]], held_rest[0, :, columns])
        for depth in range(1, 4):
            total = total + dot(left[:, chunks[depth]], held_rest[depth, :, columns])
        return total

    for index in range(4):
        wide[:, chunks[index]] = product(active_one, chunks[index]) + bias_two[:, chunks[index]]
    bend(active_two, slope_two)
    tail = pl.ds(P_SIZE, Z)
    result = product(active_two, tail) + bias_three[...]
    wanted = features[...]
    inner = jnp.sum(result * wanted, axis=-1, keepdims=True)
    own = jnp.sum(result * result, axis=-1, keepdims=True) + NORM_EPS
    length = jnp.sqrt(own) * jnp.sqrt(jnp.sum(wanted * wanted, axis=-1, keepdims=True) + NORM_EPS)
    cosine = inner / length
    loss_out[...] = jnp.broadcast_to(-0.5 / TOK * row_sum(cosine), (8, 128))
    grad_result = (-0.5 / TOK) * (wanted / length - result * (cosine / own))
    grad_bias_three[...] = row_sum(grad_result)
    grad_three = bf16(grad_result)
    for depth in range(4):
        made_rest[depth, :, tail] = bf16(dot_tokens(active_two[:, chunks[depth]], grad_three))

    def bend_back(grad, slope, depth, grad_bias):
        columns = source(depth)
        low[:, columns] = moved_back(
            bf16(grad * slope[:, chunks[depth]].astype(FULL)), chunk_order[...]
        )
        grad_bias[:, columns] = row_sum(low[:, columns].astype(FULL))

    for depth in range(4):
        bend_back(dot_rows(grad_three, held_rest[depth, :, tail]), slope_two, depth, grad_bias_two)
    given = []
    main = pl.ds(0, P_SIZE)
    for depth in range(4):
        made_rest[depth, :, main] = bf16(dot_tokens(active_one[:, chunks[depth]], low[...]))
        given += give(made_rest, depth, rest_mine, rest_theirs, rest_sent)
    for depth in range(4):
        wide[:, chunks[depth]] = dot_rows(low[...], held_rest[depth, :, main])
    for depth in range(4):
        bend_back(wide[:, chunks[depth]], slope_one, depth, grad_bias_one)
    running = 0
    grad_first = None
    for block, width in enumerate(ONE_WIDTHS):
        grad_part = low[:, running : running + width]
        made_one[block, :, :width] = bf16(dot_tokens(first_low, grad_part))
        if width < D:
            made_one[block, :, width:] = jnp.zeros((D, D - width), LOW)
        given += give(made_one, block, one_mine, one_theirs, one_sent)
        part = dot_rows(grad_part, held_one[block, :, :width])
        grad_first = part if grad_first is None else grad_first + part
        running += width
    grad_first_out[...] = moved_back_wide(grad_first, order[...])
    wait_all(given)


def head_kernel(
    hidden,
    mods,
    head,
    head_bias,
    targets,
    time_weight,
    grad_hidden_out,
    grad_mods_out,
    grad_head_out,
    grad_head_bias_out,
    loss_out,
):
    unit, scale = norm_parts(hidden[...])
    final_low = bf16(unit * (1.0 + mods[1:2]) + mods[0:1])
    residual = dot(final_low, head[...]) + head_bias[...] - targets[...]
    weight = time_weight[...]
    square = jnp.sum(row_sum(residual * residual), axis=1, keepdims=True)
    loss_out[...] = jnp.broadcast_to(square * weight / (TOK * PD), (8, 128))
    grad_output = (2.0 / (TOK * PD)) * weight * residual
    grad_head_bias_out[...] = row_sum(grad_output)
    grad_low = bf16(grad_output)
    grad_head_out[...] = dot_tokens(final_low, grad_low)
    grad_unit = dot_rows(grad_low, head[...])
    grad_mods_out[0:1] = row_sum(grad_unit)
    grad_mods_out[1:2] = row_sum(grad_unit * unit)
    grad_hidden_out[...] = norm_back(unit, scale, grad_unit * (1.0 + mods[1:2]))


def full_sum(values):
    return row_sum(jnp.sum(values, axis=1, keepdims=True))


def update_kernel(
    count,
    raw_in,
    raw_down,
    raw_main,
    raw_rest,
    old_in,
    old_down,
    old_main,
    old_rest,
    rows_in,
    rows_down,
    rows_main,
    rows_rest,
    cols_in,
    cols_down,
    cols_main,
    cols_rest,
    squares_in,
    squares_down,
    squares_main,
    squares_rest,
    row_sums,
    late_bias,
    head_sum,
    scales_out,
    new_in,
    clip_in,
    copy_in,
    new_cols_in,
    new_down,
    clip_down,
    copy_down,
    new_cols_down,
    new_main,
    clip_main,
    copy_main,
    new_cols_main,
    new_rest,
    clip_rest,
    copy_rest,
    new_cols_rest,
):
    total = row_sums[0:1, 6:7] + full_sum(late_bias[...] * late_bias[...])
    total = total + full_sum(head_sum[...] * head_sum[...])
    for squares in (squares_in, squares_down, squares_main, squares_rest):
        total = total + full_sum(squares[...])
    norm = jnp.sqrt(total)
    clip = jnp.minimum(1.0, CLIP_LIMIT / norm)
    scales_out[0:1] = jnp.broadcast_to(norm, (1, 128))
    scales_out[1:2] = jnp.broadcast_to(clip, (1, 128))

    def step(place, old, raw, pair, col_old, squares):
        rows, columns = raw.shape
        rows_all = count * rows
        row_new = DECAY_RATE * pair[:, 0:1] + (1.0 - DECAY_RATE) * (
            clip * (clip * (pair[:, 1:2] / columns)) + FACTOR_EPS
        )
        col_new = DECAY_RATE * col_old + (1.0 - DECAY_RATE) * (
            clip * (clip * (squares / rows_all)) + FACTOR_EPS
        )
        row_mean = (
            DECAY_RATE * row_sums[0:1, place : place + 1]
            + (1.0 - DECAY_RATE) * (clip * (clip * (full_sum(squares) / columns)))
        ) / rows_all + (1.0 - DECAY_RATE) * FACTOR_EPS
        clipped = clip * raw
        estimate = row_new * col_new / row_mean
        return old - LEARN_RATE * clipped * lax.rsqrt(estimate), clipped, col_new

    for level in range(L):
        one = slice(level, level + 1)
        for place, old, raw, pair, col_old, squares, new, clipped, copy, cols in (
            (level, old_in, raw_in, rows_in, cols_in, squares_in, new_in, clip_in, copy_in, new_cols_in),
            (
                L + level,
                old_down,
                raw_down,
                rows_down,
                cols_down,
                squares_down,
                new_down,
                clip_down,
                copy_down,
                new_cols_down,
            ),
        ):
            made = step(
                place, old[level], raw[level], pair[level], col_old[one], squares[one]
            )
            new[level], clipped[level], cols[one] = made
            copy[level] = bf16(made[0])
    for place, old, raw, pair, col_old, squares, new, clipped, copy, cols in (
        (
            2 * L,
            old_main,
            raw_main,
            rows_main,
            cols_main,
            squares_main,
            new_main,
            clip_main,
            copy_main,
            new_cols_main,
        ),
        (
            2 * L + 1,
            old_rest,
            raw_rest,
            rows_rest,
            cols_rest,
            squares_rest,
            new_rest,
            clip_rest,
            copy_rest,
            new_cols_rest,
        ),
    ):
        made = step(place, old[...], raw[...], pair[...], col_old[...], squares[...])
        new[...], clipped[...], cols[...] = made
        copy[...] = bf16(made[0])


def cost(microseconds):
    return pl.CostEstimate(flops=microseconds, bytes_accessed=0, transcendentals=0)


VMEM_GRANT = 60 * 2**20
VMEM_WHOLE = pl.BlockSpec(memory_space=pltpu.VMEM)
IN_PLACE = pl.BlockSpec(memory_space=pl.ANY)


def shaped(kind, *shape):
    return jax.ShapeDtypeStruct(shape, kind)


def call(kernel, inputs, far_inputs, outputs, far_outputs, scratch, microseconds, limit):
    return pl.pallas_call(
        kernel,
        in_specs=[VMEM_WHOLE] * len(inputs) + [IN_PLACE] * len(far_inputs),
        out_specs=[VMEM_WHOLE] * len(outputs) + [IN_PLACE] * len(far_outputs),
        out_shape=[*outputs, *far_outputs],
        scratch_shapes=scratch,
        cost_estimate=cost(microseconds),
        compiler_params=pltpu.CompilerParams(vmem_limit_bytes=VMEM_GRANT),
    )(*inputs, *far_inputs)


BLOCK_SEMAPHORES = pltpu.SemaphoreType.DMA((4, 8))


def orders_kernel(narrow_source, down_source, chunk_source, narrow, down, chunk):
    for source, order in [(narrow_source, narrow), (down_source, down), (chunk_source, chunk)]:
        rows = lax.broadcasted_iota(jnp.int32, order.shape, 0)
        order[...] = jnp.where(rows == source[...], 1.0, 0.0).astype(LOW)


class Orders:
    def __init__(self, position, relative):
        self.relative = relative
        near, depth = (position & 7, position >> 3) if relative else (0, 0)

        def places(index):
            if not relative:
                return index
            return near ^ (((index & 3) << 1) | (index >> 2))

        column = jnp.arange(D)
        narrow = column
        if relative:
            group, deep, inner = column // 96, (column // 24) % 4, column % 24
            narrow = ((deep ^ depth) * 8 + places(group)) * 24 + inner
        down = places(column // 96) * 96 + column % 96
        column = jnp.arange(CHUNK)
        chunk = places(column // 64) * 64 + column % 64
        sources = [source[None].astype(jnp.int32) for source in (narrow, down, chunk)]
        self.narrow, self.down, self.chunk = pl.pallas_call(
            orders_kernel,
            in_specs=[VMEM_WHOLE] * 3,
            out_specs=[VMEM_WHOLE] * 3,
            out_shape=[shaped(LOW, D, D), shaped(LOW, D, D), shaped(LOW, CHUNK, CHUNK)],
            cost_estimate=cost(3),
            compiler_params=pltpu.CompilerParams(vmem_limit_bytes=VMEM_GRANT),
        )(*sources)


def attn_forward(hidden, mods, bias, orders, gathered):
    return call(
        functools.partial(attn_forward_kernel, gathered.half),
        [hidden, mods, bias, orders.narrow],
        gathered.groups,
        [
            shaped(LOW, TOK, D),
            shaped(LOW, 3, TOK, D),
            shaped(FULL, TOK, 128),
            shaped(LOW, TOK, D),
            shaped(FULL, TOK, D),
            shaped(FULL, TOK, D),
        ],
        [],
        [pltpu.VMEM((4, D, D), LOW), pltpu.VMEM((TOK, D), LOW), BLOCK_SEMAPHORES],
        11,
        32,
    )


def mlp_forward(middle, mods, bias, orders, gathered):
    return call(
        functools.partial(
            mlp_forward_kernel, gathered.half, gathered.first_down, orders.relative
        ),
        [middle, mods, bias, orders.narrow, orders.down],
        gathered.groups,
        [
            shaped(LOW, TOK, D),
            shaped(LOW, 4, TOK, D),
            shaped(LOW, 4, TOK, D),
            shaped(FULL, TOK, D),
            shaped(FULL, TOK, D),
        ],
        [],
        [
            pltpu.VMEM((4, D, D), LOW),
            pltpu.VMEM((4, D, D), LOW),
            pltpu.VMEM((TOK, D), FULL),
            pltpu.VMEM((4, TOK, D), FULL),
            BLOCK_SEMAPHORES,
            BLOCK_SEMAPHORES,
        ],
        11,
        40,
    )


def mlp_backward(grad_out, mods, kept, orders, gathered):
    return call(
        functools.partial(
            mlp_backward_kernel, gathered.half, gathered.first_down, orders.relative
        ),
        [grad_out, mods, *kept, orders.narrow, orders.down],
        gathered.groups,
        [shaped(FULL, TOK, D), shaped(FULL, 3, D), shaped(FULL, 5, D)],
        [shaped(LOW, 8, D // 2, D)] + [shaped(LOW, 2, D // 2, D)] * 4,
        [
            pltpu.VMEM((4, D, D), LOW),
            pltpu.VMEM((4, D, D), LOW),
            pltpu.VMEM((8, D, D), LOW),
            pltpu.VMEM((4, TOK, D), LOW),
            pltpu.VMEM((TOK, D), FULL),
            BLOCK_SEMAPHORES,
            BLOCK_SEMAPHORES,
            pltpu.SemaphoreType.DMA((2, 8)),
        ],
        16,
        48,
    )


def attn_backward(grad_middle, mods, kept, orders, gathered):
    return call(
        functools.partial(attn_backward_kernel, gathered.half),
        [grad_middle, mods, *kept, orders.narrow],
        gathered.groups,
        [shaped(FULL, TOK, D), shaped(FULL, 3, D), shaped(FULL, 4, D)],
        [shaped(LOW, 4, D // 2, D)] + [shaped(LOW, 2, D // 2, D)] * 2,
        [
            pltpu.VMEM((4, D, D), LOW),
            pltpu.VMEM((4, D, D), LOW),
            pltpu.VMEM((3, TOK, D), LOW),
            pltpu.VMEM((TOK, D), LOW),
            pltpu.VMEM((TOK, D), FULL),
            BLOCK_SEMAPHORES,
            pltpu.SemaphoreType.DMA((2, 4)),
        ],
        13,
        40,
    )


def projector(first, features, bias_one, bias_two, bias_three, orders, gathered, rest_gathered):
    return call(
        functools.partial(
            projector_kernel, gathered.half, gathered.first_one, orders.relative
        ),
        [first, features, bias_one, bias_two, bias_three, orders.narrow, orders.chunk],
        [*gathered.groups, *rest_gathered.groups],
        [
            shaped(FULL, TOK, D),
            shaped(FULL, 8, 128),
            shaped(FULL, 1, P_SIZE),
            shaped(FULL, 1, P_SIZE),
            shaped(FULL, 1, Z),
        ],
        [
            shaped(LOW, 3, D // 2, D),
            shaped(LOW, 3, D // 2, D),
            shaped(LOW, 4, CHUNK // 2, REST),
        ]
        + [shaped(LOW, 1, CHUNK // 2, REST)] * 4,
        [
            pltpu.VMEM((3, D, D), LOW),
            pltpu.VMEM((4, CHUNK, REST), LOW),
            pltpu.VMEM((3, D, D), LOW),
            pltpu.VMEM((4, CHUNK, REST), LOW),
            pltpu.VMEM((TOK, P_SIZE), LOW),
            pltpu.VMEM((TOK, P_SIZE), LOW),
            pltpu.VMEM((TOK, P_SIZE), LOW),
            pltpu.VMEM((TOK, P_SIZE), LOW),
            pltpu.VMEM((TOK, P_SIZE), FULL),
            pltpu.VMEM((TOK, P_SIZE), LOW),
            pltpu.SemaphoreType.DMA((3, 8)),
            BLOCK_SEMAPHORES,
            pltpu.SemaphoreType.DMA((2, 3)),
            pltpu.SemaphoreType.DMA((2, 4)),
        ],
        27,
        56,
    )


def head(hidden, mods, head_low, head_bias, targets, time_weight):
    return call(
        head_kernel,
        [hidden, mods, head_low, head_bias, targets, time_weight],
        [],
        [
            shaped(FULL, TOK, D),
            shaped(FULL, 2, D),
            shaped(FULL, D, PD),
            shaped(FULL, 1, PD),
            shaped(FULL, 8, 128),
        ],
        [],
        [],
        5,
        24,
    )


def swap(array, mask, count):
    return lax.ppermute(array, "fsdp", [(place, place ^ mask) for place in range(count)])


def bit_of(position, bit):
    return (position >> bit) & 1


def pick(array, bits, chosen):
    sizes, starts, lengths = [], [], []
    previous = None
    for bit in bits:
        fixed = bit in chosen
        if fixed != previous:
            sizes.append(1)
            starts.append(0)
            lengths.append(1)
        sizes[-1] *= 2
        if fixed:
            starts[-1] = starts[-1] * 2 + chosen[bit]
        else:
            lengths[-1] *= 2
        previous = fixed
    ahead, tail = array.shape[:1], array.shape[2:]
    view = array.reshape(ahead + tuple(sizes) + tail)
    starts = [jnp.int32(0)] + [jnp.asarray(start, jnp.int32) for start in starts]
    starts += [jnp.int32(0)] * len(tail)
    taken = lax.dynamic_slice(view, starts, ahead + tuple(lengths) + tail)
    return taken.reshape(ahead + (-1,) + tail)


def scatter_sum(parts, bit_order, position, count, kind, before=()):
    before = dict(before)
    all_bits = list(reversed(range(count.bit_length() - 1)))
    held = [(parts, all_bits)]
    fixed = {}

    def totals(chosen):
        summed = [None] * len(parts)
        for arrays, bits in held:
            wanted = {bit: value for bit, value in chosen.items() if bit in bits}
            for slot, array in enumerate(arrays):
                piece = pick(array, bits, wanted).astype(jnp.float32)
                summed[slot] = piece if summed[slot] is None else summed[slot] + piece
        return summed

    for bit in bit_order:
        mine = bit_of(position, bit)
        pieces = [piece.astype(kind) for piece in totals({**fixed, bit: 1 - mine})]
        if bit in before:
            pieces = before[bit](pieces)
        shapes = [piece.shape for piece in pieces]
        if len(pieces) == 1:
            received = [swap(pieces[0], 1 << bit, count)]
        else:
            width = pieces[0].shape[-1]
            flat = [piece.reshape(-1, width) for piece in pieces]
            moved = swap(jnp.concatenate(flat), 1 << bit, count)
            received, running = [], 0
            for piece, shape in zip(flat, shapes):
                received.append(moved[running : running + piece.shape[0]].reshape(shape))
                running += piece.shape[0]
        fixed[bit] = mine
        held.append((received, [other for other in all_bits if other not in fixed]))
    return [piece[:, 0] for piece in totals(fixed)]


def meet(*values):
    return lax.optimization_barrier(values)


class Gather:
    def __init__(self, pack, wide, count):
        self.pack, self.wide, self.count = pack, wide, count

    def move(self, array, mask):
        return swap(array, mask, self.count)

    def merged(self, packs):
        width = self.pack.shape[-1]
        long = [pack[self.wide :].reshape(1, -1, width) for pack in packs]
        if not self.wide:
            return jnp.concatenate(long)
        short = jnp.stack([pack[: self.wide] for pack in packs], axis=1)
        return jnp.concatenate([short.reshape(self.wide, -1, width)] + long)

    def along_z(self):
        self.deep = [self.pack] + [self.move(self.pack, mask) for mask in (8, 16, 24)]

    def along_xy(self):
        self.quad = self.merged(self.deep)
        self.half = self.quad.shape[0] // 2
        self.by_y = self.move(self.quad, 4)
        self.by_x = self.move(self.quad, 2)

    def across(self):
        self.far = [
            self.move(self.by_y[: self.half], 2),
            self.move(self.by_x[self.half :], 4),
        ]

    def finish(self):
        own = [self.quad, self.by_x, self.by_y, *self.far]
        self.groups = own + [self.move(group, 1) for group in own]


class PlainGather(Gather):
    def along_z(self):
        pass

    along_xy = across = along_z

    def finish(self):
        full = lax.all_gather(self.pack, "fsdp")
        _, _, rows, width = full.shape
        long = full[:, self.wide :].reshape(4, 8, -1, width)
        blocks = long
        if self.wide:
            short = jnp.swapaxes(full[:, : self.wide], 0, 1).reshape(self.wide, 8, -1, width)
            blocks = jnp.concatenate([short, long])
        self.half = blocks.shape[0] // 2
        self.groups = []
        for core in range(2):
            group = [blocks[:, 4 * core + place] for place in range(4)]
            self.groups += group[:3] + [group[3][: self.half], group[3][self.half :]]


def across_kernel(counts, rows, half, *refs):
    arrays, (far_y, far_x, own, other, semaphores) = refs[:-5], refs[-5:]
    copies = load_sums(arrays, counts, 3 * rows, rows, own, other, semaphores)
    start_all(copies)
    wait_all(copies)
    for block in range(sum(map(sum, counts))):
        total = bf16(own[block].astype(FULL) + other[block].astype(FULL))
        if block < half:
            far_y[block] = total
        else:
            far_x[block - half] = total


def load_sums(arrays, counts, first, rows, own, other, semaphores):
    copies, running, index = [], 0, 0

    def load(target, start, size):
        source = arrays[index].at[:, pl.ds(first, rows)]
        copies.append(fetch(source, target.at[pl.ds(start, size)], semaphores.at[index]))

    for sizes in counts:
        load(own, running, sum(sizes))
        index += 1
        for size in sizes:
            load(other, running, size)
            index += 1
            running += size
    return copies


def along_xy_kernel(counts, rows, half, far_y, far_x, *refs):
    arrays, (to_x, to_y, own, other, semaphores) = refs[:-5], refs[-5:]
    copies = load_sums(arrays, counts, rows, 2 * rows, own, other, semaphores)
    start_all(copies)
    wait_all(copies)
    for block in range(sum(map(sum, counts))):
        total = own[block, :rows].astype(FULL) + other[block, :rows].astype(FULL)
        if block < half:
            total = total + far_y[block].astype(FULL)
        to_x[block] = bf16(total)
        total = own[block, rows:].astype(FULL) + other[block, rows:].astype(FULL)
        if block >= half:
            total = total + far_x[block - half].astype(FULL)
        to_y[block] = bf16(total)


def along_z_kernel(counts, rows, kinds, by_x, by_y, *refs):
    arrays, outs, (own, other, semaphores) = refs[:-7], refs[-7:-3], refs[-3:]
    copies = load_sums(arrays, counts, 0, rows, own, other, semaphores)
    start_all(copies)
    wait_all(copies)
    made = 0
    for block, (kind, depth) in enumerate(kinds):
        total = own[block].astype(FULL) + other[block].astype(FULL)
        total = total + by_x[block].astype(FULL) + by_y[block].astype(FULL)
        if kind == "long":
            step = outs[0].shape[1]
            for index in range(rows // step):
                part = total[index * step : (index + 1) * step]
                outs[depth][made + index] = part.astype(outs[depth].dtype)
            made += rows // step if depth == 3 else 0
        else:
            step = rows // 4
            for deep in range(4):
                part = total[deep * step : (deep + 1) * step]
                outs[deep][made] = part.astype(outs[deep].dtype)
            made += 1


class Scatter:
    def __init__(self, parts, count):
        self.parts, self.count = parts, count
        self.sizes = [[piece.shape[0] for piece in theirs] for _, theirs, _, _ in parts]
        self.blocks = sum(map(sum, self.sizes))
        self.half = self.blocks // 2
        self.rows, self.width = parts[0][0].shape[1] // 4, parts[0][0].shape[2]

    def move(self, array, mask):
        return swap(array, mask, self.count)

    def cores(self):
        self.held = []
        for mine, theirs, _, _ in self.parts:
            self.held += [mine] + [self.move(piece, 1) for piece in theirs]

    def call(self, kernel, extra, near, outs, length):
        return pl.pallas_call(
            kernel,
            in_specs=[VMEM_WHOLE] * len(near) + [IN_PLACE] * len(self.held),
            out_specs=[VMEM_WHOLE] * len(outs),
            out_shape=outs,
            scratch_shapes=[
                pltpu.VMEM((self.blocks, length, self.width), LOW),
                pltpu.VMEM((self.blocks, length, self.width), LOW),
                pltpu.SemaphoreType.DMA((len(self.held),)),
            ],
            cost_estimate=cost(4),
            compiler_params=pltpu.CompilerParams(vmem_limit_bytes=VMEM_GRANT),
        )(*near, *self.held)

    def make_far(self):
        self.to_far = self.call(
            functools.partial(across_kernel, self.sizes, self.rows, self.half),
            (),
            [],
            [
                shaped(LOW, self.half, self.rows, self.width),
                shaped(LOW, self.blocks - self.half, self.rows, self.width),
            ],
            self.rows,
        )

    def across(self):
        self.far = [self.move(self.to_far[0], 4), self.move(self.to_far[1], 2)]

    def make_near(self):
        self.to_near = self.call(
            functools.partial(along_xy_kernel, self.sizes, self.rows, self.half),
            (),
            self.far,
            [shaped(LOW, self.blocks, self.rows, self.width)] * 2,
            2 * self.rows,
        )

    def along_xy(self):
        self.near = [self.move(self.to_near[0], 2), self.move(self.to_near[1], 4)]

    def make_deep(self):
        kinds = []
        for _, _, short, long in self.parts:
            kinds += [("short", 0)] * short + [("long", depth) for depth in range(long)]
        shorts = sum(short for _, _, short, _ in self.parts)
        step, made = (self.rows // 4, self.blocks) if shorts else (self.rows, 1)
        outs = [shaped(FULL, made, step, self.width)]
        outs += [shaped(LOW, made, step, self.width)] * 3
        self.own, *self.to_deep = self.call(
            functools.partial(along_z_kernel, self.sizes, self.rows, kinds),
            (),
            self.near,
            outs,
            self.rows,
        )

    def along_z(self):
        self.deep = [self.move(part, mask) for part, mask in zip(self.to_deep, (8, 16, 24))]

    def result(self):
        total = self.own
        for part in self.deep:
            total = total + part.astype(FULL)
        return total


class PlainScatter(Scatter):
    def cores(self):
        pass

    make_far = across = make_near = along_xy = make_deep = along_z = cores

    def result(self):
        whole = []
        for mine, theirs, short, long in self.parts:
            full = jnp.concatenate([mine, jnp.concatenate(theirs)], axis=1)
            if short:
                whole.append(full[:short].reshape(short, self.count, -1, self.width))
            if long:
                whole.append(full[short:].reshape(1, self.count, -1, self.width))
        position = lax.axis_index("fsdp")
        order = range(self.count.bit_length() - 1)
        sums = scatter_sum(whole, order, position, self.count, LOW)
        rows = min(part.shape[1] for part in sums)
        return jnp.concatenate([part.reshape(-1, rows, self.width) for part in sums])


def order_of(places, position):
    device = jnp.arange(len(places))[:, None]
    return (device == (jnp.array(places)[None, :] ^ position)).astype(LOW)


def ordered(blocks, places, position):
    flat = dot(order_of(places, position), blocks.reshape(len(places), -1))
    return flat.astype(LOW).reshape(blocks.shape)


def gather_all(array, position, count, masks, between=None):
    blocks = array[None]
    places = [0]
    for step, mask in enumerate(masks):
        if step == 2 and between is not None:
            blocks = between(blocks)
        blocks = jnp.concatenate([blocks, swap(blocks, mask, count)], axis=0)
        places = places + [place ^ mask for place in places]
    return ordered(blocks, places, position)


def gather_and_turn(array, parts, position, count, between):
    blocks = array[None]
    places = [0]
    turned = ordered(parts, list(range(count)), position)
    rows = parts.shape[1]
    for bit in reversed(range(count.bit_length() - 1)):
        if bit == 2 or bit == 0:
            blocks = between[bit](blocks)
        halves = turned.reshape(-1, 2, 1 << bit, rows, 128)
        kept, sent = halves[:, 0], halves[:, 1]
        sent = jnp.concatenate([blocks.reshape(-1, 128), sent.reshape(-1, 128)])
        received = swap(sent, 1 << bit, count)
        size = blocks.shape[0] * blocks.shape[1]
        blocks = jnp.concatenate([blocks, received[:size].reshape(blocks.shape)])
        places = places + [place ^ (1 << bit) for place in places]
        turned = jnp.stack([kept, received[size:].reshape(kept.shape)], axis=1)
    turned = turned.reshape(parts.shape)
    return ordered(blocks, places, position), ordered(turned, list(range(count)), position)


def gather_and_sum(array, parts, position, count, between):
    blocks = array[None]
    all_bits = list(reversed(range(count.bit_length() - 1)))
    held = [(parts[None], all_bits)]
    fixed = {}

    def total(chosen):
        summed = None
        for part, bits in held:
            wanted = {bit: value for bit, value in chosen.items() if bit in bits}
            piece = pick(part, bits, wanted).astype(FULL)
            summed = piece if summed is None else summed + piece
        return summed

    for bit in range(count.bit_length() - 1):
        mine = bit_of(position, bit)
        piece = total({**fixed, bit: 1 - mine}).astype(LOW)
        sent = jnp.concatenate([blocks.reshape(-1, 128), piece.reshape(-1, 128)])
        if bit in between:
            sent = between[bit](sent)
        received = swap(sent, 1 << bit, count)
        size = blocks.shape[0] * blocks.shape[1]
        blocks = jnp.concatenate([blocks, received[:size].reshape(blocks.shape)])
        fixed[bit] = mine
        left = [other for other in all_bits if other not in fixed]
        held.append((received[size:].reshape(piece.shape), left))
    return blocks, total(fixed)[0, 0]


def sum_all(array, count):
    mask = 1
    while mask < count:
        array = array + swap(array, mask, count)
        mask *= 2
    return array


def split_high(values):
    return (values // 32).astype(jnp.bfloat16), (values % 32).astype(jnp.bfloat16)


def factored(weight, raw, row_old, col_old, row_square, col_square, row_old_sum, rows_all, clip):
    columns = weight.shape[-1]
    row_new = DECAY_RATE * row_old + (1.0 - DECAY_RATE) * (
        clip * (clip * (row_square / columns)) + FACTOR_EPS
    )
    col_new = DECAY_RATE * col_old + (1.0 - DECAY_RATE) * (
        clip * (clip * (col_square / rows_all)) + FACTOR_EPS
    )
    row_mean = (
        DECAY_RATE * row_old_sum
        + (1.0 - DECAY_RATE) * (clip * (clip * (jnp.sum(col_square) / columns)))
    ) / rows_all + (1.0 - DECAY_RATE) * FACTOR_EPS
    clipped = clip * raw
    estimate = row_new[:, None] * col_new[None, :] / row_mean
    return (weight - LEARN_RATE * clipped * lax.rsqrt(estimate), clipped, row_new, col_new)


def body(
    count,
    latents,
    targets,
    features,
    time_weights,
    timesteps,
    classes,
    block_in,
    block_in_rows,
    block_in_cols,
    block_down,
    block_down_rows,
    block_down_cols,
    stem_main,
    stem_main_rows,
    stem_main_cols,
    stem_proj,
    stem_proj_rows,
    stem_proj_cols,
    head_weight,
    head_rows,
    head_cols,
    biases,
    bias_second,
):
    position = lax.axis_index("fsdp")
    images = count * latents.shape[0]
    width_rows = block_in.shape[1]
    bias_part = biases.shape[0]
    bias_cols = -(-bias_part // width_rows)
    bits = count.bit_length() - 1
    gather = Gather if count == 32 else PlainGather
    scatter = Scatter if count == 32 else PlainScatter
    time_out_part, final_ada_part, table_part, patch_part, proj_one_part, time_in_part = cut_parts(
        stem_main, [D, 2 * D, NCLS, PD, P_SIZE, TF]
    )
    main_width = 3 * D + D + F
    main_blocks = main_width // D
    def blocks_of(part, width):
        return jnp.swapaxes(part.astype(LOW).reshape(part.shape[0], -1, width), 0, 1)

    one_part = jnp.pad(proj_one_part, ((0, 0), (0, 3 * D - P_SIZE)))
    layers = []
    for level in range(L):
        main = [blocks_of(block_in[level, :, :main_width], D)]
        if level == 0:
            main.append(blocks_of(one_part, D))
        down = block_down[level].astype(LOW).reshape(4, width_rows, D)
        wide = sum(part.shape[0] for part in main)
        layers.append(gather(jnp.concatenate(main + [down]), wide, count))
        layers[level].first_one = main_blocks
        layers[level].first_down = wide
    rest = gather(stem_proj.astype(LOW)[None], 0, count)

    time_high, time_low = split_high(timesteps)
    class_high, class_low = split_high(classes)
    small = jnp.concatenate(
        [
            biases.astype(LOW),
            patch_part.astype(LOW).reshape(-1),
            time_high,
            time_low,
            class_high,
            class_low,
        ]
    )
    used = small.shape[0]
    small = jnp.pad(small, (0, -used % 2048))
    head_size = small.shape[0]
    small = jnp.concatenate([small, time_in_part.astype(LOW).reshape(-1)])
    small = jnp.pad(small, (0, -small.shape[0] % 2048)).reshape(-1, 128)
    turned = jnp.swapaxes(time_out_part.astype(LOW).reshape(width_rows, count, width_rows), 0, 1)
    turned = turned.reshape(count, -1)
    turned_used = turned.shape[1]
    turned = jnp.pad(turned, ((0, 0), (0, -turned_used % 2048))).reshape(count, -1, 128)

    def start_gathers(blocks):
        blocks, layers[0].pack = meet(blocks, layers[0].pack)
        layers[0].along_z()
        return blocks

    def see_one(blocks):
        if count == 32:
            blocks, layers[0].deep[1], layers[0].deep[3] = meet(
                blocks, layers[0].deep[1], layers[0].deep[3]
            )
        return blocks

    small_all, time_out_mine = gather_and_turn(
        small, turned, position, count, {2: start_gathers, 0: see_one}
    )
    small_all = small_all.reshape(count, -1)
    orders = Orders(position, count == 32)
    bias_full = small_all[:, :bias_part].reshape(-1).astype(FULL)
    patch_t = small_all[:, bias_part : used - 4].reshape(D, PD)
    marks = small_all[:, used - 4 : used].astype(jnp.int32)
    time_in = small_all[:, head_size : head_size + width_rows * TF].reshape(D, TF)
    time_out_mine = time_out_mine.reshape(count, -1)[:, :turned_used].reshape(D, width_rows)
    times_all = marks[:, 0] * 32 + marks[:, 1]
    classes_all = marks[:, 2] * 32 + marks[:, 3]
    block_bias = bias_full[: L * VB].reshape(L, VB // D, D)
    stem_bias = bias_full[L * VB :]
    bias_tin, bias_tout, bias_final, bias_patch, bias_one, bias_two, bias_three = cut_parts(
        stem_bias, [D, D, 2 * D, D, P_SIZE, P_SIZE, Z]
    )

    def mine(values):
        return lax.dynamic_slice_in_dim(values, position * width_rows, width_rows)

    latent_low = latents.reshape(TOK, PD).astype(jnp.bfloat16)
    hidden = (
        lax.dot_general(
            latent_low, patch_t, (((1,), (1,)), ((), ())), preferred_element_type=jnp.float32
        )
        + bias_patch
        + positions()
    )
    freq_low = time_freq(times_all).astype(LOW)
    embed_hidden = dot_rows(time_in, freq_low) + bias_tin[:, None]
    embed_act = jax.nn.silu(embed_hidden).astype(LOW)
    one_hot = classes_all[:, None] == jnp.arange(NCLS)[None, :]
    class_embed = dot_rows(table_part.astype(LOW), one_hot.astype(LOW))
    condition = dot_tokens(time_out_mine, embed_act) + mine(bias_tout)[:, None] + class_embed
    cond_low = jax.nn.silu(condition).astype(LOW)

    ada_mine = jnp.concatenate(
        [block_in[level, :, 3 * D + D + F :] for level in range(L)] + [final_ada_part], axis=1
    ).astype(LOW)
    mod_part = dot_tokens(cond_low, ada_mine).reshape(1, images, -1, 128)
    before = {}
    if count == 32:

        def start_near(pieces):
            pieces, layers[0].deep = meet(pieces, layers[0].deep)
            layers[0].along_xy()
            return pieces

        before = {3: start_near}
    (mods,) = scatter_sum([mod_part], range(bits), position, count, FULL, before)
    mods, rest.pack = meet(mods, rest.pack)
    rest.along_z()
    if count == 32:
        mods, layers[0].by_x, layers[0].by_y, rest.deep, hidden, block_bias = meet(
            mods, layers[0].by_x, layers[0].by_y, rest.deep, hidden, block_bias
        )
    mods = mods.reshape(-1)
    bias_ada = jnp.concatenate(
        [block_bias[level, 8:14].reshape(-1) for level in range(L)] + [bias_final]
    )
    mods = (mods + bias_ada).reshape(-1, D)

    layers[0].across()
    if count == 32:
        layers[0].far, rest.deep, layers[1].pack = meet(
            layers[0].far, rest.deep, layers[1].pack
        )
    layers[0].finish()
    rest.along_xy()
    layers[1].along_z()

    def forward(level, hidden):
        level_mods = mods[6 * level : 6 * level + 6]
        normed, packed, logs, attended, branch, middle = attn_forward(
            hidden, level_mods, block_bias[level], orders, layers[level]
        )
        kept_attn = [hidden, normed, packed, logs, attended, branch]
        if count == 32 and level == 0:
            middle, rest.by_x, rest.by_y, layers[1].deep = meet(
                middle, rest.by_x, rest.by_y, layers[1].deep
            )
            rest.across()
        if count == 32 and level == 1:
            middle, rest_sum.to_far = meet(middle, rest_sum.to_far)
            rest_sum.across()
        normed, slope, active, branch, hidden = mlp_forward(
            middle, level_mods, block_bias[level], orders, layers[level]
        )
        return hidden, kept_attn, [middle, normed, slope, active, branch]

    kept = [None] * L
    hidden, *kept[0] = forward(0, hidden)
    first_out = hidden
    if count == 32:
        hidden, rest.far, layers[1].deep = meet(hidden, rest.far, layers[1].deep)
    first_out = hidden
    layers[1].along_xy()
    rest.finish()
    (
        grad_first,
        cosine_part,
        grad_one,
        grad_two,
        grad_three,
        one_mine,
        one_theirs,
        rest_mine,
        *rest_theirs,
    ) = projector(
        first_out,
        features.reshape(TOK, Z),
        bias_one[None],
        bias_two[None],
        bias_three[None],
        orders,
        layers[0],
        rest,
    )
    layers[1].across()
    layers[1].finish()
    rest_sum = scatter([(rest_mine, rest_theirs, 0, 4)], count)
    rest_sum.cores()
    rest_sum.make_far()
    hidden, *kept[1] = forward(1, hidden)
    grad_hidden, grad_final_mods, grad_head, grad_head_bias, head_loss = head(
        hidden,
        mods[6 * L :],
        head_weight[:D].astype(LOW),
        head_weight[D:],
        targets.reshape(TOK, PD),
        time_weights.reshape(1, 1),
    )
    bias_grads, mod_grads = [None] * L, [None] * L

    def backward(level, grad_hidden):
        level_mods = mods[6 * level : 6 * level + 6]
        grad_middle, mlp_mods, mlp_bias, mlp_mine, *mlp_theirs = mlp_backward(
            grad_hidden, level_mods, kept[level][1], orders, layers[level]
        )
        if count == 32 and level == 0:
            one_sum.far, rest_sum.deep = meet(one_sum.far, rest_sum.deep)
            one_sum.make_near()
            grad_middle, one_sum.to_near = meet(grad_middle, one_sum.to_near)
            one_sum.along_xy()
        grad_hidden, attn_mods, attn_bias, attn_mine, *attn_theirs = attn_backward(
            grad_middle, level_mods, kept[level][0], orders, layers[level]
        )
        mod_grads[level] = jnp.concatenate([attn_mods, mlp_mods])
        bias_grads[level] = (attn_bias, mlp_bias)
        if count == 32 and level == 1:
            attn_theirs, rest_sum.near = meet(attn_theirs, rest_sum.near)
        parts = [(attn_mine, attn_theirs, 4, 0), (mlp_mine, mlp_theirs, 4, 4)]
        return grad_hidden, parts

    rest_sum.make_near()
    if count == 32:
        grad_hidden, rest_sum.to_near = meet(grad_hidden, rest_sum.to_near)
    rest_sum.along_xy()
    grad_hidden, parts = backward(1, grad_hidden)
    one_sum = scatter(parts + [(one_mine, [one_theirs], 3, 0)], count)
    one_sum.cores()
    one_sum.make_far()
    grad_hidden = grad_hidden + grad_first
    if count == 32:
        grad_hidden, one_sum.to_far = meet(grad_hidden, one_sum.to_far)
    one_sum.across()
    rest_sum.make_deep()
    rest_sum.along_z()
    grad_hidden, parts = backward(0, grad_hidden)
    zero_sum = scatter(parts, count)
    zero_sum.cores()
    zero_sum.make_far()
    grad_mods = jnp.concatenate(mod_grads + [grad_final_mods]).astype(LOW).reshape(-1, 128)
    mod_rows = grad_mods.shape[0]
    grad_mods = jnp.pad(grad_mods, ((0, -mod_rows % 16), (0, 0)))
    left = (
        (grad_hidden, grad_one, grad_two, grad_three, grad_final_mods, bias_grads, mod_grads),
        (grad_head, grad_head_bias, head_loss, cosine_part),
        (block_in, stem_main, stem_main_rows, stem_proj_rows, block_in_rows, block_down_rows),
    )
    if count == 32:
        grad_mods, one_sum.near, zero_sum.to_far, left = meet(
            grad_mods, one_sum.near, zero_sum.to_far, left
        )
    grad_hidden, grad_one, grad_two, grad_three, grad_final_mods, bias_grads, mod_grads = left[0]
    grad_head, grad_head_bias, head_loss, cosine_part = left[1]
    block_in, stem_main, stem_main_rows, stem_proj_rows, block_in_rows, block_down_rows = left[2]
    zero_sum.across()
    one_sum.make_deep()
    one_sum.along_z()
    time_out_part, final_ada_part = stem_main[:, :D], stem_main[:, D : 3 * D]
    ada_mine = jnp.concatenate(
        [block_in[level, :, main_width:] for level in range(L)] + [final_ada_part], axis=1
    ).astype(LOW)
    local_loss = head_loss[0, 0] + cosine_part[0, 0]
    grad_head_full = jnp.concatenate([grad_head, grad_head_bias], axis=0)
    bias_grads = [
        jnp.concatenate([attn_bias, mlp_bias[:4], grads, mlp_bias[4:]]).reshape(-1)
        for (attn_bias, mlp_bias), grads in zip(bias_grads, mod_grads)
    ]
    grad_patch = lax.dot_general(
        grad_hidden.astype(jnp.bfloat16),
        latent_low,
        (((0,), (0,)), ((), ())),
        preferred_element_type=jnp.float32,
    )
    grad_bias_all = jnp.concatenate(
        bias_grads
        + [
            jnp.zeros((2 * D,), jnp.float32),
            grad_final_mods.reshape(-1),
            total_rows(grad_hidden),
            grad_one.reshape(-1),
            grad_two.reshape(-1),
            grad_three.reshape(-1),
        ]
    )
    extra = jnp.concatenate(
        [grad_patch.reshape(count, -1), grad_bias_all.reshape(count, bias_part)], axis=1
    )
    extra = jnp.pad(extra, ((0, 0), (0, -extra.shape[1] % 2048))).reshape(count, -1, 128)
    def start_near(sent):
        if count == 32:
            sent, zero_sum.far = meet(sent, zero_sum.far)
        zero_sum.make_near()
        zero_sum.along_xy()
        return sent

    def see_deep(sent):
        if count == 32:
            sent, one_sum.deep = meet(sent, one_sum.deep)
        return sent

    grad_mods_all, extra = gather_and_sum(
        grad_mods, extra, position, count, {2: start_near, 3: see_deep}
    )
    grad_mods_all = grad_mods_all[:, :mod_rows].reshape(images, -1)
    turned = order_of(list(range(count)), position)
    cond_turned = dot(cond_low, turned).astype(LOW)
    extra = extra.reshape(-1)
    patch_shard = extra[: width_rows * PD].reshape(width_rows, PD)
    bias_shard = extra[width_rows * PD : width_rows * PD + bias_part]

    grad_ada_mine = dot(cond_turned, grad_mods_all)
    grad_cond_mine = jnp.dot(
        dot_rows(ada_mine, grad_mods_all),
        turned.astype(FULL),
        precision=lax.Precision.HIGHEST,
    )
    grad_condition = silu_back(condition, grad_cond_mine)
    grad_table = jnp.dot(
        grad_condition, one_hot.astype(jnp.float32), precision=lax.Precision.HIGHEST
    )
    grad_condition_low = grad_condition.astype(LOW)

    def between(blocks):
        if count == 32:
            blocks, zero_sum.near = meet(blocks, zero_sum.near)
        zero_sum.make_deep()
        zero_sum.along_z()
        return blocks

    masks = [1 << bit for bit in range(3, bits)] + [4, 2, 1]
    grad_condition_low = gather_all(grad_condition_low, position, count, masks, between)
    grad_condition_low = grad_condition_low.reshape(D, images)
    grad_time_out = dot_rows(mine(embed_act), grad_condition_low)
    grad_embed_act = dot(time_out_part.astype(LOW), grad_condition_low)
    grad_embed = silu_back(mine(embed_hidden), grad_embed_act)
    grad_time_in = dot(grad_embed.astype(LOW), freq_low)
    late_bias = jnp.zeros((2, D), jnp.float32)
    late_bias = lax.dynamic_update_slice(
        late_bias,
        jnp.stack([jnp.sum(grad_embed, axis=1), jnp.sum(grad_condition, axis=1)]),
        (0, position * width_rows),
    )

    def side_by_side(blocks):
        return jnp.swapaxes(blocks, 0, 1).reshape(blocks.shape[1], -1)

    shards = [zero_sum.result(), one_sum.result()]
    ada_zero, ada_one, grad_final_ada = cut_parts(grad_ada_mine, [6 * D, 6 * D, 2 * D])
    raw_in = jnp.stack(
        [
            jnp.concatenate(
                [side_by_side(shards[level][:8]), ada], axis=1
            )
            for level, ada in enumerate([ada_zero, ada_one])
        ]
    )
    raw_down = jnp.stack([shards[0][8:].reshape(-1, D), shards[1][8:12].reshape(-1, D)])
    raw_main = jnp.concatenate(
        [
            grad_time_out,
            grad_final_ada,
            grad_table,
            patch_shard,
            side_by_side(shards[1][12:])[:, :P_SIZE],
            grad_time_in,
        ],
        axis=1,
    )
    raw_proj = rest_sum.result()[0]
    raws = [raw_in[0], raw_in[1], raw_down[0], raw_down[1], raw_main, raw_proj]
    row_olds = [
        block_in_rows[0],
        block_in_rows[1],
        block_down_rows[0],
        block_down_rows[1],
        stem_main_rows,
        stem_proj_rows,
    ]
    squares = [raw * raw for raw in raws]
    row_squares = [jnp.sum(square, axis=1) for square in squares]
    late_list = [jnp.sum(square, axis=0) for square in squares] + [
        jnp.stack([jnp.sum(row_old) for row_old in row_olds]),
        jnp.stack([jnp.sum(bias_shard * bias_shard), local_loss]),
        late_bias.reshape(-1),
        grad_head_full.reshape(-1),
    ]
    late_sizes = [values.shape[0] for values in late_list]
    late_all = jnp.concatenate(late_list)
    late_all = jnp.pad(late_all, (0, -late_all.shape[0] % 1024)).reshape(-1, 128)
    late_all = sum_all(late_all, count).reshape(-1)
    late_sums = []
    running = 0
    for size in late_sizes:
        late_sums.append(late_all[running : running + size])
        running += size
    col_squares = late_sums[:6]
    row_old_sums, bias_loss, late_bias, head_sum = late_sums[6:]
    head_sum = head_sum.reshape(D + 1, PD)
    loss_total = bias_loss[1]
    row_sums = jnp.pad(jnp.concatenate([row_old_sums, bias_loss])[None], ((0, 0), (0, 120)))
    pairs = [
        jnp.stack([row_old, square], axis=-1) for row_old, square in zip(row_olds, row_squares)
    ]
    olds = [block_in, block_down, stem_main, stem_proj]
    raw_list = [raw_in, raw_down, raw_main, raw_proj]
    outputs = [shaped(FULL, 8, 128)]
    col_old_list = [block_in_cols, block_down_cols, stem_main_cols[None], stem_proj_cols[None]]
    for old, col_old in zip(olds, col_old_list):
        outputs += [shaped(FULL, *old.shape), shaped(FULL, *old.shape), shaped(LOW, *old.shape)]
        outputs.append(shaped(FULL, *col_old.shape))
    made = call(
        functools.partial(update_kernel, count),
        [
            *raw_list,
            *olds,
            jnp.stack(pairs[0:2]),
            jnp.stack(pairs[2:4]),
            pairs[4],
            pairs[5],
            *col_old_list,
            jnp.stack(col_squares[0:2]),
            jnp.stack(col_squares[2:4]),
            col_squares[4][None],
            col_squares[5][None],
            row_sums,
            late_bias.reshape(2, D),
            head_sum,
        ],
        [],
        outputs,
        [],
        [],
        12,
        0,
    )
    grad_norm, clip = made[0][0, 0], made[0][1, 0]
    (
        (new_in, clip_in, copy_in, cols_in),
        (new_down, clip_down, copy_down, cols_down),
        (new_main, clip_main, copy_main, cols_main),
        (new_proj, clip_proj, copy_proj, cols_proj),
    ) = (made[1 + 4 * slot : 5 + 4 * slot] for slot in range(4))

    def new_rows(row_old, row_square, columns):
        return DECAY_RATE * row_old + (1.0 - DECAY_RATE) * (
            clip * (clip * (row_square / columns)) + FACTOR_EPS
        )

    rows_in = new_rows(block_in_rows, jnp.stack(row_squares[0:2]), block_in.shape[-1])
    rows_down = new_rows(block_down_rows, jnp.stack(row_squares[2:4]), D)
    rows_main = new_rows(stem_main_rows, row_squares[4], stem_main.shape[-1])
    rows_proj = new_rows(stem_proj_rows, row_squares[5], stem_proj.shape[-1])
    head_square = head_sum * head_sum
    new_head, head_clip, rows_head, cols_head = factored(
        head_weight,
        head_sum,
        head_rows,
        head_cols,
        jnp.sum(head_square, axis=1),
        jnp.sum(head_square, axis=0),
        jnp.sum(head_rows),
        D + 1,
        clip,
    )
    late_flat = jnp.zeros((count * bias_part,), jnp.float32)
    late_flat = lax.dynamic_update_slice(late_flat, late_bias, (L * VB,))
    bias_raw = bias_shard + lax.dynamic_slice(late_flat, (position * bias_part,), (bias_part,))
    clip_bias = clip * bias_raw
    second_new = DECAY_RATE * bias_second + (1.0 - DECAY_RATE) * (
        clip_bias * clip_bias + FACTOR_EPS
    )
    new_bias = biases - LEARN_RATE * clip_bias * lax.rsqrt(second_new)
    return (
        loss_total,
        grad_norm,
        new_in,
        clip_in,
        rows_in,
        cols_in,
        copy_in,
        new_down,
        clip_down,
        rows_down,
        cols_down,
        copy_down,
        new_main,
        clip_main,
        rows_main,
        cols_main[0],
        copy_main,
        new_proj,
        clip_proj,
        rows_proj,
        cols_proj[0],
        copy_proj,
        new_head,
        head_clip,
        rows_head,
        cols_head,
        new_bias,
        clip_bias,
        second_new,
    )


def solution(mesh):
    return jax.shard_map(
        functools.partial(body, mesh.shape["fsdp"]),
        mesh=mesh,
        in_specs=(
            P("fsdp", None, None),
            P("fsdp", None, None),
            P("fsdp", None, None),
            P("fsdp"),
            P("fsdp"),
            P("fsdp"),
            P(None, "fsdp", None),
            P(None, "fsdp"),
            P(),
            P(None, "fsdp", None),
            P(None, "fsdp"),
            P(),
            P("fsdp", None),
            P("fsdp"),
            P(),
            P("fsdp", None),
            P("fsdp"),
            P(),
            P(),
            P(),
            P(),
            P("fsdp"),
            P("fsdp"),
        ),
        out_specs=(
            P(),
            P(),
            P(None, "fsdp", None),
            P(None, "fsdp", None),
            P(None, "fsdp"),
            P(),
            P(None, "fsdp", None),
            P(None, "fsdp", None),
            P(None, "fsdp", None),
            P(None, "fsdp"),
            P(),
            P(None, "fsdp", None),
            P("fsdp", None),
            P("fsdp", None),
            P("fsdp"),
            P(),
            P("fsdp", None),
            P("fsdp", None),
            P("fsdp", None),
            P("fsdp"),
            P(),
            P("fsdp", None),
            P(),
            P(),
            P(),
            P(),
            P("fsdp"),
            P("fsdp"),
            P("fsdp"),
        ),
        check_vma=False,
    )
```

```python
import functools
import math

import jax
import jax.numpy as jnp
from jax import lax
from jax.experimental import pallas as pl
from jax.experimental.pallas import tpu as pltpu
from jax.sharding import PartitionSpec as P

D = 768
HD = 64
F = 3072
P_SIZE = 2048
Z = 768
NCLS = 1001
PD = 16
TF = 256
L = 2
GRID = 16
TOK = 256
VB = 11520


NORM_EPS = 1e-06
SCORE_SCALE = 0.125
LEARN_RATE = 0.03
DECAY_RATE = 0.5
CLIP_LIMIT = 0.05
FACTOR_EPS = 1e-30


def cut_parts(array, part_widths):
    borders = []
    running = 0
    for part_width in part_widths[:-1]:
        running += part_width
        borders.append(running)
    return jnp.split(array, borders, axis=-1)


def positions():
    quarter = D // 4
    omega_rate = jnp.exp(-math.log(10000.0) * jnp.arange(quarter, dtype=jnp.float32) / quarter)
    token_place = jnp.arange(TOK)
    column = (token_place % GRID).astype(jnp.float32)
    row_place = (token_place // GRID).astype(jnp.float32)

    def encode(coords):
        angles = coords[:, None] * omega_rate[None, :]
        return jnp.concatenate([jnp.sin(angles), jnp.cos(angles)], axis=1)

    return jnp.concatenate([encode(column), encode(row_place)], axis=1)


def time_freq(timesteps):
    half_width = TF // 2
    freq_rate = jnp.exp(-math.log(10000.0) * jnp.arange(half_width, dtype=jnp.float32) / half_width)
    angles = timesteps.astype(jnp.float32)[:, None] * freq_rate[None, :]
    return jnp.concatenate([jnp.cos(angles), jnp.sin(angles)], axis=1)


def silu_back(before, grad_after):
    return jax.vjp(jax.nn.silu, before)[1](grad_after)[0]


def total_rows(values):
    return jnp.sum(values.reshape(-1, values.shape[-1]), axis=0)


def linear(left_side, weight_side):
    return jnp.dot(left_side, weight_side, preferred_element_type=jnp.float32)


LOW = jnp.bfloat16
FULL = jnp.float32


def dot(left, right):
    return jnp.dot(left, right, preferred_element_type=jnp.float32)


def dot_rows(left, right):
    return lax.dot_general(
        left, right, (((1,), (1,)), ((), ())), preferred_element_type=jnp.float32
    )


def dot_tokens(left, right):
    return lax.dot_general(
        left, right, (((0,), (0,)), ((), ())), preferred_element_type=jnp.float32
    )


def bf16(values):
    return values.astype(jnp.bfloat16)


def moved(values, order):
    return bf16(dot(values, order))


def moved_back(values, order):
    return bf16(dot_rows(values, order))


def moved_back_wide(values, order):
    high = bf16(values)
    return dot_rows(high, order) + dot_rows(bf16(values - high.astype(FULL)), order)


def row_sum(values):
    return jnp.sum(values, axis=0, keepdims=True)


def norm_parts(values):
    centred = values - jnp.mean(values, axis=-1, keepdims=True)
    scale = lax.rsqrt(jnp.mean(centred * centred, axis=-1, keepdims=True) + NORM_EPS)
    return centred * scale, scale


def norm_back(unit, scale, grad_unit):
    mean_grad = jnp.mean(grad_unit, axis=-1, keepdims=True)
    mean_both = jnp.mean(grad_unit * unit, axis=-1, keepdims=True)
    return scale * (grad_unit - mean_grad - unit * mean_both)


GELU_ROOT = math.sqrt(2.0 / math.pi)
GELU_CUBE = 0.044715


def gelu_parts(values):
    square = values * values
    bent = jnp.tanh(GELU_ROOT * values * (1.0 + GELU_CUBE * square))
    half = 0.5 * (1.0 + bent)
    slope = half + 0.5 * values * (1.0 - bent * bent) * GELU_ROOT * (
        1.0 + 3.0 * GELU_CUBE * square
    )
    return values * half, slope


def silu_parts(values):
    gate = jax.nn.sigmoid(values)
    return values * gate, gate * (1.0 + values * (1.0 - gate))


def half_lanes(shape, which):
    lane = lax.broadcasted_iota(jnp.int32, shape, 1)
    return (lane < HD) if which == 0 else (lane >= HD)


def fetch(source, target, semaphore):
    return pltpu.make_async_copy(source, target, semaphore)


def group_of(groups, place, block, half):
    base = 5 * (place // 4)
    if place % 4 < 3:
        return groups[base + place % 4].at[block]
    if block < half:
        return groups[base + 3].at[block]
    return groups[base + 4].at[block - half]


def load_blocks(groups, half, first, size, held, semaphores, rows):
    copies = []
    for block in range(size):
        copies.append(
            [
                fetch(
                    group_of(groups, place, first + block, half),
                    held.at[block, pl.ds(place * rows, rows)],
                    semaphores.at[block, place],
                )
                for place in range(8)
            ]
        )
    return copies


def start_all(copies):
    for copy in copies:
        copy.start()


def wait_all(copies):
    for copy in copies:
        copy.wait()


def depth_of(relative, index):
    if not relative:
        return index
    return index ^ (lax.axis_index("fsdp") // 8)


def attn_forward_kernel(
    half,
    hidden,
    mods,
    bias,
    order,
    *refs,
):
    groups = refs[:10]
    normed_out, packed_out, log_out, attended_out, branch_out, middle_out = refs[10:16]
    held, attended, semaphores = refs[16:]
    copies = load_blocks(groups, half, 0, 4, held, semaphores, 96)
    for block in range(4):
        start_all(copies[block])
    unit, _ = norm_parts(hidden[...])
    normed_out[...] = moved(bf16(unit * (1.0 + mods[1:2]) + mods[0:1]), order[...])
    for block in range(3):
        wait_all(copies[block])
        packed_out[block] = bf16(dot(normed_out[...], held[block]) + bias[block : block + 1])
    lanes = lax.broadcasted_iota(jnp.int32, (TOK, 128), 1)

    def pair(index, logs):
        columns = pl.ds(pl.multiple_of(index * 128, 128), 128)
        queries, keys, values = (packed_out[part, :, columns] for part in range(3))
        halves = []
        for which in range(2):
            mask = half_lanes((TOK, 128), which)
            scores = dot_rows(jnp.where(mask, queries, 0), keys) * SCORE_SCALE
            top = jnp.max(scores, axis=-1, keepdims=True)
            raised = jnp.exp(scores - top)
            total = jnp.sum(raised, axis=-1, keepdims=True)
            halves.append(dot(bf16(raised * (1.0 / total)), values))
            logs = jnp.where(lanes == 2 * index + which, top + jnp.log(total), logs)
        attended[:, columns] = bf16(jnp.where(half_lanes((TOK, 128), 0), *halves))
        return logs

    log_out[...] = lax.fori_loop(0, D // 128, pair, jnp.zeros((TOK, 128), jnp.float32))
    attended_out[...] = moved(attended[...], order[...])
    wait_all(copies[3])
    branch = dot(attended_out[...], held[3]) + bias[3:4]
    branch_out[...] = branch
    middle_out[...] = hidden[...] + mods[2:3] * branch


def mlp_forward_kernel(half, first_down, relative, middle, mods, bias, order, down_order, *refs):
    groups = refs[:10]
    normed_out, slope_out, active_out, branch_out, hidden_out = refs[10:15]
    held_up, held_down, total, before, semaphores_up, semaphores_down = refs[15:]
    ups = load_blocks(groups, half, 4, 4, held_up, semaphores_up, 96)
    downs = load_blocks(groups, half, first_down, 4, held_down, semaphores_down, 96)
    for block in range(4):
        start_all(ups[block])
    for block in range(4):
        start_all(downs[block])
    unit, _ = norm_parts(middle[...])
    normed_out[...] = moved(bf16(unit * (1.0 + mods[4:5]) + mods[3:4]), order[...])
    for block in range(4):
        wait_all(ups[block])
        before[block] = dot(normed_out[...], held_up[block]) + bias[block + 4 : block + 5]
    for depth in range(4):
        active, slope = gelu_parts(before[depth_of(relative, depth)])
        active_out[depth] = moved(bf16(active), down_order[...])
        slope_out[depth] = moved(bf16(slope), down_order[...])
        wait_all(downs[depth])
        part = dot(active_out[depth], held_down[depth])
        total[...] = part if depth == 0 else total[...] + part
    branch = total[...] + bias[14:15]
    branch_out[...] = branch
    hidden_out[...] = middle[...] + mods[5:6] * branch


def mlp_backward_kernel(
    half,
    first_down,
    relative,
    grad_out,
    mods,
    middle,
    normed,
    slope,
    active,
    branch,
    order,
    down_order,
    *refs,
):
    groups = refs[:10]
    grad_middle_out, grad_mods_out, grad_bias_out, mine_out = refs[10:14]
    theirs_out = refs[14:18]
    held_up, held_down, made, low, grad_normed, semaphores_up, semaphores_down, sent = refs[18:]
    ups = load_blocks(groups, half, 4, 4, held_up, semaphores_up, 96)
    downs = load_blocks(groups, half, first_down, 4, held_down, semaphores_down, 96)
    for block in range(4):
        start_all(downs[block])
    for block in range(4):
        start_all(ups[block])
    grad_hidden = grad_out[...]
    grad_branch = grad_hidden * mods[5:6]
    grad_mods_out[2:3] = row_sum(grad_hidden * branch[...])
    grad_bias_out[4:5] = row_sum(grad_branch)
    grad_low = bf16(grad_branch)
    given = []
    for depth in range(4):
        wait_all(downs[depth])
        grad_active = dot_rows(grad_low, held_down[depth])
        made[4 + depth] = bf16(dot_tokens(active[depth], grad_low))
        given += give(made, 4 + depth, mine_out, theirs_out, sent)
        before_low = moved_back(
            bf16(grad_active * slope[depth].astype(FULL)), down_order[...]
        )
        low[depth_of(relative, depth)] = before_low
    for block in range(4):
        before_low = low[block]
        grad_bias_out[block : block + 1] = row_sum(before_low.astype(FULL))
        made[block] = bf16(dot_tokens(normed[...], before_low))
        given += give(made, block, mine_out, theirs_out, sent)
        wait_all(ups[block])
        part = dot_rows(before_low, held_up[block])
        grad_normed[...] = part if block == 0 else grad_normed[...] + part
    unit, scale = norm_parts(middle[...])
    grad_unit = moved_back_wide(grad_normed[...], order[...])
    grad_mods_out[0:1] = row_sum(grad_unit)
    grad_mods_out[1:2] = row_sum(grad_unit * unit)
    grad_middle_out[...] = grad_hidden + norm_back(unit, scale, grad_unit * (1.0 + mods[4:5]))
    wait_all(given)


def give(made, block, mine_out, theirs_outs, sent):
    length = made.shape[1] // 2
    step = theirs_outs[0].shape[0]
    theirs_out = theirs_outs[block // step].at[block % step]
    copies = [
        fetch(made.at[block, pl.ds(0, length)], mine_out.at[block], sent.at[0, block]),
        fetch(made.at[block, pl.ds(length, length)], theirs_out, sent.at[1, block]),
    ]
    start_all(copies)
    return copies


def attn_backward_kernel(
    half,
    grad_middle,
    mods,
    hidden,
    normed,
    packed,
    logs,
    attended,
    branch,
    order,
    *refs,
):
    groups = refs[:10]
    grad_hidden_out, grad_mods_out, grad_bias_out, mine_out = refs[10:14]
    theirs_out = refs[14:16]
    held, made, grad_packed, grad_attended, grad_normed, semaphores, sent = refs[16:]
    copies = load_blocks(groups, half, 0, 4, held, semaphores, 96)
    for block in (3, 0, 1, 2):
        start_all(copies[block])
    grad_mid = grad_middle[...]
    grad_branch = grad_mid * mods[2:3]
    grad_mods_out[2:3] = row_sum(grad_mid * branch[...])
    grad_bias_out[3:4] = row_sum(grad_branch)
    grad_low = bf16(grad_branch)
    made[3] = bf16(dot_tokens(attended[...], grad_low))
    given = give(made, 3, mine_out, theirs_out, sent)
    wait_all(copies[3])
    grad_attended[...] = moved_back(bf16(dot_rows(grad_low, held[3])), order[...])
    lanes = lax.broadcasted_iota(jnp.int32, (TOK, 128), 1)
    first = half_lanes((TOK, 128), 0)

    def pair(index, carry):
        columns = pl.ds(pl.multiple_of(index * 128, 128), 128)
        queries, keys, values = (packed[part, :, columns] for part in range(3))
        grad_pair = grad_attended[:, columns]
        grads = []
        for which in range(2):
            mask = half_lanes((TOK, 128), which)
            log_total = jnp.sum(
                jnp.where(lanes == 2 * index + which, logs[...], 0.0), axis=-1, keepdims=True
            )
            scores = dot_rows(jnp.where(mask, queries, 0), keys) * SCORE_SCALE
            attention = jnp.exp(scores - log_total)
            grad_attention = dot_rows(jnp.where(mask, grad_pair, 0), values)
            grad_values = dot_tokens(bf16(attention), grad_pair)
            weighted = attention * grad_attention
            grad_scores = weighted - attention * jnp.sum(weighted, axis=-1, keepdims=True)
            score_low = bf16(grad_scores * SCORE_SCALE)
            grads.append((dot(score_low, keys), dot_tokens(score_low, queries), grad_values))
        for part in range(3):
            both = jnp.where(first, grads[0][part], grads[1][part])
            grad_bias_out[part : part + 1, columns] = row_sum(both)
            grad_packed[part, :, columns] = bf16(both)
        return carry

    lax.fori_loop(0, D // 128, pair, 0)
    for block in range(3):
        grad_part = grad_packed[block]
        made[block] = bf16(dot_tokens(normed[...], grad_part))
        given += give(made, block, mine_out, theirs_out, sent)
        wait_all(copies[block])
        part = dot_rows(grad_part, held[block])
        grad_normed[...] = part if block == 0 else grad_normed[...] + part
    unit, scale = norm_parts(hidden[...])
    grad_unit = moved_back_wide(grad_normed[...], order[...])
    grad_mods_out[0:1] = row_sum(grad_unit)
    grad_mods_out[1:2] = row_sum(grad_unit * unit)
    grad_hidden_out[...] = grad_mid + norm_back(unit, scale, grad_unit * (1.0 + mods[1:2]))
    wait_all(given)


ONE_WIDTHS = (D, D, P_SIZE - 2 * D)
REST = P_SIZE + Z
CHUNK = P_SIZE // 4


def projector_kernel(
    half,
    first_one,
    relative,
    first,
    features,
    bias_one,
    bias_two,
    bias_three,
    order,
    chunk_order,
    *refs,
):
    groups, rest_groups = refs[:10], refs[10:20]
    outs = refs[20:32]
    grad_first_out, loss_out, grad_bias_one, grad_bias_two, grad_bias_three = outs[:5]
    one_mine, one_theirs, rest_mine, rest_theirs = outs[5], outs[6:7], outs[7], outs[8:]
    (
        held_one,
        held_rest,
        made_one,
        made_rest,
        slope_one,
        slope_two,
        active_one,
        active_two,
        wide,
        low,
        one_semaphores,
        rest_semaphores,
        one_sent,
        rest_sent,
    ) = refs[32:]
    ones = load_blocks(groups, half, first_one, 3, held_one, one_semaphores, 96)
    rests = load_blocks(rest_groups, 2, 0, 4, held_rest, rest_semaphores, 64)
    for copies in ones + rests:
        start_all(copies)
    chunks = [pl.ds(CHUNK * index, CHUNK) for index in range(4)]

    def source(depth):
        return pl.ds(pl.multiple_of(depth_of(relative, depth) * CHUNK, CHUNK), CHUNK)

    def bend(active, slope):
        for depth in range(4):
            values, slopes = silu_parts(wide[:, source(depth)])
            active[:, chunks[depth]] = moved(bf16(values), chunk_order[...])
            slope[:, chunks[depth]] = moved(bf16(slopes), chunk_order[...])

    first_low = moved(bf16(first[...]), order[...])
    running = 0
    for block, width in enumerate(ONE_WIDTHS):
        columns = slice(running, running + width)
        wait_all(ones[block])
        wide[:, columns] = dot(first_low, held_one[block, :, :width]) + bias_one[:, columns]
        running += width
    bend(active_one, slope_one)
    for copies in rests:
        wait_all(copies)

    def product(left, columns):
        total = dot(left[:, chunks[0]], held_rest[0, :, columns])
        for depth in range(1, 4):
            total = total + dot(left[:, chunks[depth]], held_rest[depth, :, columns])
        return total

    for index in range(4):
        wide[:, chunks[index]] = product(active_one, chunks[index]) + bias_two[:, chunks[index]]
    bend(active_two, slope_two)
    tail = pl.ds(P_SIZE, Z)
    result = product(active_two, tail) + bias_three[...]
    wanted = features[...]
    inner = jnp.sum(result * wanted, axis=-1, keepdims=True)
    own = jnp.sum(result * result, axis=-1, keepdims=True) + NORM_EPS
    length = jnp.sqrt(own) * jnp.sqrt(jnp.sum(wanted * wanted, axis=-1, keepdims=True) + NORM_EPS)
    cosine = inner / length
    loss_out[...] = jnp.broadcast_to(-0.5 / TOK * row_sum(cosine), (8, 128))
    grad_result = (-0.5 / TOK) * (wanted / length - result * (cosine / own))
    grad_bias_three[...] = row_sum(grad_result)
    grad_three = bf16(grad_result)
    for depth in range(4):
        made_rest[depth, :, tail] = bf16(dot_tokens(active_two[:, chunks[depth]], grad_three))

    def bend_back(grad, slope, depth, grad_bias):
        columns = source(depth)
        low[:, columns] = moved_back(
            bf16(grad * slope[:, chunks[depth]].astype(FULL)), chunk_order[...]
        )
        grad_bias[:, columns] = row_sum(low[:, columns].astype(FULL))

    for depth in range(4):
        bend_back(dot_rows(grad_three, held_rest[depth, :, tail]), slope_two, depth, grad_bias_two)
    given = []
    main = pl.ds(0, P_SIZE)
    for depth in range(4):
        made_rest[depth, :, main] = bf16(dot_tokens(active_one[:, chunks[depth]], low[...]))
        given += give(made_rest, depth, rest_mine, rest_theirs, rest_sent)
    for depth in range(4):
        wide[:, chunks[depth]] = dot_rows(low[...], held_rest[depth, :, main])
    for depth in range(4):
        bend_back(wide[:, chunks[depth]], slope_one, depth, grad_bias_one)
    running = 0
    grad_first = None
    for block, width in enumerate(ONE_WIDTHS):
        grad_part = low[:, running : running + width]
        made_one[block, :, :width] = bf16(dot_tokens(first_low, grad_part))
        if width < D:
            made_one[block, :, width:] = jnp.zeros((D, D - width), LOW)
        given += give(made_one, block, one_mine, one_theirs, one_sent)
        part = dot_rows(grad_part, held_one[block, :, :width])
        grad_first = part if grad_first is None else grad_first + part
        running += width
    grad_first_out[...] = moved_back_wide(grad_first, order[...])
    wait_all(given)


def head_kernel(
    hidden,
    mods,
    head,
    head_bias,
    targets,
    time_weight,
    grad_hidden_out,
    grad_mods_out,
    grad_head_out,
    grad_head_bias_out,
    loss_out,
):
    unit, scale = norm_parts(hidden[...])
    final_low = bf16(unit * (1.0 + mods[1:2]) + mods[0:1])
    residual = dot(final_low, head[...]) + head_bias[...] - targets[...]
    weight = time_weight[...]
    square = jnp.sum(row_sum(residual * residual), axis=1, keepdims=True)
    loss_out[...] = jnp.broadcast_to(square * weight / (TOK * PD), (8, 128))
    grad_output = (2.0 / (TOK * PD)) * weight * residual
    grad_head_bias_out[...] = row_sum(grad_output)
    grad_low = bf16(grad_output)
    grad_head_out[...] = dot_tokens(final_low, grad_low)
    grad_unit = dot_rows(grad_low, head[...])
    grad_mods_out[0:1] = row_sum(grad_unit)
    grad_mods_out[1:2] = row_sum(grad_unit * unit)
    grad_hidden_out[...] = norm_back(unit, scale, grad_unit * (1.0 + mods[1:2]))


def full_sum(values):
    return row_sum(jnp.sum(values, axis=1, keepdims=True))


def update_kernel(
    count,
    raw_in,
    raw_down,
    raw_main,
    raw_rest,
    old_in,
    old_down,
    old_main,
    old_rest,
    rows_in,
    rows_down,
    rows_main,
    rows_rest,
    cols_in,
    cols_down,
    cols_main,
    cols_rest,
    squares_in,
    squares_down,
    squares_main,
    squares_rest,
    row_sums,
    late_bias,
    head_sum,
    head_old,
    head_row_old,
    head_col_old,
    flat_in,
    flat_down,
    flat_main,
    flat_rest,
    bias_raw,
    bias_old,
    bias_second,
    scales_out,
    new_head,
    clip_head,
    new_head_rows,
    new_head_cols,
    new_rows_in,
    new_rows_down,
    new_rows_main,
    new_rows_rest,
    new_bias,
    clip_bias,
    new_second,
    new_in,
    clip_in,
    copy_in,
    new_cols_in,
    new_down,
    clip_down,
    copy_down,
    new_cols_down,
    new_main,
    clip_main,
    copy_main,
    new_cols_main,
    new_rest,
    clip_rest,
    copy_rest,
    new_cols_rest,
):
    total = row_sums[0:1, 6:7] + full_sum(late_bias[...] * late_bias[...])
    total = total + full_sum(head_sum[...] * head_sum[...])
    for squares in (squares_in, squares_down, squares_main, squares_rest):
        total = total + full_sum(squares[...])
    norm = jnp.sqrt(total)
    clip = jnp.minimum(1.0, CLIP_LIMIT / norm)
    scales_out[0:1] = jnp.broadcast_to(norm, (1, 128))
    scales_out[1:2] = jnp.broadcast_to(clip, (1, 128))

    def decayed(old, squares, length):
        return DECAY_RATE * old + (1.0 - DECAY_RATE) * (
            clip * (clip * (squares / length)) + FACTOR_EPS
        )

    head_clip = clip * head_sum[...]
    head_squares = head_sum[...] * head_sum[...]
    head_rows = decayed(
        head_row_old[...], jnp.sum(head_squares, axis=1, keepdims=True), head_sum.shape[1]
    )
    head_cols = decayed(head_col_old[...], row_sum(head_squares), head_sum.shape[0])
    head_mean = row_sum(head_rows) / head_sum.shape[0]
    clip_head[...] = head_clip
    new_head_rows[...] = head_rows
    new_head_cols[...] = head_cols
    new_head[...] = head_old[...] - LEARN_RATE * head_clip * lax.rsqrt(
        head_rows * head_cols / head_mean
    )
    half = flat_in.shape[0] // 2
    new_rows_in[...] = decayed(flat_in[:half], flat_in[half:], raw_in.shape[2])
    half = flat_down.shape[0] // 2
    new_rows_down[...] = decayed(flat_down[:half], flat_down[half:], raw_down.shape[2])
    new_rows_main[...] = decayed(flat_main[0:1], flat_main[1:2], raw_main.shape[1])
    new_rows_rest[...] = decayed(flat_rest[0:1], flat_rest[1:2], raw_rest.shape[1])
    bias_clip = clip * bias_raw[...]
    second = DECAY_RATE * bias_second[...] + (1.0 - DECAY_RATE) * (
        bias_clip * bias_clip + FACTOR_EPS
    )
    clip_bias[...] = bias_clip
    new_second[...] = second
    new_bias[...] = bias_old[...] - LEARN_RATE * bias_clip * lax.rsqrt(second)

    def step(place, old, raw, pair, col_old, squares):
        rows, columns = raw.shape
        rows_all = count * rows
        row_new = decayed(pair[:, 0:1], pair[:, 1:2], columns)
        col_new = decayed(col_old, squares, rows_all)
        row_mean = (
            DECAY_RATE * row_sums[0:1, place : place + 1]
            + (1.0 - DECAY_RATE) * (clip * (clip * (full_sum(squares) / columns)))
        ) / rows_all + (1.0 - DECAY_RATE) * FACTOR_EPS
        clipped = clip * raw
        estimate = row_new * col_new / row_mean
        return old - LEARN_RATE * clipped * lax.rsqrt(estimate), clipped, col_new

    for level in range(L):
        one = slice(level, level + 1)
        for place, old, raw, pair, col_old, squares, new, clipped, copy, cols in (
            (level, old_in, raw_in, rows_in, cols_in, squares_in, new_in, clip_in, copy_in, new_cols_in),
            (
                L + level,
                old_down,
                raw_down,
                rows_down,
                cols_down,
                squares_down,
                new_down,
                clip_down,
                copy_down,
                new_cols_down,
            ),
        ):
            made = step(
                place, old[level], raw[level], pair[level], col_old[one], squares[one]
            )
            new[level], clipped[level], cols[one] = made
            copy[level] = bf16(made[0])
    for place, old, raw, pair, col_old, squares, new, clipped, copy, cols in (
        (
            2 * L,
            old_main,
            raw_main,
            rows_main,
            cols_main,
            squares_main,
            new_main,
            clip_main,
            copy_main,
            new_cols_main,
        ),
        (
            2 * L + 1,
            old_rest,
            raw_rest,
            rows_rest,
            cols_rest,
            squares_rest,
            new_rest,
            clip_rest,
            copy_rest,
            new_cols_rest,
        ),
    ):
        made = step(place, old[...], raw[...], pair[...], col_old[...], squares[...])
        new[...], clipped[...], cols[...] = made
        copy[...] = bf16(made[0])


def cost(microseconds):
    return pl.CostEstimate(flops=microseconds, bytes_accessed=0, transcendentals=0)


VMEM_GRANT = 60 * 2**20
VMEM_WHOLE = pl.BlockSpec(memory_space=pltpu.VMEM)
IN_PLACE = pl.BlockSpec(memory_space=pl.ANY)


def shaped(kind, *shape):
    return jax.ShapeDtypeStruct(shape, kind)


def call(kernel, inputs, far_inputs, outputs, far_outputs, scratch, microseconds, limit):
    return pl.pallas_call(
        kernel,
        in_specs=[VMEM_WHOLE] * len(inputs) + [IN_PLACE] * len(far_inputs),
        out_specs=[VMEM_WHOLE] * len(outputs) + [IN_PLACE] * len(far_outputs),
        out_shape=[*outputs, *far_outputs],
        scratch_shapes=scratch,
        cost_estimate=cost(microseconds),
        compiler_params=pltpu.CompilerParams(vmem_limit_bytes=VMEM_GRANT),
    )(*inputs, *far_inputs)


BLOCK_SEMAPHORES = pltpu.SemaphoreType.DMA((4, 8))


def orders_kernel(narrow_source, down_source, chunk_source, narrow, down, chunk):
    for source, order in [(narrow_source, narrow), (down_source, down), (chunk_source, chunk)]:
        rows = lax.broadcasted_iota(jnp.int32, order.shape, 0)
        order[...] = jnp.where(rows == source[...], 1.0, 0.0).astype(LOW)


class Orders:
    def __init__(self, position, relative):
        self.relative = relative
        near, depth = (position & 7, position >> 3) if relative else (0, 0)

        def places(index):
            if not relative:
                return index
            return near ^ (((index & 3) << 1) | (index >> 2))

        column = jnp.arange(D)
        narrow = column
        if relative:
            group, deep, inner = column // 96, (column // 24) % 4, column % 24
            narrow = ((deep ^ depth) * 8 + places(group)) * 24 + inner
        down = places(column // 96) * 96 + column % 96
        column = jnp.arange(CHUNK)
        chunk = places(column // 64) * 64 + column % 64
        sources = [source[None].astype(jnp.int32) for source in (narrow, down, chunk)]
        self.narrow, self.down, self.chunk = pl.pallas_call(
            orders_kernel,
            in_specs=[VMEM_WHOLE] * 3,
            out_specs=[VMEM_WHOLE] * 3,
            out_shape=[shaped(LOW, D, D), shaped(LOW, D, D), shaped(LOW, CHUNK, CHUNK)],
            cost_estimate=cost(3),
            compiler_params=pltpu.CompilerParams(vmem_limit_bytes=VMEM_GRANT),
        )(*sources)


def attn_forward(hidden, mods, bias, orders, gathered):
    return call(
        functools.partial(attn_forward_kernel, gathered.half),
        [hidden, mods, bias, orders.narrow],
        gathered.groups,
        [
            shaped(LOW, TOK, D),
            shaped(LOW, 3, TOK, D),
            shaped(FULL, TOK, 128),
            shaped(LOW, TOK, D),
            shaped(FULL, TOK, D),
            shaped(FULL, TOK, D),
        ],
        [],
        [pltpu.VMEM((4, D, D), LOW), pltpu.VMEM((TOK, D), LOW), BLOCK_SEMAPHORES],
        11,
        32,
    )


def mlp_forward(middle, mods, bias, orders, gathered):
    return call(
        functools.partial(
            mlp_forward_kernel, gathered.half, gathered.first_down, orders.relative
        ),
        [middle, mods, bias, orders.narrow, orders.down],
        gathered.groups,
        [
            shaped(LOW, TOK, D),
            shaped(LOW, 4, TOK, D),
            shaped(LOW, 4, TOK, D),
            shaped(FULL, TOK, D),
            shaped(FULL, TOK, D),
        ],
        [],
        [
            pltpu.VMEM((4, D, D), LOW),
            pltpu.VMEM((4, D, D), LOW),
            pltpu.VMEM((TOK, D), FULL),
            pltpu.VMEM((4, TOK, D), FULL),
            BLOCK_SEMAPHORES,
            BLOCK_SEMAPHORES,
        ],
        11,
        40,
    )


def mlp_backward(grad_out, mods, kept, orders, gathered):
    return call(
        functools.partial(
            mlp_backward_kernel, gathered.half, gathered.first_down, orders.relative
        ),
        [grad_out, mods, *kept, orders.narrow, orders.down],
        gathered.groups,
        [shaped(FULL, TOK, D), shaped(FULL, 3, D), shaped(FULL, 5, D)],
        [shaped(LOW, 8, D // 2, D)] + [shaped(LOW, 2, D // 2, D)] * 4,
        [
            pltpu.VMEM((4, D, D), LOW),
            pltpu.VMEM((4, D, D), LOW),
            pltpu.VMEM((8, D, D), LOW),
            pltpu.VMEM((4, TOK, D), LOW),
            pltpu.VMEM((TOK, D), FULL),
            BLOCK_SEMAPHORES,
            BLOCK_SEMAPHORES,
            pltpu.SemaphoreType.DMA((2, 8)),
        ],
        16,
        48,
    )


def attn_backward(grad_middle, mods, kept, orders, gathered):
    return call(
        functools.partial(attn_backward_kernel, gathered.half),
        [grad_middle, mods, *kept, orders.narrow],
        gathered.groups,
        [shaped(FULL, TOK, D), shaped(FULL, 3, D), shaped(FULL, 4, D)],
        [shaped(LOW, 4, D // 2, D)] + [shaped(LOW, 2, D // 2, D)] * 2,
        [
            pltpu.VMEM((4, D, D), LOW),
            pltpu.VMEM((4, D, D), LOW),
            pltpu.VMEM((3, TOK, D), LOW),
            pltpu.VMEM((TOK, D), LOW),
            pltpu.VMEM((TOK, D), FULL),
            BLOCK_SEMAPHORES,
            pltpu.SemaphoreType.DMA((2, 4)),
        ],
        13,
        40,
    )


def projector(first, features, bias_one, bias_two, bias_three, orders, gathered, rest_gathered):
    return call(
        functools.partial(
            projector_kernel, gathered.half, gathered.first_one, orders.relative
        ),
        [first, features, bias_one, bias_two, bias_three, orders.narrow, orders.chunk],
        [*gathered.groups, *rest_gathered.groups],
        [
            shaped(FULL, TOK, D),
            shaped(FULL, 8, 128),
            shaped(FULL, 1, P_SIZE),
            shaped(FULL, 1, P_SIZE),
            shaped(FULL, 1, Z),
        ],
        [
            shaped(LOW, 3, D // 2, D),
            shaped(LOW, 3, D // 2, D),
            shaped(LOW, 4, CHUNK // 2, REST),
        ]
        + [shaped(LOW, 1, CHUNK // 2, REST)] * 4,
        [
            pltpu.VMEM((3, D, D), LOW),
            pltpu.VMEM((4, CHUNK, REST), LOW),
            pltpu.VMEM((3, D, D), LOW),
            pltpu.VMEM((4, CHUNK, REST), LOW),
            pltpu.VMEM((TOK, P_SIZE), LOW),
            pltpu.VMEM((TOK, P_SIZE), LOW),
            pltpu.VMEM((TOK, P_SIZE), LOW),
            pltpu.VMEM((TOK, P_SIZE), LOW),
            pltpu.VMEM((TOK, P_SIZE), FULL),
            pltpu.VMEM((TOK, P_SIZE), LOW),
            pltpu.SemaphoreType.DMA((3, 8)),
            BLOCK_SEMAPHORES,
            pltpu.SemaphoreType.DMA((2, 3)),
            pltpu.SemaphoreType.DMA((2, 4)),
        ],
        27,
        56,
    )


def head(hidden, mods, head_low, head_bias, targets, time_weight):
    return call(
        head_kernel,
        [hidden, mods, head_low, head_bias, targets, time_weight],
        [],
        [
            shaped(FULL, TOK, D),
            shaped(FULL, 2, D),
            shaped(FULL, D, PD),
            shaped(FULL, 1, PD),
            shaped(FULL, 8, 128),
        ],
        [],
        [],
        5,
        24,
    )


def swap(array, mask, count):
    return lax.ppermute(array, "fsdp", [(place, place ^ mask) for place in range(count)])


def bit_of(position, bit):
    return (position >> bit) & 1


def pick(array, bits, chosen):
    sizes, starts, lengths = [], [], []
    previous = None
    for bit in bits:
        fixed = bit in chosen
        if fixed != previous:
            sizes.append(1)
            starts.append(0)
            lengths.append(1)
        sizes[-1] *= 2
        if fixed:
            starts[-1] = starts[-1] * 2 + chosen[bit]
        else:
            lengths[-1] *= 2
        previous = fixed
    ahead, tail = array.shape[:1], array.shape[2:]
    view = array.reshape(ahead + tuple(sizes) + tail)
    starts = [jnp.int32(0)] + [jnp.asarray(start, jnp.int32) for start in starts]
    starts += [jnp.int32(0)] * len(tail)
    taken = lax.dynamic_slice(view, starts, ahead + tuple(lengths) + tail)
    return taken.reshape(ahead + (-1,) + tail)


def scatter_sum(parts, bit_order, position, count, kind, before=()):
    before = dict(before)
    all_bits = list(reversed(range(count.bit_length() - 1)))
    held = [(parts, all_bits)]
    fixed = {}

    def totals(chosen):
        summed = [None] * len(parts)
        for arrays, bits in held:
            wanted = {bit: value for bit, value in chosen.items() if bit in bits}
            for slot, array in enumerate(arrays):
                piece = pick(array, bits, wanted).astype(jnp.float32)
                summed[slot] = piece if summed[slot] is None else summed[slot] + piece
        return summed

    for bit in bit_order:
        mine = bit_of(position, bit)
        pieces = [piece.astype(kind) for piece in totals({**fixed, bit: 1 - mine})]
        if bit in before:
            pieces = before[bit](pieces)
        shapes = [piece.shape for piece in pieces]
        if len(pieces) == 1:
            received = [swap(pieces[0], 1 << bit, count)]
        else:
            width = pieces[0].shape[-1]
            flat = [piece.reshape(-1, width) for piece in pieces]
            moved = swap(jnp.concatenate(flat), 1 << bit, count)
            received, running = [], 0
            for piece, shape in zip(flat, shapes):
                received.append(moved[running : running + piece.shape[0]].reshape(shape))
                running += piece.shape[0]
        fixed[bit] = mine
        held.append((received, [other for other in all_bits if other not in fixed]))
    return [piece[:, 0] for piece in totals(fixed)]


def meet(*values):
    return lax.optimization_barrier(values)


class Gather:
    def __init__(self, pack, wide, count):
        self.pack, self.wide, self.count = pack, wide, count

    def move(self, array, mask):
        return swap(array, mask, self.count)

    def merged(self, packs):
        width = self.pack.shape[-1]
        long = [pack[self.wide :].reshape(1, -1, width) for pack in packs]
        if not self.wide:
            return jnp.concatenate(long)
        short = jnp.stack([pack[: self.wide] for pack in packs], axis=1)
        return jnp.concatenate([short.reshape(self.wide, -1, width)] + long)

    def along_z(self):
        self.deep = [self.pack] + [self.move(self.pack, mask) for mask in (8, 16, 24)]

    def merge(self):
        self.quad = self.merged(self.deep)
        self.half = self.quad.shape[0] // 2

    def along_xy(self):
        self.by_y = self.move(self.quad, 4)
        self.by_x = self.move(self.quad, 2)

    def across(self):
        self.far = [
            self.move(self.by_y[: self.half], 2),
            self.move(self.by_x[self.half :], 4),
        ]

    def finish(self):
        own = [self.quad, self.by_x, self.by_y, *self.far]
        self.groups = own + [self.move(group, 1) for group in own]


class PlainGather(Gather):
    def along_z(self):
        pass

    merge = along_xy = across = along_z

    def finish(self):
        full = lax.all_gather(self.pack, "fsdp")
        _, _, rows, width = full.shape
        long = full[:, self.wide :].reshape(4, 8, -1, width)
        blocks = long
        if self.wide:
            short = jnp.swapaxes(full[:, : self.wide], 0, 1).reshape(self.wide, 8, -1, width)
            blocks = jnp.concatenate([short, long])
        self.half = blocks.shape[0] // 2
        self.groups = []
        for core in range(2):
            group = [blocks[:, 4 * core + place] for place in range(4)]
            self.groups += group[:3] + [group[3][: self.half], group[3][self.half :]]


def across_kernel(counts, rows, half, *refs):
    arrays, (far_y, far_x, own, other, semaphores) = refs[:-5], refs[-5:]
    copies = load_sums(arrays, counts, 3 * rows, rows, own, other, semaphores)
    start_all(copies)
    wait_all(copies)
    for block in range(sum(map(sum, counts))):
        total = bf16(own[block].astype(FULL) + other[block].astype(FULL))
        if block < half:
            far_y[block] = total
        else:
            far_x[block - half] = total


def load_sums(arrays, counts, first, rows, own, other, semaphores):
    copies, running, index = [], 0, 0

    def load(target, start, size):
        source = arrays[index].at[:, pl.ds(first, rows)]
        copies.append(fetch(source, target.at[pl.ds(start, size)], semaphores.at[index]))

    for sizes in counts:
        load(own, running, sum(sizes))
        index += 1
        for size in sizes:
            load(other, running, size)
            index += 1
            running += size
    return copies


def along_xy_kernel(counts, rows, half, far_y, far_x, *refs):
    arrays, (to_x, to_y, own, other, semaphores) = refs[:-5], refs[-5:]
    copies = load_sums(arrays, counts, rows, 2 * rows, own, other, semaphores)
    start_all(copies)
    wait_all(copies)
    for block in range(sum(map(sum, counts))):
        total = own[block, :rows].astype(FULL) + other[block, :rows].astype(FULL)
        if block < half:
            total = total + far_y[block].astype(FULL)
        to_x[block] = bf16(total)
        total = own[block, rows:].astype(FULL) + other[block, rows:].astype(FULL)
        if block >= half:
            total = total + far_x[block - half].astype(FULL)
        to_y[block] = bf16(total)


def along_z_kernel(counts, rows, kinds, by_x, by_y, *refs):
    arrays, outs, (own, other, semaphores) = refs[:-7], refs[-7:-3], refs[-3:]
    copies = load_sums(arrays, counts, 0, rows, own, other, semaphores)
    start_all(copies)
    wait_all(copies)
    made = 0
    for block, (kind, depth) in enumerate(kinds):
        total = own[block].astype(FULL) + other[block].astype(FULL)
        total = total + by_x[block].astype(FULL) + by_y[block].astype(FULL)
        if kind == "long":
            step = outs[0].shape[1]
            for index in range(rows // step):
                part = total[index * step : (index + 1) * step]
                outs[depth][made + index] = part.astype(outs[depth].dtype)
            made += rows // step if depth == 3 else 0
        else:
            step = rows // 4
            for deep in range(4):
                part = total[deep * step : (deep + 1) * step]
                outs[deep][made] = part.astype(outs[deep].dtype)
            made += 1


class Scatter:
    def __init__(self, parts, count):
        self.parts, self.count = parts, count
        self.sizes = [[piece.shape[0] for piece in theirs] for _, theirs, _, _ in parts]
        self.blocks = sum(map(sum, self.sizes))
        self.half = self.blocks // 2
        self.rows, self.width = parts[0][0].shape[1] // 4, parts[0][0].shape[2]

    def move(self, array, mask):
        return swap(array, mask, self.count)

    def cores(self):
        self.held = []
        for mine, theirs, _, _ in self.parts:
            self.held += [mine] + [self.move(piece, 1) for piece in theirs]

    def call(self, kernel, extra, near, outs, length):
        return pl.pallas_call(
            kernel,
            in_specs=[VMEM_WHOLE] * len(near) + [IN_PLACE] * len(self.held),
            out_specs=[VMEM_WHOLE] * len(outs),
            out_shape=outs,
            scratch_shapes=[
                pltpu.VMEM((self.blocks, length, self.width), LOW),
                pltpu.VMEM((self.blocks, length, self.width), LOW),
                pltpu.SemaphoreType.DMA((len(self.held),)),
            ],
            cost_estimate=cost(4),
            compiler_params=pltpu.CompilerParams(vmem_limit_bytes=VMEM_GRANT),
        )(*near, *self.held)

    def make_far(self):
        self.to_far = self.call(
            functools.partial(across_kernel, self.sizes, self.rows, self.half),
            (),
            [],
            [
                shaped(LOW, self.half, self.rows, self.width),
                shaped(LOW, self.blocks - self.half, self.rows, self.width),
            ],
            self.rows,
        )

    def across(self):
        self.far = [self.move(self.to_far[0], 4), self.move(self.to_far[1], 2)]

    def make_near(self):
        self.to_near = self.call(
            functools.partial(along_xy_kernel, self.sizes, self.rows, self.half),
            (),
            self.far,
            [shaped(LOW, self.blocks, self.rows, self.width)] * 2,
            2 * self.rows,
        )

    def along_xy(self):
        self.near = [self.move(self.to_near[0], 2), self.move(self.to_near[1], 4)]

    def make_deep(self):
        kinds = []
        for _, _, short, long in self.parts:
            kinds += [("short", 0)] * short + [("long", depth) for depth in range(long)]
        shorts = sum(short for _, _, short, _ in self.parts)
        step, made = (self.rows // 4, self.blocks) if shorts else (self.rows, 1)
        outs = [shaped(FULL, made, step, self.width)]
        outs += [shaped(LOW, made, step, self.width)] * 3
        self.own, *self.to_deep = self.call(
            functools.partial(along_z_kernel, self.sizes, self.rows, kinds),
            (),
            self.near,
            outs,
            self.rows,
        )

    def along_z(self):
        self.deep = [self.move(part, mask) for part, mask in zip(self.to_deep, (8, 16, 24))]

    def result(self):
        total = self.own
        for part in self.deep:
            total = total + part.astype(FULL)
        return total


class PlainScatter(Scatter):
    def cores(self):
        pass

    make_far = across = make_near = along_xy = make_deep = along_z = cores

    def result(self):
        whole = []
        for mine, theirs, short, long in self.parts:
            full = jnp.concatenate([mine, jnp.concatenate(theirs)], axis=1)
            if short:
                whole.append(full[:short].reshape(short, self.count, -1, self.width))
            if long:
                whole.append(full[short:].reshape(1, self.count, -1, self.width))
        position = lax.axis_index("fsdp")
        order = range(self.count.bit_length() - 1)
        sums = scatter_sum(whole, order, position, self.count, LOW)
        rows = min(part.shape[1] for part in sums)
        return jnp.concatenate([part.reshape(-1, rows, self.width) for part in sums])


def order_of(places, position):
    device = jnp.arange(len(places))[:, None]
    return (device == (jnp.array(places)[None, :] ^ position)).astype(LOW)


def ordered(blocks, places, position):
    flat = dot(order_of(places, position), blocks.reshape(len(places), -1))
    return flat.astype(LOW).reshape(blocks.shape)


def gather_all(array, position, count, masks, between=None):
    blocks = array[None]
    places = [0]
    for step, mask in enumerate(masks):
        if step == 2 and between is not None:
            blocks = between(blocks)
        blocks = jnp.concatenate([blocks, swap(blocks, mask, count)], axis=0)
        places = places + [place ^ mask for place in places]
    return ordered(blocks, places, position)


def gather_and_turn(array, parts, position, count, between):
    blocks = array[None]
    places = [0]
    turned = ordered(parts, list(range(count)), position)
    rows = parts.shape[1]
    for bit in reversed(range(count.bit_length() - 1)):
        if bit == 2 or bit == 0:
            blocks = between[bit](blocks)
        halves = turned.reshape(-1, 2, 1 << bit, rows, 128)
        kept, sent = halves[:, 0], halves[:, 1]
        sent = jnp.concatenate([blocks.reshape(-1, 128), sent.reshape(-1, 128)])
        received = swap(sent, 1 << bit, count)
        size = blocks.shape[0] * blocks.shape[1]
        blocks = jnp.concatenate([blocks, received[:size].reshape(blocks.shape)])
        places = places + [place ^ (1 << bit) for place in places]
        turned = jnp.stack([kept, received[size:].reshape(kept.shape)], axis=1)
    turned = turned.reshape(parts.shape)
    return ordered(blocks, places, position), ordered(turned, list(range(count)), position)


def gather_and_sum(array, parts, position, count, between):
    blocks = array[None]
    all_bits = list(reversed(range(count.bit_length() - 1)))
    held = [(parts[None], all_bits)]
    fixed = {}

    def total(chosen):
        summed = None
        for part, bits in held:
            wanted = {bit: value for bit, value in chosen.items() if bit in bits}
            piece = pick(part, bits, wanted).astype(FULL)
            summed = piece if summed is None else summed + piece
        return summed

    for bit in range(count.bit_length() - 1):
        mine = bit_of(position, bit)
        piece = total({**fixed, bit: 1 - mine}).astype(LOW)
        sent = jnp.concatenate([blocks.reshape(-1, 128), piece.reshape(-1, 128)])
        if bit in between:
            sent = between[bit](sent)
        received = swap(sent, 1 << bit, count)
        size = blocks.shape[0] * blocks.shape[1]
        blocks = jnp.concatenate([blocks, received[:size].reshape(blocks.shape)])
        fixed[bit] = mine
        left = [other for other in all_bits if other not in fixed]
        held.append((received[size:].reshape(piece.shape), left))
    return blocks, total(fixed)[0, 0]


def sum_all(array, count):
    mask = 1
    while mask < count:
        array = array + swap(array, mask, count)
        mask *= 2
    return array


def split_high(values):
    return (values // 32).astype(jnp.bfloat16), (values % 32).astype(jnp.bfloat16)


def body(
    count,
    latents,
    targets,
    features,
    time_weights,
    timesteps,
    classes,
    block_in,
    block_in_rows,
    block_in_cols,
    block_down,
    block_down_rows,
    block_down_cols,
    stem_main,
    stem_main_rows,
    stem_main_cols,
    stem_proj,
    stem_proj_rows,
    stem_proj_cols,
    head_weight,
    head_rows,
    head_cols,
    biases,
    bias_second,
):
    position = lax.axis_index("fsdp")
    images = count * latents.shape[0]
    width_rows = block_in.shape[1]
    bias_part = biases.shape[0]
    bias_cols = -(-bias_part // width_rows)
    bits = count.bit_length() - 1
    gather = Gather if count == 32 else PlainGather
    scatter = Scatter if count == 32 else PlainScatter
    time_out_part, final_ada_part, table_part, patch_part, proj_one_part, time_in_part = cut_parts(
        stem_main, [D, 2 * D, NCLS, PD, P_SIZE, TF]
    )
    main_width = 3 * D + D + F
    main_blocks = main_width // D
    def blocks_of(part, width):
        return jnp.swapaxes(part.astype(LOW).reshape(part.shape[0], -1, width), 0, 1)

    one_part = jnp.pad(proj_one_part, ((0, 0), (0, 3 * D - P_SIZE)))
    layers = []
    for level in range(L):
        main = [blocks_of(block_in[level, :, :main_width], D)]
        if level == 0:
            main.append(blocks_of(one_part, D))
        down = block_down[level].astype(LOW).reshape(4, width_rows, D)
        wide = sum(part.shape[0] for part in main)
        layers.append(gather(jnp.concatenate(main + [down]), wide, count))
        layers[level].first_one = main_blocks
        layers[level].first_down = wide
    rest = gather(stem_proj.astype(LOW)[None], 0, count)

    time_high, time_low = split_high(timesteps)
    class_high, class_low = split_high(classes)
    small = jnp.concatenate(
        [
            biases.astype(LOW),
            patch_part.astype(LOW).reshape(-1),
            time_high,
            time_low,
            class_high,
            class_low,
        ]
    )
    used = small.shape[0]
    small = jnp.pad(small, (0, -used % 2048))
    head_size = small.shape[0]
    small = jnp.concatenate([small, time_in_part.astype(LOW).reshape(-1)])
    small = jnp.pad(small, (0, -small.shape[0] % 2048)).reshape(-1, 128)
    turned = jnp.swapaxes(time_out_part.astype(LOW).reshape(width_rows, count, width_rows), 0, 1)
    turned = turned.reshape(count, -1)
    turned_used = turned.shape[1]
    turned = jnp.pad(turned, ((0, 0), (0, -turned_used % 2048))).reshape(count, -1, 128)

    def start_gathers(blocks):
        blocks, layers[0].pack = meet(blocks, layers[0].pack)
        layers[0].along_z()
        return blocks

    def see_one(blocks):
        if count == 32:
            blocks, layers[0].deep[2] = meet(blocks, layers[0].deep[2])
        return blocks

    small_all, time_out_mine = gather_and_turn(
        small, turned, position, count, {2: start_gathers, 0: see_one}
    )
    small_all = small_all.reshape(count, -1)
    orders = Orders(position, count == 32)
    bias_full = small_all[:, :bias_part].reshape(-1).astype(FULL)
    patch_t = small_all[:, bias_part : used - 4].reshape(D, PD)
    marks = small_all[:, used - 4 : used].astype(jnp.int32)
    time_in = small_all[:, head_size : head_size + width_rows * TF].reshape(D, TF)
    time_out_mine = time_out_mine.reshape(count, -1)[:, :turned_used].reshape(D, width_rows)
    times_all = marks[:, 0] * 32 + marks[:, 1]
    classes_all = marks[:, 2] * 32 + marks[:, 3]
    block_bias = bias_full[: L * VB].reshape(L, VB // D, D)
    stem_bias = bias_full[L * VB :]
    bias_tin, bias_tout, bias_final, bias_patch, bias_one, bias_two, bias_three = cut_parts(
        stem_bias, [D, D, 2 * D, D, P_SIZE, P_SIZE, Z]
    )

    def mine(values):
        return lax.dynamic_slice_in_dim(values, position * width_rows, width_rows)

    latent_low = latents.reshape(TOK, PD).astype(jnp.bfloat16)
    hidden = (
        lax.dot_general(
            latent_low, patch_t, (((1,), (1,)), ((), ())), preferred_element_type=jnp.float32
        )
        + bias_patch
        + positions()
    )
    freq_low = time_freq(times_all).astype(LOW)
    embed_hidden = dot_rows(time_in, freq_low) + bias_tin[:, None]
    embed_act = jax.nn.silu(embed_hidden).astype(LOW)
    one_hot = classes_all[:, None] == jnp.arange(NCLS)[None, :]
    class_embed = dot_rows(table_part.astype(LOW), one_hot.astype(LOW))
    condition = dot_tokens(time_out_mine, embed_act) + mine(bias_tout)[:, None] + class_embed
    cond_low = jax.nn.silu(condition).astype(LOW)

    ada_mine = jnp.concatenate(
        [block_in[level, :, 3 * D + D + F :] for level in range(L)] + [final_ada_part], axis=1
    ).astype(LOW)
    mod_part = dot_tokens(cond_low, ada_mine).reshape(1, images, -1, 128)
    before = {}
    if count == 32:

        def start_near(pieces):
            pieces, layers[0].deep = meet(pieces, layers[0].deep)
            layers[0].merge()
            layers[0].along_xy()
            return pieces

        before = {3: start_near}
    (mods,) = scatter_sum([mod_part], range(bits), position, count, FULL, before)
    mods, rest.pack = meet(mods, rest.pack)
    rest.along_z()
    if count == 32:
        mods, layers[0].by_x, layers[0].by_y, rest.deep, hidden, block_bias = meet(
            mods, layers[0].by_x, layers[0].by_y, rest.deep, hidden, block_bias
        )
    mods = mods.reshape(-1)
    bias_ada = jnp.concatenate(
        [block_bias[level, 8:14].reshape(-1) for level in range(L)] + [bias_final]
    )
    mods = (mods + bias_ada).reshape(-1, D)

    layers[0].across()
    if count == 32:
        rest.merge()
        layers[0].far, rest.quad, layers[1].pack = meet(
            layers[0].far, rest.quad, layers[1].pack
        )
    layers[0].finish()
    rest.along_xy()
    layers[1].along_z()

    def forward(level, hidden):
        level_mods = mods[6 * level : 6 * level + 6]
        normed, packed, logs, attended, branch, middle = attn_forward(
            hidden, level_mods, block_bias[level], orders, layers[level]
        )
        kept_attn = [hidden, normed, packed, logs, attended, branch]
        if count == 32 and level == 0:
            middle, rest.by_x, rest.by_y, layers[1].deep = meet(
                middle, rest.by_x, rest.by_y, layers[1].deep
            )
            rest.across()
        if count == 32 and level == 1:
            middle, rest_sum.to_far = meet(middle, rest_sum.to_far)
            rest_sum.across()
        normed, slope, active, branch, hidden = mlp_forward(
            middle, level_mods, block_bias[level], orders, layers[level]
        )
        return hidden, kept_attn, [middle, normed, slope, active, branch]

    kept = [None] * L
    hidden, *kept[0] = forward(0, hidden)
    first_out = hidden
    if count == 32:
        layers[1].merge()
        hidden, rest.far, layers[1].quad = meet(hidden, rest.far, layers[1].quad)
    first_out = hidden
    layers[1].along_xy()
    rest.finish()
    (
        grad_first,
        cosine_part,
        grad_one,
        grad_two,
        grad_three,
        one_mine,
        one_theirs,
        rest_mine,
        *rest_theirs,
    ) = projector(
        first_out,
        features.reshape(TOK, Z),
        bias_one[None],
        bias_two[None],
        bias_three[None],
        orders,
        layers[0],
        rest,
    )
    layers[1].across()
    layers[1].finish()
    rest_sum = scatter([(rest_mine, rest_theirs, 0, 4)], count)
    rest_sum.cores()
    rest_sum.make_far()
    hidden, *kept[1] = forward(1, hidden)
    grad_hidden, grad_final_mods, grad_head, grad_head_bias, head_loss = head(
        hidden,
        mods[6 * L :],
        head_weight[:D].astype(LOW),
        head_weight[D:],
        targets.reshape(TOK, PD),
        time_weights.reshape(1, 1),
    )
    bias_grads, mod_grads = [None] * L, [None] * L

    def backward(level, grad_hidden):
        level_mods = mods[6 * level : 6 * level + 6]
        grad_middle, mlp_mods, mlp_bias, mlp_mine, *mlp_theirs = mlp_backward(
            grad_hidden, level_mods, kept[level][1], orders, layers[level]
        )
        if count == 32 and level == 0:
            one_sum.make_near()
            grad_middle, one_sum.to_near = meet(grad_middle, one_sum.to_near)
            one_sum.along_xy()
            grad_middle, rest_sum.deep = meet(grad_middle, rest_sum.deep)
        grad_hidden, attn_mods, attn_bias, attn_mine, *attn_theirs = attn_backward(
            grad_middle, level_mods, kept[level][0], orders, layers[level]
        )
        mod_grads[level] = jnp.concatenate([attn_mods, mlp_mods])
        bias_grads[level] = (attn_bias, mlp_bias)
        if count == 32 and level == 1:
            attn_theirs, rest_sum.near = meet(attn_theirs, rest_sum.near)
        parts = [(attn_mine, attn_theirs, 4, 0), (mlp_mine, mlp_theirs, 4, 4)]
        return grad_hidden, parts

    rest_sum.make_near()
    if count == 32:
        grad_hidden, rest_sum.to_near = meet(grad_hidden, rest_sum.to_near)
    rest_sum.along_xy()
    grad_hidden, parts = backward(1, grad_hidden)
    one_sum = scatter(parts + [(one_mine, [one_theirs], 3, 0)], count)
    one_sum.cores()
    one_sum.make_far()
    grad_hidden = grad_hidden + grad_first
    if count == 32:
        grad_hidden, one_sum.to_far = meet(grad_hidden, one_sum.to_far)
    one_sum.across()
    rest_sum.make_deep()
    rest_sum.along_z()
    grad_hidden, parts = backward(0, grad_hidden)
    zero_sum = scatter(parts, count)
    zero_sum.cores()
    zero_sum.make_far()
    grad_mods = jnp.concatenate(mod_grads + [grad_final_mods]).astype(LOW).reshape(-1, 128)
    mod_rows = grad_mods.shape[0]
    grad_mods = jnp.pad(grad_mods, ((0, -mod_rows % 16), (0, 0)))
    left = (
        (grad_hidden, grad_one, grad_two, grad_three, grad_final_mods, bias_grads, mod_grads),
        (grad_head, grad_head_bias, head_loss, cosine_part),
        (block_in, stem_main, stem_main_rows, stem_proj_rows, block_in_rows, block_down_rows),
    )
    if count == 32:
        grad_mods, one_sum.near, zero_sum.to_far, left = meet(
            grad_mods, one_sum.near, zero_sum.to_far, left
        )
    grad_hidden, grad_one, grad_two, grad_three, grad_final_mods, bias_grads, mod_grads = left[0]
    grad_head, grad_head_bias, head_loss, cosine_part = left[1]
    block_in, stem_main, stem_main_rows, stem_proj_rows, block_in_rows, block_down_rows = left[2]
    zero_sum.across()
    one_sum.make_deep()
    one_sum.along_z()
    time_out_part, final_ada_part = stem_main[:, :D], stem_main[:, D : 3 * D]
    ada_mine = jnp.concatenate(
        [block_in[level, :, main_width:] for level in range(L)] + [final_ada_part], axis=1
    ).astype(LOW)
    local_loss = head_loss[0, 0] + cosine_part[0, 0]
    grad_head_full = jnp.concatenate([grad_head, grad_head_bias], axis=0)
    bias_grads = [
        jnp.concatenate([attn_bias, mlp_bias[:4], grads, mlp_bias[4:]]).reshape(-1)
        for (attn_bias, mlp_bias), grads in zip(bias_grads, mod_grads)
    ]
    grad_patch = lax.dot_general(
        grad_hidden.astype(jnp.bfloat16),
        latent_low,
        (((0,), (0,)), ((), ())),
        preferred_element_type=jnp.float32,
    )
    grad_bias_all = jnp.concatenate(
        bias_grads
        + [
            jnp.zeros((2 * D,), jnp.float32),
            grad_final_mods.reshape(-1),
            total_rows(grad_hidden),
            grad_one.reshape(-1),
            grad_two.reshape(-1),
            grad_three.reshape(-1),
        ]
    )
    extra = jnp.concatenate(
        [grad_patch.reshape(count, -1), grad_bias_all.reshape(count, bias_part)], axis=1
    )
    extra = jnp.pad(extra, ((0, 0), (0, -extra.shape[1] % 2048))).reshape(count, -1, 128)
    def start_near(sent):
        if count == 32:
            sent, zero_sum.far = meet(sent, zero_sum.far)
        zero_sum.make_near()
        zero_sum.along_xy()
        return sent

    def see_deep(sent):
        if count == 32:
            sent, one_sum.deep = meet(sent, one_sum.deep)
        return sent

    grad_mods_all, extra = gather_and_sum(
        grad_mods, extra, position, count, {2: start_near, 3: see_deep}
    )
    grad_mods_all = grad_mods_all[:, :mod_rows].reshape(images, -1)
    turned = order_of(list(range(count)), position)
    cond_turned = dot(cond_low, turned).astype(LOW)
    extra = extra.reshape(-1)
    patch_shard = extra[: width_rows * PD].reshape(width_rows, PD)
    bias_shard = extra[width_rows * PD : width_rows * PD + bias_part]

    grad_ada_mine = dot(cond_turned, grad_mods_all)
    grad_cond_mine = jnp.dot(
        dot_rows(ada_mine, grad_mods_all),
        turned.astype(FULL),
        precision=lax.Precision.HIGHEST,
    )
    grad_condition = silu_back(condition, grad_cond_mine)
    grad_table = jnp.dot(
        grad_condition, one_hot.astype(jnp.float32), precision=lax.Precision.HIGHEST
    )
    grad_condition_low = grad_condition.astype(LOW)

    def between(blocks):
        if count == 32:
            blocks, zero_sum.near = meet(blocks, zero_sum.near)
        zero_sum.make_deep()
        zero_sum.along_z()
        return blocks

    masks = [1 << bit for bit in range(3, bits)] + [4, 2, 1]
    grad_condition_low = gather_all(grad_condition_low, position, count, masks, between)
    grad_condition_low = grad_condition_low.reshape(D, images)
    grad_time_out = dot_rows(mine(embed_act), grad_condition_low)
    grad_embed_act = dot(time_out_part.astype(LOW), grad_condition_low)
    grad_embed = silu_back(mine(embed_hidden), grad_embed_act)
    grad_time_in = dot(grad_embed.astype(LOW), freq_low)
    late_bias = jnp.zeros((2, D), jnp.float32)
    late_bias = lax.dynamic_update_slice(
        late_bias,
        jnp.stack([jnp.sum(grad_embed, axis=1), jnp.sum(grad_condition, axis=1)]),
        (0, position * width_rows),
    )

    def side_by_side(blocks):
        return jnp.swapaxes(blocks, 0, 1).reshape(blocks.shape[1], -1)

    shards = [zero_sum.result(), one_sum.result()]
    ada_zero, ada_one, grad_final_ada = cut_parts(grad_ada_mine, [6 * D, 6 * D, 2 * D])
    raw_in = jnp.stack(
        [
            jnp.concatenate(
                [side_by_side(shards[level][:8]), ada], axis=1
            )
            for level, ada in enumerate([ada_zero, ada_one])
        ]
    )
    raw_down = jnp.stack([shards[0][8:].reshape(-1, D), shards[1][8:12].reshape(-1, D)])
    raw_main = jnp.concatenate(
        [
            grad_time_out,
            grad_final_ada,
            grad_table,
            patch_shard,
            side_by_side(shards[1][12:])[:, :P_SIZE],
            grad_time_in,
        ],
        axis=1,
    )
    raw_proj = rest_sum.result()[0]
    raws = [raw_in[0], raw_in[1], raw_down[0], raw_down[1], raw_main, raw_proj]
    row_olds = [
        block_in_rows[0],
        block_in_rows[1],
        block_down_rows[0],
        block_down_rows[1],
        stem_main_rows,
        stem_proj_rows,
    ]
    squares = [raw * raw for raw in raws]
    row_squares = [jnp.sum(square, axis=1) for square in squares]
    late_list = [jnp.sum(square, axis=0) for square in squares] + [
        jnp.stack([jnp.sum(row_old) for row_old in row_olds]),
        jnp.stack([jnp.sum(bias_shard * bias_shard), local_loss]),
        late_bias.reshape(-1),
        grad_head_full.reshape(-1),
    ]
    late_sizes = [values.shape[0] for values in late_list]
    late_all = jnp.concatenate(late_list)
    late_all = jnp.pad(late_all, (0, -late_all.shape[0] % 1024)).reshape(-1, 128)
    late_all = sum_all(late_all, count).reshape(-1)
    late_sums = []
    running = 0
    for size in late_sizes:
        late_sums.append(late_all[running : running + size])
        running += size
    col_squares = late_sums[:6]
    row_old_sums, bias_loss, late_bias, head_sum = late_sums[6:]
    head_sum = head_sum.reshape(D + 1, PD)
    loss_total = bias_loss[1]
    row_sums = jnp.pad(jnp.concatenate([row_old_sums, bias_loss])[None], ((0, 0), (0, 120)))
    pairs = [
        jnp.stack([row_old, square], axis=-1) for row_old, square in zip(row_olds, row_squares)
    ]
    olds = [block_in, block_down, stem_main, stem_proj]
    raw_list = [raw_in, raw_down, raw_main, raw_proj]
    late_flat = jnp.zeros((count * bias_part,), jnp.float32)
    late_flat = lax.dynamic_update_slice(late_flat, late_bias, (L * VB,))
    bias_raw = bias_shard + lax.dynamic_slice(late_flat, (position * bias_part,), (bias_part,))
    flat_rows = [
        jnp.stack(row_olds[0:2] + row_squares[0:2]),
        jnp.stack(row_olds[2:4] + row_squares[2:4]),
        jnp.stack([row_olds[4], row_squares[4]]),
        jnp.stack([row_olds[5], row_squares[5]]),
    ]
    outputs = [
        shaped(FULL, 8, 128),
        shaped(FULL, *head_weight.shape),
        shaped(FULL, *head_weight.shape),
        shaped(FULL, head_weight.shape[0], 1),
        shaped(FULL, 1, head_weight.shape[1]),
        shaped(FULL, *block_in_rows.shape),
        shaped(FULL, *block_down_rows.shape),
        shaped(FULL, 1, *stem_main_rows.shape),
        shaped(FULL, 1, *stem_proj_rows.shape),
    ] + [shaped(FULL, 1, bias_part)] * 3
    col_old_list = [block_in_cols, block_down_cols, stem_main_cols[None], stem_proj_cols[None]]
    for old, col_old in zip(olds, col_old_list):
        outputs += [shaped(FULL, *old.shape), shaped(FULL, *old.shape), shaped(LOW, *old.shape)]
        outputs.append(shaped(FULL, *col_old.shape))
    made = call(
        functools.partial(update_kernel, count),
        [
            *raw_list,
            *olds,
            jnp.stack(pairs[0:2]),
            jnp.stack(pairs[2:4]),
            pairs[4],
            pairs[5],
            *col_old_list,
            jnp.stack(col_squares[0:2]),
            jnp.stack(col_squares[2:4]),
            col_squares[4][None],
            col_squares[5][None],
            row_sums,
            late_bias.reshape(2, D),
            head_sum,
            head_weight,
            head_rows[:, None],
            head_cols[None],
            *flat_rows,
            bias_raw[None],
            biases[None],
            bias_second[None],
        ],
        [],
        outputs,
        [],
        [],
        12,
        0,
    )
    grad_norm = made[0][0, 0]
    new_head, head_clip, rows_head, cols_head = made[1], made[2], made[3][:, 0], made[4][0]
    rows_in, rows_down, rows_main, rows_proj = made[5], made[6], made[7][0], made[8][0]
    new_bias, clip_bias, second_new = (part[0] for part in made[9:12])
    (
        (new_in, clip_in, copy_in, cols_in),
        (new_down, clip_down, copy_down, cols_down),
        (new_main, clip_main, copy_main, cols_main),
        (new_proj, clip_proj, copy_proj, cols_proj),
    ) = (made[12 + 4 * slot : 16 + 4 * slot] for slot in range(4))
    return (
        loss_total,
        grad_norm,
        new_in,
        clip_in,
        rows_in,
        cols_in,
        copy_in,
        new_down,
        clip_down,
        rows_down,
        cols_down,
        copy_down,
        new_main,
        clip_main,
        rows_main,
        cols_main[0],
        copy_main,
        new_proj,
        clip_proj,
        rows_proj,
        cols_proj[0],
        copy_proj,
        new_head,
        head_clip,
        rows_head,
        cols_head,
        new_bias,
        clip_bias,
        second_new,
    )


def solution(mesh):
    return jax.shard_map(
        functools.partial(body, mesh.shape["fsdp"]),
        mesh=mesh,
        in_specs=(
            P("fsdp", None, None),
            P("fsdp", None, None),
            P("fsdp", None, None),
            P("fsdp"),
            P("fsdp"),
            P("fsdp"),
            P(None, "fsdp", None),
            P(None, "fsdp"),
            P(),
            P(None, "fsdp", None),
            P(None, "fsdp"),
            P(),
            P("fsdp", None),
            P("fsdp"),
            P(),
            P("fsdp", None),
            P("fsdp"),
            P(),
            P(),
            P(),
            P(),
            P("fsdp"),
            P("fsdp"),
        ),
        out_specs=(
            P(),
            P(),
            P(None, "fsdp", None),
            P(None, "fsdp", None),
            P(None, "fsdp"),
            P(),
            P(None, "fsdp", None),
            P(None, "fsdp", None),
            P(None, "fsdp", None),
            P(None, "fsdp"),
            P(),
            P(None, "fsdp", None),
            P("fsdp", None),
            P("fsdp", None),
            P("fsdp"),
            P(),
            P("fsdp", None),
            P("fsdp", None),
            P("fsdp", None),
            P("fsdp"),
            P(),
            P("fsdp", None),
            P(),
            P(),
            P(),
            P(),
            P("fsdp"),
            P("fsdp"),
            P("fsdp"),
        ),
        check_vma=False,
    )
```
